128 devices in a mesh: inner: 8 (over y_hi, x), outer: 16 (over z, y_lo, core).
Axes of the slice: x: 4, y: 4 (y_hi: 2, y_lo: 2; y = y_hi * 2 + y_lo), z: 4, core: 2. Of those that a mesh axis runs over, the one named last changes fastest.
Arguments:
- queries: bfloat16 [24576, 512], P(('inner', 'outer')), may hold values from -12 to 12
- key_value: bfloat16 [24576, 128], P(('inner', 'outer')), may hold values from -12 to 12
- positions: int32 [24576], P(('inner', 'outer')), may hold values from 0 to 24575, as said below
- sinks: float32 [8], replicated, may hold values from -1 to 4
Outputs:
- attended: bfloat16 [24576, 512], P(('inner', 'outer'))
The draws below stay inside these ranges and needn't reach their ends.
Inputs may be any that keep to these rules, and one draw needn't show every extreme that they name: Each of 0 to 24575 appears once. The 192 rows of one device are two runs of 96 consecutive increasing positions: run i first and run 256 - 1 - i second, counting runs of 96 positions from the start, with i different on every device.
All inputs are finite; a program needn't handle non-finite values.
Results may differ from the reference program's by a relative error of at most 0.004.
Values may be sent and summed in bfloat16 or wider, within the bound.
No kernel may reach another device: no remote copies, remote signals or barrier semaphores. Data moves between devices by JAX's collectives and lax.ppermute only.
A program may use at most 64 MiB of HBM per device.

```python
import jax
import jax.numpy as jnp
from jax import lax

HEADS = 8
HD = 64
TOK_DEV = 192
SPAN = 96
TOKENS = 24576


def row_scales(key, low, high):
    return jnp.exp(jax.random.uniform(key, (TOKENS, 1), jnp.float32, jnp.log(low), jnp.log(high)))


def draw_queries(key, part):
    key = jax.random.fold_in(key, 1)
    entry_key, scale_key = jax.random.split(key)
    scales = row_scales(scale_key, 0.3, 3.0)
    entries = jnp.clip(jax.random.normal(entry_key, (TOKENS, HEADS * HD), jnp.float32), -3.5, 3.5) * scales
    return entries.astype(jnp.bfloat16)


def draw_key_value(key, part):
    key = jax.random.fold_in(key, 2)
    entry_key, value_key, scale_key = jax.random.split(key, 3)
    scales = row_scales(scale_key, 0.5, 2.0)
    key_part = jnp.clip(jax.random.normal(entry_key, (TOKENS, HD), jnp.float32), -3.5, 3.5) * scales
    value_part = jnp.clip(jax.random.normal(value_key, (TOKENS, HD), jnp.float32), -3.5, 3.5)
    return jnp.concatenate([key_part, value_part], axis=1).astype(jnp.bfloat16)


def draw_positions(key, part):
    key = jax.random.fold_in(key, 11)
    devices = TOKENS // TOK_DEV
    order = jax.random.permutation(key, devices).astype(jnp.int32)
    within = jnp.arange(SPAN, dtype=jnp.int32)
    lower = order[:, None] * SPAN + within[None, :]
    upper = (2 * devices - 1 - order)[:, None] * SPAN + within[None, :]
    return jnp.concatenate([lower, upper], axis=1).reshape(TOKENS).astype(jnp.int32)


def setup_inputs(seed: int = 0) -> dict:
    splits = jax.random.split(jax.random.key(seed), 5)
    return {
        "queries": draw_queries(jax.random.fold_in(splits[4], 71), 0),
        "key_value": draw_key_value(jax.random.fold_in(splits[4], 71), 0),
        "positions": draw_positions(jax.random.fold_in(splits[4], 71), 0),
        "sinks": jnp.clip(jax.random.uniform(splits[3], (HEADS,), jnp.float32, -1.0, 4.0), -1.0, 4.0),
    }


def reference(queries, key_value, positions, sinks):
    keys = key_value[:, :HD].astype(jnp.float32)
    values = key_value[:, HD:].astype(jnp.float32)
    query_blocks = queries.reshape(TOKENS // TOK_DEV, TOK_DEV, HEADS, HD)
    pos_blocks = positions.reshape(TOKENS // TOK_DEV, TOK_DEV)
    scale = HD ** -0.5

    def one_block(inputs):
        query_rows, query_pos = inputs
        scores = jnp.einsum("thd,kd->thk", query_rows.astype(jnp.float32), keys) * scale
        visible = positions[None, None, :] <= query_pos[:, None, None]
        masked = jnp.where(visible, scores, -jnp.inf)
        top = jnp.maximum(jnp.max(masked, axis=2), sinks[None, :])
        weights = jnp.where(visible, jnp.exp(masked - top[:, :, None]), jnp.float32(0.0))
        total = jnp.exp(sinks[None, :] - top) + jnp.sum(weights, axis=2)
        rounded = weights.astype(jnp.bfloat16)
        summed = jnp.einsum("thk,kd->thd", rounded.astype(jnp.float32), values)
        result = (summed / total[:, :, None]).astype(jnp.bfloat16)
        return result.reshape(TOK_DEV, HEADS * HD)

    attended = lax.map(one_block, (query_blocks, pos_blocks))
    return attended.reshape(TOKENS, HEADS * HD)
```

```python
import functools

import jax
import jax.numpy as jnp
from jax import lax
from jax.experimental import pallas as pl
from jax.experimental.pallas import tpu as pltpu
from jax.sharding import PartitionSpec as P

HEADS = 8
HD = 64
SPAN = 96
ROWS = HEADS * SPAN
GROUP = 8
CHUNK = GROUP * SPAN
MSG = 208
QMSG = 144
PART = 160
LOG2E = 1.4426950408889634
SCALE = HD**-0.5 * LOG2E
LIMIT = 1e36
F32 = jnp.float32
BF16 = jnp.bfloat16
VMEM = pl.BlockSpec(memory_space=pltpu.VMEM)
SMEM = pl.BlockSpec(memory_space=pltpu.SMEM)
PARAMS = pltpu.CompilerParams(vmem_limit_bytes=56 << 20)


def dot(a, b):
    return jnp.dot(a, b, preferred_element_type=F32)


def prepare(pos_ref, q_ref, kv_ref, qm_ref, km_ref):
    run = pos_ref[0] // SPAN
    swapped = run >= 128
    lower = jnp.where(swapped, 255 - run, run).astype(F32)

    def halves(ref):
        first, second = ref[0:SPAN, :], ref[SPAN : 2 * SPAN, :]
        return jnp.where(swapped, second, first), jnp.where(swapped, first, second)

    lo, up = halves(kv_ref)
    km_ref[0:SPAN, :] = jnp.concatenate([lo[:, :HD], up[:, :HD]], axis=1)
    km_ref[SPAN : 2 * SPAN, :] = jnp.concatenate([lo[:, HD:], up[:, HD:]], axis=1)
    km_ref[2 * SPAN :, :] = jnp.full((MSG - 2 * SPAN, 128), lower, F32).astype(BF16)
    lo, up = halves(q_ref)
    stacked = jnp.concatenate(
        [
            jnp.concatenate([lo[:, h * HD : (h + 1) * HD], up[:, h * HD : (h + 1) * HD]], axis=1)
            for h in range(HEADS)
        ],
        axis=0,
    )
    qm_ref[0:128, :] = jnp.transpose(stacked)
    qm_ref[128:, :] = jnp.full((QMSG - 128, ROWS), lower, F32).astype(BF16)


def diagonal(qm_ref, km_ref, out_ref):
    keys = lax.broadcasted_iota(jnp.int32, (SPAN, ROWS), 0)
    rows = lax.broadcasted_iota(jnp.int32, (SPAN, ROWS), 1)
    mine = rows
    for h in range(1, HEADS):
        mine = jnp.where(rows >= h * SPAN, rows - h * SPAN, mine)
    visible = keys <= mine
    k = km_ref[0:SPAN, :]
    v = jnp.transpose(km_ref[SPAN : 2 * SPAN, :].astype(F32)).astype(BF16)
    for half in range(2):
        part = slice(half * HD, (half + 1) * HD)
        s = dot(k[:, part], qm_ref[part, :]) * SCALE
        s = jnp.where(visible, s, -1e30)
        shift = jnp.maximum(jnp.max(s, axis=0, keepdims=True), 0.0)
        p = jnp.where(visible, jnp.exp2(s - shift), 0.0)
        out_ref[part, :] = dot(v[part, :], p.astype(BF16))
        total = jnp.sum(p, axis=0, keepdims=True)
        out_ref[128 + 8 * half : 136 + 8 * half, :] = jnp.broadcast_to(total, (8, ROWS))
        out_ref[144 + 8 * half : 152 + 8 * half, :] = jnp.broadcast_to(shift, (8, ROWS))


def chunk_masks(km_ref, qm_ref, c, q):
    info = km_ref[pl.ds(c * GROUP, GROUP), 2 * SPAN : 2 * SPAN + 16, :].astype(F32)[:, 0:1, :]
    own = qm_ref[q, 128:144, 0:128].astype(F32)[0:1, :]
    below = jnp.where(info < own[None], 1.0, 0.0)
    above = jnp.where(info > own[None], 1.0, 0.0)
    return below, above


def along_lanes(mask):
    lanes = lax.broadcasted_iota(jnp.int32, (16, CHUNK), 1)
    wide = [
        jnp.concatenate([jnp.broadcast_to(mask[b], (16, 128))] * (CHUNK // 128), axis=1)
        for b in range(GROUP)
    ]
    out = wide[0]
    for b in range(1, GROUP):
        out = jnp.where(lanes >= b * SPAN, wide[b], out)
    return out


def chunk_operands(km_ref, qm_ref, c, q, vt):
    below, above = chunk_masks(km_ref, qm_ref, c, q)
    k = km_ref[pl.ds(c * GROUP, GROUP), 0:SPAN, :]
    lanes = lax.broadcasted_iota(jnp.int32, (GROUP, 1, 128), 2)
    keep = jnp.where(lanes < HD, below, above).astype(BF16)
    chosen = (k * keep).reshape(CHUNK, 128)
    low, high = along_lanes(below), along_lanes(above)
    rows = lax.broadcasted_iota(jnp.int32, (16, CHUNK), 0)
    ones = jnp.where(rows < 8, low, high).astype(BF16)
    low, high = low[0:1].astype(BF16), high[0:1].astype(BF16)
    values = jnp.concatenate([vt[:HD] * low, vt[HD:] * high, ones], axis=0)
    return k.reshape(CHUNK, 128), chosen, values


def attend(nq, nk, qm_ref, km_ref, out_ref):
    chunks = nk // GROUP
    out_ref[...] = jnp.zeros_like(out_ref)
    one = jnp.ones((16, CHUNK), BF16)

    def transposed(c):
        v = km_ref[pl.ds(c * GROUP, GROUP), SPAN : 2 * SPAN, :].reshape(CHUNK, 128)
        return jnp.transpose(v)

    @pl.loop(0, chunks)
    def _(c):
        vt = transposed(c)
        first = jnp.concatenate([vt[:HD], one], axis=0)
        for q in range(nq):
            k, chosen, values = chunk_operands(km_ref, qm_ref, c, q, vt)
            a = dot(k[:, :HD], qm_ref[q, HD:128, :])
            b = dot(chosen, qm_ref[q, 0:128, :])
            pa = jnp.exp2(a * SCALE).astype(BF16)
            pb = jnp.exp2(b * SCALE).astype(BF16)
            oa = dot(first, pa)
            ob = dot(values, pb)
            out_ref[q, 0:HD, :] += ob[:HD]
            out_ref[q, HD:128, :] += oa[:HD] + ob[HD:128]
            out_ref[q, 128:136, :] += ob[128:136]
            out_ref[q, 136:144, :] += oa[HD : HD + 8] + ob[136:144]

    for q in range(nq):
        bad = jnp.sum(jnp.where(out_ref[q, 128:144, :] < LIMIT, 0.0, 1.0))

        @pl.when(bad > 0.0)
        def _():
            careful(q, chunks, transposed, qm_ref, km_ref, out_ref)


def careful(q, chunks, transposed, qm_ref, km_ref, out_ref):
    out_ref[q] = jnp.zeros(out_ref.shape[1:], F32)

    def rounded(x):
        return jnp.maximum(x, 0.0).astype(BF16).astype(F32)

    def rescale(half, new):
        old = out_ref[q, 144 + 8 * half : 145 + 8 * half, :]
        factor = jnp.exp2(old - new)
        out_ref[q, half * HD : (half + 1) * HD, :] *= factor
        out_ref[q, 128 + 8 * half : 136 + 8 * half, :] *= factor
        out_ref[q, 144 + 8 * half : 152 + 8 * half, :] = jnp.broadcast_to(new, (8, ROWS))

    def raised(half, top):
        return jnp.maximum(out_ref[q, 144 + 8 * half : 145 + 8 * half, :], rounded(top))

    @pl.loop(0, chunks)
    def _(c):
        vt = transposed(c)
        one = jnp.ones((16, CHUNK), BF16)
        first = jnp.concatenate([vt[:HD], one], axis=0)
        k, chosen, values = chunk_operands(km_ref, qm_ref, c, q, vt)
        a = dot(k[:, :HD], qm_ref[q, HD:128, :]) * SCALE
        new = raised(1, jnp.max(a, axis=0, keepdims=True))
        rescale(1, new)
        oa = dot(first, jnp.exp2(a - new).astype(BF16))
        out_ref[q, HD:128, :] += oa[:HD]
        out_ref[q, 136:144, :] += oa[HD : HD + 8]
        b = dot(chosen, qm_ref[q, 0:128, :]) * SCALE
        b = b.reshape(GROUP, SPAN, ROWS)
        below, above = chunk_masks(km_ref, qm_ref, c, q)

        def top(mask):
            wide = jnp.concatenate([mask] * (ROWS // 128), axis=2)
            return jnp.max(jnp.max(jnp.where(wide > 0.5, b, -1e30), axis=0), axis=0, keepdims=True)

        low, high = raised(0, top(below)), raised(1, top(above))
        rescale(0, low)
        rescale(1, high)
        wide = jnp.concatenate([below] * (ROWS // 128), axis=2)
        known = jnp.concatenate([below + above] * (ROWS // 128), axis=2)
        shift = jnp.where(wide > 0.5, low[None], high[None])
        p = jnp.where(known > 0.5, jnp.exp2(b - shift), 0.0)
        ob = dot(values, p.reshape(CHUNK, ROWS).astype(BF16))
        out_ref[q, 0:128, :] += ob[0:128]
        out_ref[q, 128:144, :] += ob[128:144]


def finish(count, pos_ref, sink_ref, *refs):
    parts, out_ref = refs[:count], refs[count]
    swapped = pos_ref[0] // SPAN >= 128
    halves = []
    for half in range(2):
        part = slice(half * HD, (half + 1) * HD)
        shifts = [p[144 + 8 * half : 145 + 8 * half, :] for p in parts]
        top = functools.reduce(jnp.maximum, shifts)
        total = jnp.exp2(sink_ref[0:1, :] * LOG2E - top)
        sums = jnp.zeros((HD, ROWS), F32)
        for p, shift in zip(parts, shifts):
            factor = jnp.exp2(shift - top)
            total = total + p[128 + 8 * half : 129 + 8 * half, :] * factor
            sums = sums + p[part, :] * factor
        halves.append(sums / total)
    both = jnp.transpose(jnp.concatenate(halves, axis=0))
    for g in range(HEADS // 2):
        even, odd = both[2 * g * SPAN : (2 * g + 1) * SPAN], both[(2 * g + 1) * SPAN : (2 * g + 2) * SPAN]
        lo = jnp.concatenate([even[:, :HD], odd[:, :HD]], axis=1)
        up = jnp.concatenate([even[:, HD:], odd[:, HD:]], axis=1)
        lanes = slice(128 * g, 128 * (g + 1))
        out_ref[0:SPAN, lanes] = jnp.where(swapped, up, lo).astype(BF16)
        out_ref[SPAN : 2 * SPAN, lanes] = jnp.where(swapped, lo, up).astype(BF16)


def partials(qm, km):
    nq, nk = qm.shape[0], km.shape[0]
    pairs = nq * nk * 2 * SPAN * ROWS
    return pl.pallas_call(
        functools.partial(attend, nq, nk),
        out_shape=jax.ShapeDtypeStruct((nq, PART, ROWS), F32),
        in_specs=[VMEM, VMEM],
        out_specs=VMEM,
        compiler_params=PARAMS,
        cost_estimate=pl.CostEstimate(
            flops=pairs * 256, bytes_accessed=km.size * 2, transcendentals=pairs
        ),
        name="attend",
    )(qm, km)


def shards(queries, key_value, positions, sinks):
    qm, km = pl.pallas_call(
        prepare,
        out_shape=(
            jax.ShapeDtypeStruct((QMSG, ROWS), BF16),
            jax.ShapeDtypeStruct((MSG, 128), BF16),
        ),
        in_specs=[SMEM, VMEM, VMEM],
        out_specs=(VMEM, VMEM),
        compiler_params=PARAMS,
        name="prepare",
    )(positions, queries, key_value)
    own = pl.pallas_call(
        diagonal,
        out_shape=jax.ShapeDtypeStruct((PART, ROWS), F32),
        in_specs=[VMEM, VMEM],
        out_specs=VMEM,
        compiler_params=PARAMS,
        name="diagonal",
    )(qm, km)
    every = lax.all_gather(lax.all_gather(km, "inner"), "outer")
    part = partials(qm[None], every.reshape(-1, MSG, 128))
    sink_row = jnp.broadcast_to(jnp.repeat(sinks, SPAN)[None], (8, ROWS))
    return pl.pallas_call(
        functools.partial(finish, 2),
        out_shape=jax.ShapeDtypeStruct(queries.shape, BF16),
        in_specs=[SMEM] + [VMEM] * 3,
        out_specs=VMEM,
        compiler_params=PARAMS,
        name="finish",
    )(positions, sink_row, own, part[0])


def solution(mesh):
    return jax.shard_map(
        shards,
        mesh=mesh,
        in_specs=(
            P(("inner", "outer"), None),
            P(("inner", "outer"), None),
            P(("inner", "outer")),
            P(),
        ),
        out_specs=P(("inner", "outer"), None),
        check_vma=False,
    )
```

```python
import functools

import jax
import jax.numpy as jnp
from jax import lax
from jax.experimental import pallas as pl
from jax.experimental.pallas import tpu as pltpu
from jax.sharding import PartitionSpec as P

HEADS = 8
HD = 64
SPAN = 96
ROWS = HEADS * SPAN
GROUP = 8
CHUNK = GROUP * SPAN
MSG = 208
QMSG = 144
PART = 160
LOG2E = 1.4426950408889634
SCALE = HD**-0.5 * LOG2E
LIMIT = 1e36
F32 = jnp.float32
BF16 = jnp.bfloat16
VMEM = pl.BlockSpec(memory_space=pltpu.VMEM)
SMEM = pl.BlockSpec(memory_space=pltpu.SMEM)
PARAMS = pltpu.CompilerParams(vmem_limit_bytes=32 << 20)


def dot(a, b):
    return jnp.dot(a, b, preferred_element_type=F32)


def prepare_keys(pos_ref, kv_ref, km_ref):
    run = pos_ref[0] // SPAN
    swapped = run >= 128
    lower = jnp.where(swapped, 255 - run, run).astype(F32)
    lo, up = halves(kv_ref, swapped)
    km_ref[0:SPAN, :] = jnp.concatenate([lo[:, :HD], up[:, :HD]], axis=1)
    km_ref[SPAN : 2 * SPAN, :] = jnp.concatenate([lo[:, HD:], up[:, HD:]], axis=1)
    km_ref[2 * SPAN :, :] = jnp.full((MSG - 2 * SPAN, 128), lower, F32).astype(BF16)


def prepare_queries(pos_ref, q_ref, qm_ref):
    run = pos_ref[0] // SPAN
    swapped = run >= 128
    lower = jnp.where(swapped, 255 - run, run).astype(F32)
    lo, up = halves(q_ref, swapped)
    stacked = jnp.concatenate(
        [
            jnp.concatenate([lo[:, h * HD : (h + 1) * HD], up[:, h * HD : (h + 1) * HD]], axis=1)
            for h in range(HEADS)
        ],
        axis=0,
    )
    qm_ref[0:128, :] = jnp.transpose(stacked)
    qm_ref[128:, :] = jnp.full((QMSG - 128, ROWS), lower, F32).astype(BF16)


def halves(ref, swapped):
    first, second = ref[0:SPAN, :], ref[SPAN : 2 * SPAN, :]
    return jnp.where(swapped, second, first), jnp.where(swapped, first, second)


def diagonal(qm_ref, km_ref, out_ref):
    keys = lax.broadcasted_iota(jnp.int32, (SPAN, ROWS), 0)
    rows = lax.broadcasted_iota(jnp.int32, (SPAN, ROWS), 1)
    mine = rows
    for h in range(1, HEADS):
        mine = jnp.where(rows >= h * SPAN, rows - h * SPAN, mine)
    visible = keys <= mine
    k = km_ref[0:SPAN, :]
    v = jnp.transpose(km_ref[SPAN : 2 * SPAN, :].astype(F32)).astype(BF16)
    for half in range(2):
        part = slice(half * HD, (half + 1) * HD)
        s = dot(k[:, part], qm_ref[part, :]) * SCALE
        s = jnp.where(visible, s, -1e30)
        shift = jnp.maximum(jnp.max(s, axis=0, keepdims=True), 0.0)
        p = jnp.where(visible, jnp.exp2(s - shift), 0.0)
        out_ref[part, :] = dot(v[part, :], p.astype(BF16))
        total = jnp.sum(p, axis=0, keepdims=True)
        out_ref[128 + 8 * half : 136 + 8 * half, :] = jnp.broadcast_to(total, (8, ROWS))
        out_ref[144 + 8 * half : 152 + 8 * half, :] = jnp.broadcast_to(shift, (8, ROWS))


def chunk_masks(keys, q_ref):
    info = keys[:, 2 * SPAN : 2 * SPAN + 16, :].astype(F32)[:, 0:1, :]
    own = q_ref[128:144, 0:128].astype(F32)[0:1, :]
    below = jnp.where(info < own[None], 1.0, 0.0)
    above = jnp.where(info > own[None], 1.0, 0.0)
    return below, above


def along_lanes(mask):
    lanes = lax.broadcasted_iota(jnp.int32, (16, CHUNK), 1)
    wide = [
        jnp.concatenate([jnp.broadcast_to(mask[b], (16, 128))] * (CHUNK // 128), axis=1)
        for b in range(GROUP)
    ]
    out = wide[0]
    for b in range(1, GROUP):
        out = jnp.where(lanes >= b * SPAN, wide[b], out)
    return out


def load_chunk(key_refs):
    return jnp.concatenate([ref[...] for ref in key_refs], axis=0)


def transposed_values(keys):
    return jnp.transpose(keys[:, SPAN : 2 * SPAN, :].reshape(CHUNK, 128))


def chunk_operands(keys, q_ref, vt):
    below, above = chunk_masks(keys, q_ref)
    k = keys[:, 0:SPAN, :]
    lanes = lax.broadcasted_iota(jnp.int32, (GROUP, 1, 128), 2)
    keep = jnp.where(lanes < HD, below, above).astype(BF16)
    chosen = (k * keep).reshape(CHUNK, 128)
    low, high = along_lanes(below), along_lanes(above)
    rows = lax.broadcasted_iota(jnp.int32, (16, CHUNK), 0)
    ones = jnp.where(rows < 8, low, high).astype(BF16)
    low, high = low[0:1].astype(BF16), high[0:1].astype(BF16)
    values = jnp.concatenate([vt[:HD] * low, vt[HD:] * high, ones], axis=0)
    return k.reshape(CHUNK, 128), chosen, values


def attend(nq, nc, held, packed, *refs):
    q_refs, refs = refs[:nq], refs[nq:]
    key_refs, refs = refs[: 2 * nc], refs[2 * nc :]
    old_refs, refs = (refs[:nq], refs[nq:]) if held else ((None,) * nq, refs)
    out_refs, refs = refs[:nq], refs[nq:]
    sum_refs = refs if packed else out_refs
    one = jnp.ones((16, CHUNK), BF16)
    for c in range(nc):
        keys = load_chunk(key_refs[2 * c : 2 * c + 2])
        vt = transposed_values(keys)
        first = jnp.concatenate([vt[:HD], one], axis=0)
        for q_ref, old_ref, out_ref in zip(q_refs, old_refs, sum_refs):
            k, chosen, values = chunk_operands(keys, q_ref, vt)
            a = dot(k[:, :HD], q_ref[HD:128, :])
            b = dot(chosen, q_ref[0:128, :])
            pa = jnp.exp2(a * SCALE).astype(BF16)
            pb = jnp.exp2(b * SCALE).astype(BF16)
            oa = dot(first, pa)
            ob = dot(values, pb)
            new = [ob[:HD], oa[:HD] + ob[HD:128], ob[128:136], oa[HD : HD + 8] + ob[136:144]]
            for start, stop, part in zip((0, HD, 128, 136), (HD, 128, 136, 144), new):
                before = old_ref if c == 0 else out_ref
                out_ref[start:stop, :] = part if before is None else before[start:stop, :] + part
    for q_ref, old_ref, out_ref in zip(q_refs, old_refs, sum_refs):
        bad = jnp.sum(jnp.where(out_ref[128:144, :] < LIMIT, 0.0, 1.0))
        if held:
            bad = bad + jnp.sum(old_ref[144:160, :])
        out_ref[144:160, :] = jnp.zeros((16, ROWS), F32)

        @pl.when(bad > 0.0)
        def _():
            out_ref[...] = old_ref[...] if held else jnp.zeros((PART, ROWS), F32)
            for c in range(nc):
                careful(key_refs[2 * c : 2 * c + 2], q_ref, out_ref)

    if packed:
        for sums, out_ref in zip(sum_refs, out_refs):
            out_ref[0:128, :] = sums[0:128, :].astype(BF16)
            rows = lax.broadcasted_iota(jnp.int32, (16, ROWS), 0)
            stats = jnp.zeros((16, ROWS), F32)
            for at, start in ((0, 128), (2, 136)):
                total = jnp.broadcast_to(sums[start : start + 1, :], (16, ROWS))
                high = total.astype(BF16).astype(F32)
                stats = jnp.where(rows == at, high, stats)
                stats = jnp.where(rows == at + 1, total - high, stats)
            for at, start in ((4, 144), (5, 152)):
                shift = jnp.broadcast_to(sums[start : start + 1, :], (16, ROWS))
                stats = jnp.where(rows == at, shift, stats)
            out_ref[128:144, :] = stats.astype(BF16)


def careful(key_refs, q_ref, out_ref):
    def rounded(x):
        return jnp.maximum(x, 0.0).astype(BF16).astype(F32)

    def rescale(half, new):
        old = out_ref[144 + 8 * half : 145 + 8 * half, :]
        factor = jnp.exp2(old - new)
        out_ref[half * HD : (half + 1) * HD, :] *= factor
        out_ref[128 + 8 * half : 136 + 8 * half, :] *= factor
        out_ref[144 + 8 * half : 152 + 8 * half, :] = jnp.broadcast_to(new, (8, ROWS))

    def raised(half, top):
        return jnp.maximum(out_ref[144 + 8 * half : 145 + 8 * half, :], rounded(top))

    keys = load_chunk(key_refs)
    vt = transposed_values(keys)
    one = jnp.ones((16, CHUNK), BF16)
    first = jnp.concatenate([vt[:HD], one], axis=0)
    k, chosen, values = chunk_operands(keys, q_ref, vt)
    a = dot(k[:, :HD], q_ref[HD:128, :]) * SCALE
    new = raised(1, jnp.max(a, axis=0, keepdims=True))
    rescale(1, new)
    oa = dot(first, jnp.exp2(a - new).astype(BF16))
    out_ref[HD:128, :] += oa[:HD]
    out_ref[136:144, :] += oa[HD : HD + 8]
    b = dot(chosen, q_ref[0:128, :]) * SCALE
    b = b.reshape(GROUP, SPAN, ROWS)
    below, above = chunk_masks(keys, q_ref)

    def top(mask):
        wide = jnp.concatenate([mask] * (ROWS // 128), axis=2)
        return jnp.max(jnp.max(jnp.where(wide > 0.5, b, -1e30), axis=0), axis=0, keepdims=True)

    low, high = raised(0, top(below)), raised(1, top(above))
    rescale(0, low)
    rescale(1, high)
    wide = jnp.concatenate([below] * (ROWS // 128), axis=2)
    known = jnp.concatenate([below + above] * (ROWS // 128), axis=2)
    shift = jnp.where(wide > 0.5, low[None], high[None])
    p = jnp.where(known > 0.5, jnp.exp2(b - shift), 0.0)
    ob = dot(values, p.reshape(CHUNK, ROWS).astype(BF16))
    out_ref[0:128, :] += ob[0:128]
    out_ref[128:144, :] += ob[128:144]


def finish(held, sent, pos_ref, sink_ref, *refs):
    parts, out_ref = refs[: held + sent], refs[held + sent]
    swapped = pos_ref[0] // SPAN >= 128
    results = []
    for half in range(2):
        part = slice(half * HD, (half + 1) * HD)
        terms = [
            (p[144 + 8 * half : 145 + 8 * half, :], p[128 + 8 * half : 129 + 8 * half, :], p[part, :])
            for p in parts[:held]
        ]
        for p in parts[held:]:
            stats = p[128:144, :].astype(F32)
            total = stats[2 * half : 2 * half + 1] + stats[2 * half + 1 : 2 * half + 2]
            terms.append((stats[4 + half : 5 + half], total, p[part, :].astype(F32)))
        top = functools.reduce(jnp.maximum, [shift for shift, _, _ in terms])
        total = jnp.exp2(sink_ref[0:1, :] * LOG2E - top)
        sums = jnp.zeros((HD, ROWS), F32)
        for shift, some, weighted in terms:
            factor = jnp.exp2(shift - top)
            total = total + some * factor
            sums = sums + weighted * factor
        results.append(sums / total)
    both = jnp.transpose(jnp.concatenate(results, axis=0))
    for g in range(HEADS // 2):
        even, odd = both[2 * g * SPAN : (2 * g + 1) * SPAN], both[(2 * g + 1) * SPAN : (2 * g + 2) * SPAN]
        lo = jnp.concatenate([even[:, :HD], odd[:, :HD]], axis=1)
        up = jnp.concatenate([even[:, HD:], odd[:, HD:]], axis=1)
        lanes = slice(128 * g, 128 * (g + 1))
        out_ref[0:SPAN, lanes] = jnp.where(swapped, up, lo).astype(BF16)
        out_ref[SPAN : 2 * SPAN, lanes] = jnp.where(swapped, lo, up).astype(BF16)


def partials(queries, chunks, old=None, packed=False):
    nq, nc = len(queries), len(chunks)
    keys = [part for chunk in chunks for part in chunk]
    pairs = nq * nc * 2 * CHUNK * ROWS
    operands = [*queries, *keys, *(old or [])]
    shape = jax.ShapeDtypeStruct((PART, ROWS), F32)
    if packed:
        shape = jax.ShapeDtypeStruct((QMSG, ROWS), BF16)
    return pl.pallas_call(
        functools.partial(attend, nq, nc, old is not None, packed),
        out_shape=[shape] * nq,
        in_specs=[VMEM] * len(operands),
        out_specs=[VMEM] * nq,
        scratch_shapes=[pltpu.VMEM((PART, ROWS), F32)] * nq if packed else [],
        compiler_params=PARAMS,
        cost_estimate=pl.CostEstimate(
            flops=pairs * 640, bytes_accessed=nc * 2**18, transcendentals=pairs
        ),
        name="attend",
    )(*operands)


def simple(kernel, shape, name, *operands):
    return pl.pallas_call(
        kernel,
        out_shape=shape,
        in_specs=[SMEM] + [VMEM] * (len(operands) - 1),
        out_specs=VMEM,
        compiler_params=PARAMS,
        name=name,
    )(*operands)


def place(index):
    inner, outer = divmod(index, 16)
    return inner % 4, inner // 4 * 2 + outer // 2 % 2, outer // 4, outer % 2


def index_of(x, y, z, core):
    return (y // 2 * 4 + x) * 16 + z * 4 + y % 2 * 2 + core


def move(array, dx=0, dy=0, dz=0, dcore=0):
    pairs = []
    for source in range(128):
        x, y, z, core = place(source)
        target = index_of((x + dx) % 4, (y + dy) % 4, (z + dz) % 4, (core + dcore) % 2)
        pairs.append((source, target))
    return lax.ppermute(array, ("inner", "outer"), pairs)


def shards(queries, key_value, positions, sinks):
    km = simple(
        prepare_keys, jax.ShapeDtypeStruct((MSG, 128), BF16), "prepare_keys", positions, key_value
    )
    qm = simple(
        prepare_queries, jax.ShapeDtypeStruct((QMSG, ROWS), BF16), "prepare_queries", positions, queries
    )
    own = pl.pallas_call(
        diagonal,
        out_shape=jax.ShapeDtypeStruct((PART, ROWS), F32),
        in_specs=[VMEM, VMEM],
        out_specs=VMEM,
        compiler_params=PARAMS,
        name="diagonal",
    )(qm, km)
    row = jnp.stack([km, move(km, dx=1), move(km, dx=-1), move(km, dx=2)])
    near = [qm, move(qm, dy=1), move(qm, dy=-1), move(qm, dy=2)]
    planes = [row, move(row, dz=1), move(row, dz=-1), move(row, dz=2)]
    chunks = [(plane, move(plane, dcore=1)) for plane in planes]
    held = partials(near, chunks[:1])
    held = partials(near, chunks[1:3], held)
    back = []
    for k, dy in ((3, -2), (1, -1), (2, 1)):
        (message,) = partials(near[k : k + 1], chunks[3:], held[k : k + 1], packed=True)
        back.append(move(message, dy=dy))
    (mine,) = partials(near[:1], chunks[3:], held[:1])
    sink_row = jnp.broadcast_to(jnp.repeat(sinks, SPAN)[None], (8, ROWS))
    return simple(
        functools.partial(finish, 2, 3),
        jax.ShapeDtypeStruct(queries.shape, BF16),
        "finish",
        positions,
        sink_row,
        own,
        mine,
        *back,
    )


def solution(mesh):
    return jax.shard_map(
        shards,
        mesh=mesh,
        in_specs=(
            P(("inner", "outer"), None),
            P(("inner", "outer"), None),
            P(("inner", "outer")),
            P(),
        ),
        out_specs=P(("inner", "outer"), None),
        check_vma=False,
    )
```

```python
import functools

import jax
import jax.numpy as jnp
from jax import lax
from jax.experimental import pallas as pl
from jax.experimental.pallas import tpu as pltpu
from jax.sharding import PartitionSpec as P

HEADS = 8
HD = 64
SPAN = 96
ROWS = HEADS * SPAN
GROUP = 8
CHUNK = GROUP * SPAN
MSG = 208
QMSG = 144
PART = 160
LOG2E = 1.4426950408889634
SCALE = HD**-0.5 * LOG2E
LIMIT = 1e36
F32 = jnp.float32
BF16 = jnp.bfloat16
VMEM = pl.BlockSpec(memory_space=pltpu.VMEM)
SMEM = pl.BlockSpec(memory_space=pltpu.SMEM)
PARAMS = pltpu.CompilerParams(vmem_limit_bytes=32 << 20)


def dot(a, b):
    return jnp.dot(a, b, preferred_element_type=F32)


def prepare_keys(pos_ref, kv_ref, km_ref):
    run = pos_ref[0] // SPAN
    swapped = run >= 128
    lower = jnp.where(swapped, 255 - run, run).astype(F32)
    lo, up = halves(kv_ref, swapped)
    km_ref[0:SPAN, :] = jnp.concatenate([lo[:, :HD], up[:, :HD]], axis=1)
    km_ref[SPAN : 2 * SPAN, :] = jnp.concatenate([lo[:, HD:], up[:, HD:]], axis=1)
    km_ref[2 * SPAN :, :] = jnp.full((MSG - 2 * SPAN, 128), lower, F32).astype(BF16)


def prepare_queries(pos_ref, q_ref, qm_ref):
    run = pos_ref[0] // SPAN
    swapped = run >= 128
    lower = jnp.where(swapped, 255 - run, run).astype(F32)
    lo, up = halves(q_ref, swapped)
    stacked = jnp.concatenate(
        [
            jnp.concatenate([lo[:, h * HD : (h + 1) * HD], up[:, h * HD : (h + 1) * HD]], axis=1)
            for h in range(HEADS)
        ],
        axis=0,
    )
    qm_ref[0:128, :] = jnp.transpose(stacked)
    qm_ref[128:, :] = jnp.full((QMSG - 128, ROWS), lower, F32).astype(BF16)


def halves(ref, swapped):
    first, second = ref[0:SPAN, :], ref[SPAN : 2 * SPAN, :]
    return jnp.where(swapped, second, first), jnp.where(swapped, first, second)


def diagonal(qm_ref, km_ref, out_ref):
    keys = lax.broadcasted_iota(jnp.int32, (SPAN, ROWS), 0)
    rows = lax.broadcasted_iota(jnp.int32, (SPAN, ROWS), 1)
    mine = rows
    for h in range(1, HEADS):
        mine = jnp.where(rows >= h * SPAN, rows - h * SPAN, mine)
    visible = keys <= mine
    k = km_ref[0:SPAN, :]
    v = jnp.transpose(km_ref[SPAN : 2 * SPAN, :].astype(F32)).astype(BF16)
    for half in range(2):
        part = slice(half * HD, (half + 1) * HD)
        s = dot(k[:, part], qm_ref[part, :]) * SCALE
        s = jnp.where(visible, s, -1e30)
        shift = jnp.maximum(jnp.max(s, axis=0, keepdims=True), 0.0)
        p = jnp.where(visible, jnp.exp2(s - shift), 0.0)
        out_ref[part, :] = dot(v[part, :], p.astype(BF16))
        total = jnp.sum(p, axis=0, keepdims=True)
        out_ref[128 + 8 * half : 136 + 8 * half, :] = jnp.broadcast_to(total, (8, ROWS))
        out_ref[144 + 8 * half : 152 + 8 * half, :] = jnp.broadcast_to(shift, (8, ROWS))


def chunk_masks(keys, q_ref):
    info = keys[:, 2 * SPAN : 2 * SPAN + 16, :].astype(F32)[:, 0:1, :]
    own = q_ref[128:144, 0:128].astype(F32)[0:1, :]
    below = jnp.where(info < own[None], 1.0, 0.0)
    above = jnp.where(info > own[None], 1.0, 0.0)
    return below, above


def along_lanes(mask):
    lanes = lax.broadcasted_iota(jnp.int32, (16, CHUNK), 1)
    wide = [
        jnp.concatenate([jnp.broadcast_to(mask[b], (16, 128))] * (CHUNK // 128), axis=1)
        for b in range(GROUP)
    ]
    out = wide[0]
    for b in range(1, GROUP):
        out = jnp.where(lanes >= b * SPAN, wide[b], out)
    return out


def load_chunk(key_refs):
    return jnp.concatenate([ref[...] for ref in key_refs], axis=0)


def transposed_values(keys):
    return jnp.transpose(keys[:, SPAN : 2 * SPAN, :].reshape(CHUNK, 128))


def chunk_operands(keys, q_ref, vt):
    below, above = chunk_masks(keys, q_ref)
    k = keys[:, 0:SPAN, :]
    lanes = lax.broadcasted_iota(jnp.int32, (GROUP, 1, 128), 2)
    keep = jnp.where(lanes < HD, below, above).astype(BF16)
    chosen = (k * keep).reshape(CHUNK, 128)
    low, high = along_lanes(below), along_lanes(above)
    rows = lax.broadcasted_iota(jnp.int32, (16, CHUNK), 0)
    ones = jnp.where(rows < 8, low, high).astype(BF16)
    low, high = low[0:1].astype(BF16), high[0:1].astype(BF16)
    values = jnp.concatenate([vt[:HD] * low, vt[HD:] * high, ones], axis=0)
    return k.reshape(CHUNK, 128), chosen, values


def attend(nq, nc, held, packed, *refs):
    q_refs, refs = refs[:nq], refs[nq:]
    key_refs, refs = refs[: 2 * nc], refs[2 * nc :]
    old_refs, refs = (refs[:nq], refs[nq:]) if held else ((None,) * nq, refs)
    out_refs, refs = refs[:nq], refs[nq:]
    sum_refs = refs if packed else out_refs
    one = jnp.ones((16, CHUNK), BF16)
    for c in range(nc):
        keys = load_chunk(key_refs[2 * c : 2 * c + 2])
        vt = transposed_values(keys)
        first = jnp.concatenate([vt[:HD], one], axis=0)
        for q_ref, old_ref, out_ref in zip(q_refs, old_refs, sum_refs):
            k, chosen, values = chunk_operands(keys, q_ref, vt)
            a = dot(k[:, :HD], q_ref[HD:128, :])
            b = dot(chosen, q_ref[0:128, :])
            pa = jnp.exp2(a * SCALE).astype(BF16)
            pb = jnp.exp2(b * SCALE).astype(BF16)
            oa = dot(first, pa)
            ob = dot(values, pb)
            new = [ob[:HD], oa[:HD] + ob[HD:128], ob[128:136], oa[HD : HD + 8] + ob[136:144]]
            for start, stop, part in zip((0, HD, 128, 136), (HD, 128, 136, 144), new):
                before = old_ref if c == 0 else out_ref
                out_ref[start:stop, :] = part if before is None else before[start:stop, :] + part
    for q_ref, old_ref, out_ref in zip(q_refs, old_refs, sum_refs):
        bad = jnp.sum(jnp.where(out_ref[128:144, :] < LIMIT, 0.0, 1.0))
        if held:
            bad = bad + jnp.sum(old_ref[144:160, :])
        out_ref[144:160, :] = jnp.zeros((16, ROWS), F32)

        @pl.when(bad > 0.0)
        def _():
            out_ref[...] = old_ref[...] if held else jnp.zeros((PART, ROWS), F32)
            for c in range(nc):
                careful(key_refs[2 * c : 2 * c + 2], q_ref, out_ref)

    if packed:
        for sums, out_ref in zip(sum_refs, out_refs):
            out_ref[0:128, :] = sums[0:128, :].astype(BF16)
            rows = lax.broadcasted_iota(jnp.int32, (16, ROWS), 0)
            stats = jnp.zeros((16, ROWS), F32)
            for at, start in ((0, 128), (2, 136)):
                total = jnp.broadcast_to(sums[start : start + 1, :], (16, ROWS))
                high = total.astype(BF16).astype(F32)
                stats = jnp.where(rows == at, high, stats)
                stats = jnp.where(rows == at + 1, total - high, stats)
            for at, start in ((4, 144), (5, 152)):
                shift = jnp.broadcast_to(sums[start : start + 1, :], (16, ROWS))
                stats = jnp.where(rows == at, shift, stats)
            out_ref[128:144, :] = stats.astype(BF16)


def careful(key_refs, q_ref, out_ref):
    def rounded(x):
        return jnp.maximum(x, 0.0).astype(BF16).astype(F32)

    def rescale(half, new):
        old = out_ref[144 + 8 * half : 145 + 8 * half, :]
        factor = jnp.exp2(old - new)
        out_ref[half * HD : (half + 1) * HD, :] *= factor
        out_ref[128 + 8 * half : 136 + 8 * half, :] *= factor
        out_ref[144 + 8 * half : 152 + 8 * half, :] = jnp.broadcast_to(new, (8, ROWS))

    def raised(half, top):
        return jnp.maximum(out_ref[144 + 8 * half : 145 + 8 * half, :], rounded(top))

    keys = load_chunk(key_refs)
    vt = transposed_values(keys)
    one = jnp.ones((16, CHUNK), BF16)
    first = jnp.concatenate([vt[:HD], one], axis=0)
    k, chosen, values = chunk_operands(keys, q_ref, vt)
    a = dot(k[:, :HD], q_ref[HD:128, :]) * SCALE
    new = raised(1, jnp.max(a, axis=0, keepdims=True))
    rescale(1, new)
    oa = dot(first, jnp.exp2(a - new).astype(BF16))
    out_ref[HD:128, :] += oa[:HD]
    out_ref[136:144, :] += oa[HD : HD + 8]
    b = dot(chosen, q_ref[0:128, :]) * SCALE
    b = b.reshape(GROUP, SPAN, ROWS)
    below, above = chunk_masks(keys, q_ref)

    def top(mask):
        wide = jnp.concatenate([mask] * (ROWS // 128), axis=2)
        return jnp.max(jnp.max(jnp.where(wide > 0.5, b, -1e30), axis=0), axis=0, keepdims=True)

    low, high = raised(0, top(below)), raised(1, top(above))
    rescale(0, low)
    rescale(1, high)
    wide = jnp.concatenate([below] * (ROWS // 128), axis=2)
    known = jnp.concatenate([below + above] * (ROWS // 128), axis=2)
    shift = jnp.where(wide > 0.5, low[None], high[None])
    p = jnp.where(known > 0.5, jnp.exp2(b - shift), 0.0)
    ob = dot(values, p.reshape(CHUNK, ROWS).astype(BF16))
    out_ref[0:128, :] += ob[0:128]
    out_ref[128:144, :] += ob[128:144]


def finish(held, sent, pos_ref, sink_ref, *refs):
    parts, out_ref = refs[: held + sent], refs[held + sent]
    swapped = pos_ref[0] // SPAN >= 128
    results = []
    for half in range(2):
        part = slice(half * HD, (half + 1) * HD)
        terms = [
            (p[144 + 8 * half : 145 + 8 * half, :], p[128 + 8 * half : 129 + 8 * half, :], p[part, :])
            for p in parts[:held]
        ]
        for p in parts[held:]:
            stats = p[128:144, :].astype(F32)
            total = stats[2 * half : 2 * half + 1] + stats[2 * half + 1 : 2 * half + 2]
            terms.append((stats[4 + half : 5 + half], total, p[part, :].astype(F32)))
        top = functools.reduce(jnp.maximum, [shift for shift, _, _ in terms])
        total = jnp.exp2(sink_ref[0:1, :] * LOG2E - top)
        sums = jnp.zeros((HD, ROWS), F32)
        for shift, some, weighted in terms:
            factor = jnp.exp2(shift - top)
            total = total + some * factor
            sums = sums + weighted * factor
        results.append(sums / total)
    both = jnp.transpose(jnp.concatenate(results, axis=0))
    for g in range(HEADS // 2):
        even, odd = both[2 * g * SPAN : (2 * g + 1) * SPAN], both[(2 * g + 1) * SPAN : (2 * g + 2) * SPAN]
        lo = jnp.concatenate([even[:, :HD], odd[:, :HD]], axis=1)
        up = jnp.concatenate([even[:, HD:], odd[:, HD:]], axis=1)
        lanes = slice(128 * g, 128 * (g + 1))
        out_ref[0:SPAN, lanes] = jnp.where(swapped, up, lo).astype(BF16)
        out_ref[SPAN : 2 * SPAN, lanes] = jnp.where(swapped, lo, up).astype(BF16)


def partials(queries, chunks, old=None, packed=False):
    nq, nc = len(queries), len(chunks)
    keys = [part for chunk in chunks for part in chunk]
    pairs = nq * nc * 2 * CHUNK * ROWS
    operands = [*queries, *keys, *(old or [])]
    shape = jax.ShapeDtypeStruct((PART, ROWS), F32)
    if packed:
        shape = jax.ShapeDtypeStruct((QMSG, ROWS), BF16)
    return pl.pallas_call(
        functools.partial(attend, nq, nc, old is not None, packed),
        out_shape=[shape] * nq,
        in_specs=[VMEM] * len(operands),
        out_specs=[VMEM] * nq,
        scratch_shapes=[pltpu.VMEM((PART, ROWS), F32)] * nq if packed else [],
        compiler_params=PARAMS,
        cost_estimate=pl.CostEstimate(
            flops=pairs * 16, bytes_accessed=nc * 2**14, transcendentals=0
        ),
        name="attend",
    )(*operands)


def simple(kernel, shape, name, *operands):
    return pl.pallas_call(
        kernel,
        out_shape=shape,
        in_specs=[SMEM] + [VMEM] * (len(operands) - 1),
        out_specs=VMEM,
        compiler_params=PARAMS,
        name=name,
    )(*operands)


def place(index):
    inner, outer = divmod(index, 16)
    return inner % 4, inner // 4 * 2 + outer // 2 % 2, outer // 4, outer % 2


def index_of(x, y, z, core):
    return (y // 2 * 4 + x) * 16 + z * 4 + y % 2 * 2 + core


def move(array, dx=0, dy=0, dz=0, dcore=0):
    pairs = []
    for source in range(128):
        x, y, z, core = place(source)
        target = index_of((x + dx) % 4, (y + dy) % 4, (z + dz) % 4, (core + dcore) % 2)
        pairs.append((source, target))
    return lax.ppermute(array, ("inner", "outer"), pairs)


def after(array, *others):
    return lax.optimization_barrier((array, *others))[0]


def shards(queries, key_value, positions, sinks):
    km = simple(
        prepare_keys, jax.ShapeDtypeStruct((MSG, 128), BF16), "prepare_keys", positions, key_value
    )
    right, left, far = move(km, dx=1), move(km, dx=-1), move(km, dx=2)
    qm = simple(
        prepare_queries, jax.ShapeDtypeStruct((QMSG, ROWS), BF16), "prepare_queries", positions, queries
    )
    asked = after(qm, right)
    near = {0: qm, 1: move(asked, dy=1), -1: move(asked, dy=-1), 2: move(asked, dy=2)}
    row = jnp.stack([km, right, left, far])
    planes = [row, move(row, dz=1), move(row, dz=-1), move(row, dz=2)]
    chunks = [(plane, move(plane, dcore=1)) for plane in planes]
    order = [(1, 0), (-1, 0), (2, 0), (2, 1), (2, 2), (1, 1), (-1, 1), (2, 3)]
    order += [(1, 2), (1, 3), (-1, 2), (-1, 3), (0, 0), (0, 1), (0, 2), (0, 3)]
    held, back, last = {}, [], None
    for k, c in order:
        query = near[k] if last is None else after(near[k], last)
        if k == 0 and c in (1, 3):
            query = after(query, back[c // 2])
        packed = k != 0 and c == 3
        old = [held[k]] if k in held else None
        (last,) = partials([query], [chunks[c]], old, packed)
        if packed:
            back.append(move(last, dy=-k))
        else:
            held[k] = last
    own = pl.pallas_call(
        diagonal,
        out_shape=jax.ShapeDtypeStruct((PART, ROWS), F32),
        in_specs=[VMEM, VMEM],
        out_specs=VMEM,
        compiler_params=PARAMS,
        name="diagonal",
    )(after(qm, last), km)
    sink_row = jnp.broadcast_to(jnp.repeat(sinks, SPAN)[None], (8, ROWS))
    return simple(
        functools.partial(finish, 2, 3),
        jax.ShapeDtypeStruct(queries.shape, BF16),
        "finish",
        positions,
        sink_row,
        own,
        held[0],
        *back,
    )


def solution(mesh):
    return jax.shard_map(
        shards,
        mesh=mesh,
        in_specs=(
            P(("inner", "outer"), None),
            P(("inner", "outer"), None),
            P(("inner", "outer")),
            P(),
        ),
        out_specs=P(("inner", "outer"), None),
        check_vma=False,
    )
```

```python
import functools

import jax
import jax.numpy as jnp
from jax import lax
from jax.experimental import pallas as pl
from jax.experimental.pallas import tpu as pltpu
from jax.sharding import PartitionSpec as P

HEADS = 8
HD = 64
SPAN = 96
ROWS = HEADS * SPAN
GROUP = 8
CHUNK = GROUP * SPAN
MSG = 208
QMSG = 144
PART = 160
LOG2E = 1.4426950408889634
SCALE = HD**-0.5 * LOG2E
LIMIT = 1e36
F32 = jnp.float32
BF16 = jnp.bfloat16
VMEM = pl.BlockSpec(memory_space=pltpu.VMEM)
SMEM = pl.BlockSpec(memory_space=pltpu.SMEM)
PARAMS = pltpu.CompilerParams(vmem_limit_bytes=32 << 20)


def dot(a, b):
    return jnp.dot(a, b, preferred_element_type=F32)


def halves(ref, swapped):
    first, second = ref[0:SPAN, :], ref[SPAN : 2 * SPAN, :]
    return jnp.where(swapped, second, first), jnp.where(swapped, first, second)


def prepare_keys(pos_ref, pos2_ref, kv_ref, kv2_ref, km_ref, flag_ref):
    for at, (pos, kv) in enumerate(((pos_ref, kv_ref), (pos2_ref, kv2_ref))):
        run = pos[0] // SPAN
        swapped = run >= 128
        lower = jnp.where(swapped, 255 - run, run).astype(F32)
        lo, up = halves(kv, swapped)
        km_ref[at, 0:SPAN, :] = jnp.concatenate([lo[:, :HD], up[:, :HD]], axis=1)
        km_ref[at, SPAN : 2 * SPAN, :] = jnp.concatenate([lo[:, HD:], up[:, HD:]], axis=1)
        km_ref[at, 2 * SPAN :, :] = jnp.full((MSG - 2 * SPAN, 128), lower, F32).astype(BF16)
        if at == 0:
            flag_ref[...] = jnp.full((8, 128), jnp.where(swapped, 1.0, 0.0), F32)


def prepare_queries(flag_ref, km_ref, q_ref, qm_ref):
    swapped = jnp.concatenate([flag_ref[0:1, :]] * (HEADS * HD // 128), axis=1) > 0.5
    swapped = jnp.broadcast_to(swapped, (SPAN, HEADS * HD))
    first, second = q_ref[0:SPAN, :].astype(F32), q_ref[SPAN : 2 * SPAN, :].astype(F32)
    lo = jnp.where(swapped, second, first).astype(BF16)
    up = jnp.where(swapped, first, second).astype(BF16)
    stacked = jnp.concatenate(
        [
            jnp.concatenate([lo[:, h * HD : (h + 1) * HD], up[:, h * HD : (h + 1) * HD]], axis=1)
            for h in range(HEADS)
        ],
        axis=0,
    )
    qm_ref[0:128, :] = jnp.transpose(stacked)
    qm_ref[128:, :] = jnp.concatenate([km_ref[0, 2 * SPAN :, :]] * (ROWS // 128), axis=1)


def diagonal(qm_ref, km_ref, out_ref):
    keys = lax.broadcasted_iota(jnp.int32, (SPAN, ROWS), 0)
    rows = lax.broadcasted_iota(jnp.int32, (SPAN, ROWS), 1)
    mine = rows
    for h in range(1, HEADS):
        mine = jnp.where(rows >= h * SPAN, rows - h * SPAN, mine)
    visible = keys <= mine
    k = km_ref[0, 0:SPAN, :]
    v = jnp.transpose(km_ref[0, SPAN : 2 * SPAN, :].astype(F32)).astype(BF16)
    for half in range(2):
        part = slice(half * HD, (half + 1) * HD)
        s = dot(k[:, part], qm_ref[part, :]) * SCALE
        s = jnp.where(visible, s, -1e30)
        shift = jnp.maximum(jnp.max(s, axis=0, keepdims=True), 0.0)
        p = jnp.where(visible, jnp.exp2(s - shift), 0.0)
        out_ref[part, :] = dot(v[part, :], p.astype(BF16))
        total = jnp.sum(p, axis=0, keepdims=True)
        out_ref[128 + 8 * half : 136 + 8 * half, :] = jnp.broadcast_to(total, (8, ROWS))
        out_ref[144 + 8 * half : 152 + 8 * half, :] = jnp.broadcast_to(shift, (8, ROWS))


def chunk_masks(keys, q_ref):
    info = keys[:, 2 * SPAN : 2 * SPAN + 16, :].astype(F32)[:, 0:1, :]
    own = q_ref[128:144, 0:128].astype(F32)[0:1, :]
    below = jnp.where(info < own[None], 1.0, 0.0)
    above = jnp.where(info > own[None], 1.0, 0.0)
    return below, above


def along_lanes(mask):
    lanes = lax.broadcasted_iota(jnp.int32, (16, CHUNK), 1)
    wide = [
        jnp.concatenate([jnp.broadcast_to(mask[b], (16, 128))] * (CHUNK // 128), axis=1)
        for b in range(GROUP)
    ]
    out = wide[0]
    for b in range(1, GROUP):
        out = jnp.where(lanes >= b * SPAN, wide[b], out)
    return out


def transposed_values(keys):
    return jnp.transpose(keys[:, SPAN : 2 * SPAN, :].reshape(CHUNK, 128))


def chunk_operands(keys, q_ref, vt):
    below, above = chunk_masks(keys, q_ref)
    k = keys[:, 0:SPAN, :]
    lanes = lax.broadcasted_iota(jnp.int32, (GROUP, 1, 128), 2)
    keep = jnp.where(lanes < HD, below, above).astype(BF16)
    chosen = (k * keep).reshape(CHUNK, 128)
    low, high = along_lanes(below), along_lanes(above)
    rows = lax.broadcasted_iota(jnp.int32, (16, CHUNK), 0)
    ones = jnp.where(rows < 8, low, high).astype(BF16)
    low, high = low[0:1].astype(BF16), high[0:1].astype(BF16)
    values = jnp.concatenate([vt[:HD] * low, vt[HD:] * high, ones], axis=0)
    return k.reshape(CHUNK, 128), chosen, values


def each(count, body):
    if count == 1:
        body(0)
    else:
        pl.loop(0, count)(body)


def attend(nq, nc, at, packed, *refs):
    q_refs, refs = refs[:nq], refs[nq:]
    key_refs, refs = refs[:nc], refs[nc:]
    if at is not None:
        old_ref, refs = refs[0], refs[1:]
    out_ref, refs = refs[0], refs[1:]
    sums = refs[0] if packed else out_ref
    queries, keys = refs[-2], refs[-1]
    for q in range(nq):
        queries[q] = q_refs[q][...]
        sums[q] = jnp.zeros((PART, ROWS), F32) if at is None else old_ref[at + q]
    for c in range(nc):
        keys[c] = key_refs[c][...]

    def add(c):
        chunk = keys[c]
        vt = transposed_values(chunk)
        first = jnp.concatenate([vt[:HD], jnp.ones((16, CHUNK), BF16)], axis=0)

        def one(q):
            q_ref = queries.at[q]
            k, chosen, values = chunk_operands(chunk, q_ref, vt)
            a = dot(k[:, :HD], q_ref[HD:128, :])
            b = dot(chosen, q_ref[0:128, :])
            pa = jnp.exp2(a * SCALE).astype(BF16)
            pb = jnp.exp2(b * SCALE).astype(BF16)
            oa = dot(first, pa)
            ob = dot(values, pb)
            sums[q, 0:HD, :] += ob[:HD]
            sums[q, HD:128, :] += oa[:HD] + ob[HD:128]
            sums[q, 128:136, :] += ob[128:136]
            sums[q, 136:144, :] += oa[HD : HD + 8] + ob[136:144]

        each(nq, one)

    each(nc, add)

    def check(q):
        bad = jnp.sum(jnp.where(sums[q, 128:144, :] < LIMIT, 0.0, 1.0))
        bad = bad + jnp.sum(sums[q, 144:160, :])

        @pl.when(bad > 0.0)
        def _():
            for k in range(nq):

                @pl.when(q == k)
                def _():
                    sums[k] = jnp.zeros((PART, ROWS), F32) if at is None else old_ref[at + k]

            @pl.loop(0, nc)
            def _(c):
                careful(keys.at[c], queries.at[q], sums.at[q])

    each(nq, check)

    if packed:
        for q in range(nq):
            out_ref[0:128, :] = sums[q, 0:128, :].astype(BF16)
            rows = lax.broadcasted_iota(jnp.int32, (16, ROWS), 0)
            stats = jnp.zeros((16, ROWS), F32)
            for row, start in ((0, 128), (2, 136)):
                total = jnp.broadcast_to(sums[q, start : start + 1, :], (16, ROWS))
                high = total.astype(BF16).astype(F32)
                stats = jnp.where(rows == row, high, stats)
                stats = jnp.where(rows == row + 1, total - high, stats)
            for row, start in ((4, 144), (5, 152)):
                shift = jnp.broadcast_to(sums[q, start : start + 1, :], (16, ROWS))
                stats = jnp.where(rows == row, shift, stats)
            out_ref[128:144, :] = stats.astype(BF16)


def careful(keys, q_ref, out_ref):
    def raise_shift(half, top):
        old = out_ref[144 + 8 * half : 145 + 8 * half, :]
        new = jnp.maximum(old, jnp.maximum(top, 0.0).astype(BF16).astype(F32))
        factor = jnp.exp2(old - new)
        out_ref[half * HD : (half + 1) * HD, :] *= factor
        out_ref[128 + 8 * half : 136 + 8 * half, :] *= factor
        out_ref[144 + 8 * half : 152 + 8 * half, :] = jnp.broadcast_to(new, (8, ROWS))
        return new

    def add(half, values, p):
        p = p.astype(BF16)
        out_ref[half * HD : (half + 1) * HD, :] += dot(values, p)
        out_ref[128 + 8 * half : 136 + 8 * half, :] += dot(jnp.ones((16, SPAN), BF16), p)[:8]

    def wide(row):
        return jnp.concatenate([row] * (ROWS // 128), axis=1)

    own = wide(q_ref[128:144, 0:128].astype(F32)[0:1, :])

    @pl.loop(0, GROUP)
    def _(b):
        k = keys[b, 0:SPAN, :]
        vt = jnp.transpose(keys[b, SPAN : 2 * SPAN, :].astype(F32)).astype(BF16)
        info = wide(keys[b, 2 * SPAN : 2 * SPAN + 16, :].astype(F32)[0:1, :])
        low = dot(k[:, :HD], q_ref[HD:128, :]) * SCALE
        shift = raise_shift(1, jnp.max(low, axis=0, keepdims=True))
        add(1, vt[:HD], jnp.exp2(low - shift))
        for half, seen in ((0, info < own), (1, info > own)):
            part = slice(half * HD, (half + 1) * HD)
            s = dot(k[:, part], q_ref[part, :]) * SCALE
            top = jnp.where(seen, jnp.max(s, axis=0, keepdims=True), -1e30)
            shift = raise_shift(half, top)
            add(half, vt[part], jnp.where(seen, jnp.exp2(s - shift), 0.0))


def finish(held, sent, flag_ref, sink_ref, *refs):
    parts, out_ref = refs[: held + sent], refs[held + sent]
    swapped = jnp.broadcast_to(flag_ref[0:1, :], (SPAN, 128)) > 0.5
    results = []
    for half in range(2):
        part = slice(half * HD, (half + 1) * HD)
        terms = [
            (p[144 + 8 * half : 145 + 8 * half, :], p[128 + 8 * half : 129 + 8 * half, :], p[part, :])
            for p in parts[:held]
        ]
        for p in parts[held:]:
            stats = p[128:144, :].astype(F32)
            total = stats[2 * half : 2 * half + 1] + stats[2 * half + 1 : 2 * half + 2]
            terms.append((stats[4 + half : 5 + half], total, p[part, :].astype(F32)))
        top = functools.reduce(jnp.maximum, [shift for shift, _, _ in terms])
        total = jnp.exp2(sink_ref[0:1, :] * LOG2E - top)
        sums = jnp.zeros((HD, ROWS), F32)
        for shift, some, weighted in terms:
            factor = jnp.exp2(shift - top)
            total = total + some * factor
            sums = sums + weighted * factor
        results.append(sums / total)
    both = jnp.transpose(jnp.concatenate(results, axis=0))
    for g in range(HEADS // 2):
        even, odd = both[2 * g * SPAN : (2 * g + 1) * SPAN], both[(2 * g + 1) * SPAN : (2 * g + 2) * SPAN]
        lo = jnp.concatenate([even[:, :HD], odd[:, :HD]], axis=1)
        up = jnp.concatenate([even[:, HD:], odd[:, HD:]], axis=1)
        lanes = slice(128 * g, 128 * (g + 1))
        out_ref[0:SPAN, lanes] = jnp.where(swapped, up, lo).astype(BF16)
        out_ref[SPAN : 2 * SPAN, lanes] = jnp.where(swapped, lo, up).astype(BF16)


def partials(queries, chunks, old=None, at=None, packed=False):
    nq, nc = len(queries), len(chunks)
    pairs = nq * nc * 2 * CHUNK * ROWS
    operands = [*queries, *chunks, *([] if at is None else [old])]
    sums = (nq, PART, ROWS)
    shape = jax.ShapeDtypeStruct(sums, F32)
    if packed:
        shape = jax.ShapeDtypeStruct((QMSG, ROWS), BF16)
    return pl.pallas_call(
        functools.partial(attend, nq, nc, at, packed),
        out_shape=shape,
        in_specs=[VMEM] * len(operands),
        out_specs=VMEM,
        scratch_shapes=([pltpu.VMEM(sums, F32)] if packed else [])
        + [pltpu.VMEM((nq, QMSG, ROWS), BF16), pltpu.VMEM((nc, GROUP, MSG, 128), BF16)],
        compiler_params=PARAMS,
        cost_estimate=pl.CostEstimate(
            flops=pairs * 16, bytes_accessed=nc * 2**14, transcendentals=0
        ),
        name="attend",
    )(*operands)


def simple(kernel, shape, name, *operands, scalars=0):
    return pl.pallas_call(
        kernel,
        out_shape=shape,
        in_specs=[SMEM] * scalars + [VMEM] * (len(operands) - scalars),
        out_specs=jax.tree.map(lambda _: VMEM, shape),
        compiler_params=PARAMS,
        name=name,
    )(*operands)


def place(index):
    inner, outer = divmod(index, 16)
    return inner % 4, inner // 4 * 2 + outer // 2 % 2, outer // 4, outer % 2


def index_of(x, y, z, core):
    return (y // 2 * 4 + x) * 16 + z * 4 + y % 2 * 2 + core


def move(array, dx=0, dy=0, dz=0, dcore=0):
    pairs = []
    for source in range(128):
        x, y, z, core = place(source)
        target = index_of((x + dx) % 4, (y + dy) % 4, (z + dz) % 4, (core + dcore) % 2)
        pairs.append((source, target))
    return lax.ppermute(array, ("inner", "outer"), pairs)


def after(array, *others):
    return lax.optimization_barrier((array, *others))[0]


def shards(queries, key_value, positions, sinks):
    pair, flag = simple(
        prepare_keys,
        (jax.ShapeDtypeStruct((2, MSG, 128), BF16), jax.ShapeDtypeStruct((8, 128), F32)),
        "prepare_keys",
        positions,
        move(positions, dcore=1),
        key_value,
        move(key_value, dcore=1),
        scalars=2,
    )
    right, left, far = move(pair, dx=1), move(pair, dx=-1), move(pair, dx=2)
    qm = simple(
        prepare_queries, jax.ShapeDtypeStruct((QMSG, ROWS), BF16), "prepare_queries", flag, pair, queries
    )
    asked = after(qm, right)
    up, down, over = move(asked, dy=1), move(asked, dy=-1), move(asked, dy=2)
    row = jnp.concatenate([pair, right, left, far], axis=0)
    above, below, beyond = move(row, dz=1), move(row, dz=-1), move(row, dz=2)
    three = partials([qm, up, down], [row])
    three = partials([qm, up, down], [after(above, three)], three, 0)
    planes = [row, above, below, beyond]
    sent = [partials([after(over, three)], planes, packed=True)]
    back = [move(sent[0], dy=2)]
    for at, query, dy in ((1, up, -1), (2, down, 1)):
        sent.append(partials([after(query, sent[-1])], planes[2:], three, at, packed=True))
        back.append(move(sent[-1], dy=dy))
    mine = partials([after(qm, sent[-1])], planes[2:3], three, 0)
    mine = partials([after(qm, mine, back[0])], planes[3:], mine, 0)
    own = pl.pallas_call(
        diagonal,
        out_shape=jax.ShapeDtypeStruct((PART, ROWS), F32),
        in_specs=[VMEM, VMEM],
        out_specs=VMEM,
        compiler_params=PARAMS,
        name="diagonal",
    )(after(qm, mine, back[1]), pair)
    sink_row = jnp.broadcast_to(jnp.repeat(sinks, SPAN)[None], (8, ROWS))
    return simple(
        functools.partial(finish, 2, 3),
        jax.ShapeDtypeStruct(queries.shape, BF16),
        "finish",
        flag,
        sink_row,
        own,
        mine.reshape(PART, ROWS),
        *back,
    )


def solution(mesh):
    return jax.shard_map(
        shards,
        mesh=mesh,
        in_specs=(
            P(("inner", "outer"), None),
            P(("inner", "outer"), None),
            P(("inner", "outer")),
            P(),
        ),
        out_specs=P(("inner", "outer"), None),
        check_vma=False,
    )
```

```python
import functools

import jax
import jax.numpy as jnp
from jax import lax
from jax.experimental import pallas as pl
from jax.experimental.pallas import tpu as pltpu
from jax.sharding import PartitionSpec as P

HEADS = 8
HD = 64
SPAN = 96
ROWS = HEADS * SPAN
GROUP = 8
CHUNK = GROUP * SPAN
MSG = 208
QMSG = 144
PART = 160
LOG2E = 1.4426950408889634
SCALE = HD**-0.5 * LOG2E
LIMIT = 1e36
F32 = jnp.float32
BF16 = jnp.bfloat16
VMEM = pl.BlockSpec(memory_space=pltpu.VMEM)
HBM = pl.BlockSpec(memory_space=pltpu.HBM)
PARAMS = pltpu.CompilerParams(vmem_limit_bytes=32 << 20)


def dot(a, b):
    return jnp.dot(a, b, preferred_element_type=F32)


def prepare(pos_hbm, q_hbm, kv_hbm, qm_ref, km_ref, flag_ref, pos_ref, q_ref, kv_ref, sems):
    copies = [
        pltpu.make_async_copy(source, target, sems.at[n])
        for n, (source, target) in enumerate(((pos_hbm, pos_ref), (kv_hbm, kv_ref), (q_hbm, q_ref)))
    ]
    for copy in copies:
        copy.start()
    copies[0].wait()
    run = pos_ref[0] // SPAN
    swapped = run >= 128
    lower = jnp.where(swapped, 255 - run, run).astype(F32)
    flag_ref[...] = jnp.full((8, 128), jnp.where(swapped, 1.0, 0.0), F32)

    def halves(ref):
        first, second = ref[0:SPAN, :], ref[SPAN : 2 * SPAN, :]
        return jnp.where(swapped, second, first), jnp.where(swapped, first, second)

    copies[1].wait()
    lo, up = halves(kv_ref)
    km_ref[0, 0:SPAN, :] = jnp.concatenate([lo[:, :HD], up[:, :HD]], axis=1)
    km_ref[0, SPAN : 2 * SPAN, :] = jnp.concatenate([lo[:, HD:], up[:, HD:]], axis=1)
    km_ref[0, 2 * SPAN :, :] = jnp.full((MSG - 2 * SPAN, 128), lower, F32).astype(BF16)
    copies[2].wait()
    lo, up = halves(q_ref)
    stacked = jnp.concatenate(
        [
            jnp.concatenate([lo[:, h * HD : (h + 1) * HD], up[:, h * HD : (h + 1) * HD]], axis=1)
            for h in range(HEADS)
        ],
        axis=0,
    )
    qm_ref[0:128, :] = jnp.transpose(stacked)
    qm_ref[128:, :] = jnp.full((QMSG - 128, ROWS), lower, F32).astype(BF16)


def diagonal(qm_ref, km_ref, out_ref):
    keys = lax.broadcasted_iota(jnp.int32, (SPAN, ROWS), 0)
    rows = lax.broadcasted_iota(jnp.int32, (SPAN, ROWS), 1)
    mine = rows
    for h in range(1, HEADS):
        mine = jnp.where(rows >= h * SPAN, rows - h * SPAN, mine)
    visible = keys <= mine
    k = km_ref[0, 0:SPAN, :]
    v = jnp.transpose(km_ref[0, SPAN : 2 * SPAN, :].astype(F32)).astype(BF16)
    for half in range(2):
        part = slice(half * HD, (half + 1) * HD)
        s = dot(k[:, part], qm_ref[part, :]) * SCALE
        s = jnp.where(visible, s, -1e30)
        shift = jnp.maximum(jnp.max(s, axis=0, keepdims=True), 0.0)
        p = jnp.where(visible, jnp.exp2(s - shift), 0.0)
        out_ref[part, :] = dot(v[part, :], p.astype(BF16))
        total = jnp.sum(p, axis=0, keepdims=True)
        out_ref[128 + 8 * half : 136 + 8 * half, :] = jnp.broadcast_to(total, (8, ROWS))
        out_ref[144 + 8 * half : 152 + 8 * half, :] = jnp.broadcast_to(shift, (8, ROWS))


def chunk_masks(keys, q_ref):
    info = keys[:, 2 * SPAN : 2 * SPAN + 16, :].astype(F32)[:, 0:1, :]
    own = q_ref[128:144, 0:128].astype(F32)[0:1, :]
    below = jnp.where(info < own[None], 1.0, 0.0)
    above = jnp.where(info > own[None], 1.0, 0.0)
    return below, above


def along_lanes(mask):
    lanes = lax.broadcasted_iota(jnp.int32, (16, CHUNK), 1)
    wide = [
        jnp.concatenate([jnp.broadcast_to(mask[b], (16, 128))] * (CHUNK // 128), axis=1)
        for b in range(GROUP)
    ]
    out = wide[0]
    for b in range(1, GROUP):
        out = jnp.where(lanes >= b * SPAN, wide[b], out)
    return out


def transposed_values(keys):
    return jnp.transpose(keys[:, SPAN : 2 * SPAN, :].reshape(CHUNK, 128))


def chunk_operands(keys, q_ref, vt):
    below, above = chunk_masks(keys, q_ref)
    k = keys[:, 0:SPAN, :]
    lanes = lax.broadcasted_iota(jnp.int32, (GROUP, 1, 128), 2)
    keep = jnp.where(lanes < HD, below, above).astype(BF16)
    chosen = (k * keep).reshape(CHUNK, 128)
    low, high = along_lanes(below), along_lanes(above)
    rows = lax.broadcasted_iota(jnp.int32, (16, CHUNK), 0)
    ones = jnp.where(rows < 8, low, high).astype(BF16)
    low, high = low[0:1].astype(BF16), high[0:1].astype(BF16)
    values = jnp.concatenate([vt[:HD] * low, vt[HD:] * high, ones], axis=0)
    return k.reshape(CHUNK, 128), chosen, values


def each(count, body):
    if count == 1:
        body(0)
    else:
        pl.loop(0, count)(body)


def attend(nq, nc, at, packed, *refs):
    q_refs, refs = refs[:nq], refs[nq:]
    key_refs, refs = refs[: 2 * nc], refs[2 * nc :]
    if at is not None:
        old_ref, refs = refs[0], refs[1:]
    out_ref, refs = refs[0], refs[1:]
    sums = refs[0] if packed else out_ref
    queries, keys = refs[-2], refs[-1]
    for q in range(nq):
        queries[q] = q_refs[q][...]
        sums[q] = jnp.zeros((PART, ROWS), F32) if at is None else old_ref[at + q]
    for c in range(nc):
        keys[c, 0 : GROUP // 2] = key_refs[2 * c][...]
        keys[c, GROUP // 2 :] = key_refs[2 * c + 1][...]

    def add(c):
        chunk = keys[c]
        vt = transposed_values(chunk)
        first = jnp.concatenate([vt[:HD], jnp.ones((16, CHUNK), BF16)], axis=0)

        def one(q):
            q_ref = queries.at[q]
            k, chosen, values = chunk_operands(chunk, q_ref, vt)
            a = dot(k[:, :HD], q_ref[HD:128, :])
            b = dot(chosen, q_ref[0:128, :])
            pa = jnp.exp2(a * SCALE).astype(BF16)
            pb = jnp.exp2(b * SCALE).astype(BF16)
            oa = dot(first, pa)
            ob = dot(values, pb)
            sums[q, 0:HD, :] += ob[:HD]
            sums[q, HD:128, :] += oa[:HD] + ob[HD:128]
            sums[q, 128:136, :] += ob[128:136]
            sums[q, 136:144, :] += oa[HD : HD + 8] + ob[136:144]

        each(nq, one)

    each(nc, add)

    def check(q):
        bad = jnp.sum(jnp.where(sums[q, 128:144, :] < LIMIT, 0.0, 1.0))
        bad = bad + jnp.sum(sums[q, 144:160, :])

        @pl.when(bad > 0.0)
        def _():
            for k in range(nq):

                @pl.when(q == k)
                def _():
                    sums[k] = jnp.zeros((PART, ROWS), F32) if at is None else old_ref[at + k]

            @pl.loop(0, nc)
            def _(c):
                careful(keys.at[c], queries.at[q], sums.at[q])

    each(nq, check)

    if packed:
        for q in range(nq):
            out_ref[0:128, :] = sums[q, 0:128, :].astype(BF16)
            rows = lax.broadcasted_iota(jnp.int32, (16, ROWS), 0)
            stats = jnp.zeros((16, ROWS), F32)
            for row, start in ((0, 128), (2, 136)):
                total = jnp.broadcast_to(sums[q, start : start + 1, :], (16, ROWS))
                high = total.astype(BF16).astype(F32)
                stats = jnp.where(rows == row, high, stats)
                stats = jnp.where(rows == row + 1, total - high, stats)
            for row, start in ((4, 144), (5, 152)):
                shift = jnp.broadcast_to(sums[q, start : start + 1, :], (16, ROWS))
                stats = jnp.where(rows == row, shift, stats)
            out_ref[128:144, :] = stats.astype(BF16)


def careful(keys, q_ref, out_ref):
    def raise_shift(half, top):
        old = out_ref[144 + 8 * half : 145 + 8 * half, :]
        new = jnp.maximum(old, jnp.maximum(top, 0.0).astype(BF16).astype(F32))
        factor = jnp.exp2(old - new)
        out_ref[half * HD : (half + 1) * HD, :] *= factor
        out_ref[128 + 8 * half : 136 + 8 * half, :] *= factor
        out_ref[144 + 8 * half : 152 + 8 * half, :] = jnp.broadcast_to(new, (8, ROWS))
        return new

    def add(half, values, p):
        p = p.astype(BF16)
        out_ref[half * HD : (half + 1) * HD, :] += dot(values, p)
        out_ref[128 + 8 * half : 136 + 8 * half, :] += dot(jnp.ones((16, SPAN), BF16), p)[:8]

    def wide(row):
        return jnp.concatenate([row] * (ROWS // 128), axis=1)

    own = wide(q_ref[128:144, 0:128].astype(F32)[0:1, :])

    @pl.loop(0, GROUP)
    def _(b):
        k = keys[b, 0:SPAN, :]
        vt = jnp.transpose(keys[b, SPAN : 2 * SPAN, :].astype(F32)).astype(BF16)
        info = wide(keys[b, 2 * SPAN : 2 * SPAN + 16, :].astype(F32)[0:1, :])
        low = dot(k[:, :HD], q_ref[HD:128, :]) * SCALE
        shift = raise_shift(1, jnp.max(low, axis=0, keepdims=True))
        add(1, vt[:HD], jnp.exp2(low - shift))
        for half, seen in ((0, info < own), (1, info > own)):
            part = slice(half * HD, (half + 1) * HD)
            s = dot(k[:, part], q_ref[part, :]) * SCALE
            top = jnp.where(seen, jnp.max(s, axis=0, keepdims=True), -1e30)
            shift = raise_shift(half, top)
            add(half, vt[part], jnp.where(seen, jnp.exp2(s - shift), 0.0))


def finish(held, sent, flag_ref, sink_ref, *refs):
    parts, out_ref = refs[: held + sent], refs[held + sent]
    swapped = jnp.broadcast_to(flag_ref[0:1, :], (SPAN, 128)) > 0.5
    results = []
    for half in range(2):
        part = slice(half * HD, (half + 1) * HD)
        terms = [
            (p[144 + 8 * half : 145 + 8 * half, :], p[128 + 8 * half : 129 + 8 * half, :], p[part, :])
            for p in parts[:held]
        ]
        for p in parts[held:]:
            stats = p[128:144, :].astype(F32)
            total = stats[2 * half : 2 * half + 1] + stats[2 * half + 1 : 2 * half + 2]
            terms.append((stats[4 + half : 5 + half], total, p[part, :].astype(F32)))
        top = functools.reduce(jnp.maximum, [shift for shift, _, _ in terms])
        total = jnp.exp2(sink_ref[0:1, :] * LOG2E - top)
        sums = jnp.zeros((HD, ROWS), F32)
        for shift, some, weighted in terms:
            factor = jnp.exp2(shift - top)
            total = total + some * factor
            sums = sums + weighted * factor
        results.append(sums / total)
    both = jnp.transpose(jnp.concatenate(results, axis=0))
    for g in range(HEADS // 2):
        even, odd = both[2 * g * SPAN : (2 * g + 1) * SPAN], both[(2 * g + 1) * SPAN : (2 * g + 2) * SPAN]
        lo = jnp.concatenate([even[:, :HD], odd[:, :HD]], axis=1)
        up = jnp.concatenate([even[:, HD:], odd[:, HD:]], axis=1)
        lanes = slice(128 * g, 128 * (g + 1))
        out_ref[0:SPAN, lanes] = jnp.where(swapped, up, lo).astype(BF16)
        out_ref[SPAN : 2 * SPAN, lanes] = jnp.where(swapped, lo, up).astype(BF16)


def partials(queries, chunks, old=None, at=None, packed=False):
    nq, nc = len(queries), len(chunks)
    pairs = nq * nc * 2 * CHUNK * ROWS
    keys = [part for chunk in chunks for part in chunk]
    operands = [*queries, *keys, *([] if at is None else [old])]
    sums = (nq, PART, ROWS)
    shape = jax.ShapeDtypeStruct(sums, F32)
    if packed:
        shape = jax.ShapeDtypeStruct((QMSG, ROWS), BF16)
    return pl.pallas_call(
        functools.partial(attend, nq, nc, at, packed),
        out_shape=shape,
        in_specs=[VMEM] * len(operands),
        out_specs=VMEM,
        scratch_shapes=([pltpu.VMEM(sums, F32)] if packed else [])
        + [pltpu.VMEM((nq, QMSG, ROWS), BF16), pltpu.VMEM((nc, GROUP, MSG, 128), BF16)],
        compiler_params=PARAMS,
        cost_estimate=pl.CostEstimate(
            flops=pairs * 16, bytes_accessed=nc * 2**14, transcendentals=0
        ),
        name="attend",
    )(*operands)


def simple(kernel, shape, name, *operands):
    return pl.pallas_call(
        kernel,
        out_shape=shape,
        in_specs=[VMEM] * len(operands),
        out_specs=VMEM,
        compiler_params=PARAMS,
        name=name,
    )(*operands)


def place(index):
    inner, outer = divmod(index, 16)
    return inner % 4, inner // 4 * 2 + outer // 2 % 2, outer // 4, outer % 2


def index_of(x, y, z, core):
    return (y // 2 * 4 + x) * 16 + z * 4 + y % 2 * 2 + core


def permute(array, target):
    pairs = []
    for source in range(128):
        x, y, z, core = place(source)
        x, y, z, core = target(x, y, z, core)
        pairs.append((source, index_of(x % 4, y % 4, z % 4, core % 2)))
    return lax.ppermute(array, ("inner", "outer"), pairs)


def along_first(array, d):
    return permute(array, lambda x, y, z, c: (x, y, z + d, c) if c else (x + d, y, z, c))


def along_second(array, d):
    return permute(array, lambda x, y, z, c: (x + d, y, z, c) if c else (x, y, z + d, c))


def along_y(array, d):
    return permute(array, lambda x, y, z, c: (x, y + d, z, c))


def other_core(array):
    return permute(array, lambda x, y, z, c: (x, y, z, c + 1))


def after(array, *others):
    return lax.optimization_barrier((array, *others))[0]


def shards(queries, key_value, positions, sinks):
    qm, km, flag = pl.pallas_call(
        prepare,
        out_shape=(
            jax.ShapeDtypeStruct((QMSG, ROWS), BF16),
            jax.ShapeDtypeStruct((1, MSG, 128), BF16),
            jax.ShapeDtypeStruct((8, 128), F32),
        ),
        in_specs=[HBM] * 3,
        out_specs=(VMEM,) * 3,
        scratch_shapes=[
            pltpu.SMEM(positions.shape, jnp.int32),
            pltpu.VMEM(queries.shape, BF16),
            pltpu.VMEM(key_value.shape, BF16),
            pltpu.SemaphoreType.DMA((3,)),
        ],
        compiler_params=pltpu.CompilerParams(vmem_limit_bytes=63 << 20),
        name="prepare",
    )(positions, queries, key_value)
    right = along_first(km, 1)
    row = jnp.concatenate([km, right, along_first(km, -1), along_first(km, 2)], axis=0)
    asked = after(qm, right)
    up, down, over = along_y(asked, 1), along_y(asked, -1), along_y(asked, 2)
    groups = [row, along_second(row, 1), along_second(row, -1), along_second(row, 2)]
    chunks = [(group, other_core(group)) for group in groups]
    own = partials([qm], chunks[:1])
    two = partials([after(up, own), down], chunks[:1])
    two = partials([after(up, two), down], chunks[1:2], two, 0)
    sent = [partials([after(over, two)], chunks, packed=True)]
    back = [along_y(sent[0], -2)]
    for at, query, d in ((0, up, -1), (1, down, 1)):
        sent.append(partials([after(query, sent[-1])], chunks[2:], two, at, packed=True))
        back.append(along_y(sent[-1], d))
    own = partials([after(qm, sent[-1])], chunks[1:2], own, 0)
    own = partials([after(qm, own, back[0])], chunks[2:], own, 0)
    diag = pl.pallas_call(
        diagonal,
        out_shape=jax.ShapeDtypeStruct((PART, ROWS), F32),
        in_specs=[VMEM, VMEM],
        out_specs=VMEM,
        compiler_params=PARAMS,
        name="diagonal",
    )(after(qm, own, back[1]), km)
    sink_row = jnp.broadcast_to(jnp.repeat(sinks, SPAN)[None], (8, ROWS))
    return simple(
        functools.partial(finish, 2, 3),
        jax.ShapeDtypeStruct(queries.shape, BF16),
        "finish",
        flag,
        sink_row,
        diag,
        own.reshape(PART, ROWS),
        *back,
    )


def solution(mesh):
    return jax.shard_map(
        shards,
        mesh=mesh,
        in_specs=(
            P(("inner", "outer"), None),
            P(("inner", "outer"), None),
            P(("inner", "outer")),
            P(),
        ),
        out_specs=P(("inner", "outer"), None),
        check_vma=False,
    )
```

```python
import functools

import jax
import jax.numpy as jnp
from jax import lax
from jax.experimental import pallas as pl
from jax.experimental.pallas import tpu as pltpu
from jax.sharding import PartitionSpec as P

HEADS = 8
HD = 64
SPAN = 96
ROWS = HEADS * SPAN
GROUP = 8
CHUNK = GROUP * SPAN
MSG = 208
QMSG = 144
PART = 160
LOG2E = 1.4426950408889634
SCALE = HD**-0.5 * LOG2E
LIMIT = 1e36
F32 = jnp.float32
BF16 = jnp.bfloat16
VMEM = pl.BlockSpec(memory_space=pltpu.VMEM)
HBM = pl.BlockSpec(memory_space=pltpu.HBM)
PARAMS = pltpu.CompilerParams(vmem_limit_bytes=32 << 20)


def dot(a, b):
    return jnp.dot(a, b, preferred_element_type=F32)


def load(pairs, sems):
    copies = [
        pltpu.make_async_copy(source, target, sems.at[n]) for n, (source, target) in enumerate(pairs)
    ]
    for copy in copies:
        copy.start()
    for copy in copies:
        copy.wait()


def order(pos_ref, ref):
    run = pos_ref[0] // SPAN
    swapped = run >= 128
    first, second = ref[0:SPAN, :], ref[SPAN : 2 * SPAN, :]
    lower = jnp.where(swapped, 255 - run, run).astype(F32)
    return swapped, lower, jnp.where(swapped, second, first), jnp.where(swapped, first, second)


def prepare_keys(pos_hbm, kv_hbm, km_ref, pos_ref, kv_ref, sems):
    load(((pos_hbm, pos_ref), (kv_hbm, kv_ref)), sems)
    _, lower, lo, up = order(pos_ref, kv_ref)
    km_ref[0, 0:SPAN, :] = jnp.concatenate([lo[:, :HD], up[:, :HD]], axis=1)
    km_ref[0, SPAN : 2 * SPAN, :] = jnp.concatenate([lo[:, HD:], up[:, HD:]], axis=1)
    km_ref[0, 2 * SPAN :, :] = jnp.full((MSG - 2 * SPAN, 128), lower, F32).astype(BF16)


def prepare_queries(pos_hbm, q_hbm, qm_ref, flag_ref, pos_ref, q_ref, sems):
    load(((pos_hbm, pos_ref), (q_hbm, q_ref)), sems)
    swapped, lower, lo, up = order(pos_ref, q_ref)
    stacked = jnp.concatenate(
        [
            jnp.concatenate([lo[:, h * HD : (h + 1) * HD], up[:, h * HD : (h + 1) * HD]], axis=1)
            for h in range(HEADS)
        ],
        axis=0,
    )
    qm_ref[0:128, :] = jnp.transpose(stacked)
    qm_ref[128:, :] = jnp.full((QMSG - 128, ROWS), lower, F32).astype(BF16)
    flag_ref[...] = jnp.full((8, ROWS), jnp.where(swapped, 1.0, 0.0), F32)


def diagonal(qm_ref, km_ref, flag_ref, out_ref):
    out_ref[PART:, :] = flag_ref[...]
    keys = lax.broadcasted_iota(jnp.int32, (SPAN, ROWS), 0)
    rows = lax.broadcasted_iota(jnp.int32, (SPAN, ROWS), 1)
    mine = rows
    for h in range(1, HEADS):
        mine = jnp.where(rows >= h * SPAN, rows - h * SPAN, mine)
    visible = keys <= mine
    k = km_ref[0, 0:SPAN, :]
    v = jnp.transpose(km_ref[0, SPAN : 2 * SPAN, :].astype(F32)).astype(BF16)
    for half in range(2):
        part = slice(half * HD, (half + 1) * HD)
        s = dot(k[:, part], qm_ref[part, :]) * SCALE
        s = jnp.where(visible, s, -1e30)
        shift = jnp.maximum(jnp.max(s, axis=0, keepdims=True), 0.0)
        p = jnp.where(visible, jnp.exp2(s - shift), 0.0)
        out_ref[part, :] = dot(v[part, :], p.astype(BF16))
        total = jnp.sum(p, axis=0, keepdims=True)
        out_ref[128 + 8 * half : 136 + 8 * half, :] = jnp.broadcast_to(total, (8, ROWS))
        out_ref[144 + 8 * half : 152 + 8 * half, :] = jnp.broadcast_to(shift, (8, ROWS))


def chunk_masks(keys, q_ref):
    info = keys[:, 2 * SPAN : 2 * SPAN + 16, :].astype(F32)[:, 0:1, :]
    own = q_ref[128:144, 0:128].astype(F32)[0:1, :]
    below = jnp.where(info < own[None], 1.0, 0.0)
    above = jnp.where(info > own[None], 1.0, 0.0)
    return below, above


def along_lanes(mask):
    lanes = lax.broadcasted_iota(jnp.int32, (16, CHUNK), 1)
    wide = [
        jnp.concatenate([jnp.broadcast_to(mask[b], (16, 128))] * (CHUNK // 128), axis=1)
        for b in range(GROUP)
    ]
    out = wide[0]
    for b in range(1, GROUP):
        out = jnp.where(lanes >= b * SPAN, wide[b], out)
    return out


def transposed_values(keys):
    return jnp.transpose(keys[:, SPAN : 2 * SPAN, :].reshape(CHUNK, 128))


def chunk_operands(keys, q_ref, vt):
    below, above = chunk_masks(keys, q_ref)
    k = keys[:, 0:SPAN, :]
    lanes = lax.broadcasted_iota(jnp.int32, (GROUP, 1, 128), 2)
    keep = jnp.where(lanes < HD, below, above).astype(BF16)
    chosen = (k * keep).reshape(CHUNK, 128)
    low, high = along_lanes(below), along_lanes(above)
    rows = lax.broadcasted_iota(jnp.int32, (16, CHUNK), 0)
    ones = jnp.where(rows < 8, low, high).astype(BF16)
    low, high = low[0:1].astype(BF16), high[0:1].astype(BF16)
    values = jnp.concatenate([vt[:HD] * low, vt[HD:] * high, ones], axis=0)
    return k.reshape(CHUNK, 128), chosen, values


def each(count, body):
    if count == 1:
        body(0)
    else:
        pl.loop(0, count)(body)


def attend(nq, nc, at, packed, *refs):
    q_refs, refs = refs[:nq], refs[nq:]
    key_refs, refs = refs[: 2 * nc], refs[2 * nc :]
    if at is not None:
        old_ref, refs = refs[0], refs[1:]
    out_ref, refs = refs[0], refs[1:]
    sums = refs[0] if packed else out_ref
    queries, keys = refs[-2], refs[-1]
    for q in range(nq):
        queries[q] = q_refs[q][...]
        sums[q] = jnp.zeros((PART, ROWS), F32) if at is None else old_ref[at + q]
    for c in range(nc):
        keys[c, 0 : GROUP // 2] = key_refs[2 * c][...]
        keys[c, GROUP // 2 :] = key_refs[2 * c + 1][...]

    def add(c):
        chunk = keys[c]
        vt = transposed_values(chunk)
        first = jnp.concatenate([vt[:HD], jnp.ones((16, CHUNK), BF16)], axis=0)

        def one(q):
            q_ref = queries.at[q]
            k, chosen, values = chunk_operands(chunk, q_ref, vt)
            a = dot(k[:, :HD], q_ref[HD:128, :])
            b = dot(chosen, q_ref[0:128, :])
            pa = jnp.exp2(a * SCALE).astype(BF16)
            pb = jnp.exp2(b * SCALE).astype(BF16)
            oa = dot(first, pa)
            ob = dot(values, pb)
            sums[q, 0:HD, :] += ob[:HD]
            sums[q, HD:128, :] += oa[:HD] + ob[HD:128]
            sums[q, 128:136, :] += ob[128:136]
            sums[q, 136:144, :] += oa[HD : HD + 8] + ob[136:144]

        each(nq, one)

    each(nc, add)

    def check(q):
        bad = jnp.sum(jnp.where(sums[q, 128:144, :] < LIMIT, 0.0, 1.0))
        bad = bad + jnp.sum(sums[q, 144:160, :])

        @pl.when(bad > 0.0)
        def _():
            for k in range(nq):

                @pl.when(q == k)
                def _():
                    sums[k] = jnp.zeros((PART, ROWS), F32) if at is None else old_ref[at + k]

            @pl.loop(0, nc)
            def _(c):
                careful(keys.at[c], queries.at[q], sums.at[q])

    each(nq, check)

    if packed:
        for q in range(nq):
            out_ref[0:128, :] = sums[q, 0:128, :].astype(BF16)
            rows = lax.broadcasted_iota(jnp.int32, (16, ROWS), 0)
            stats = jnp.zeros((16, ROWS), F32)
            for row, start in ((0, 128), (2, 136)):
                total = jnp.broadcast_to(sums[q, start : start + 1, :], (16, ROWS))
                high = total.astype(BF16).astype(F32)
                stats = jnp.where(rows == row, high, stats)
                stats = jnp.where(rows == row + 1, total - high, stats)
            for row, start in ((4, 144), (5, 152)):
                shift = jnp.broadcast_to(sums[q, start : start + 1, :], (16, ROWS))
                stats = jnp.where(rows == row, shift, stats)
            out_ref[128:144, :] = stats.astype(BF16)


def careful(keys, q_ref, out_ref):
    def raise_shift(half, top):
        old = out_ref[144 + 8 * half : 145 + 8 * half, :]
        new = jnp.maximum(old, jnp.maximum(top, 0.0).astype(BF16).astype(F32))
        factor = jnp.exp2(old - new)
        out_ref[half * HD : (half + 1) * HD, :] *= factor
        out_ref[128 + 8 * half : 136 + 8 * half, :] *= factor
        out_ref[144 + 8 * half : 152 + 8 * half, :] = jnp.broadcast_to(new, (8, ROWS))
        return new

    def add(half, values, p):
        p = p.astype(BF16)
        out_ref[half * HD : (half + 1) * HD, :] += dot(values, p)
        out_ref[128 + 8 * half : 136 + 8 * half, :] += dot(jnp.ones((16, SPAN), BF16), p)[:8]

    def wide(row):
        return jnp.concatenate([row] * (ROWS // 128), axis=1)

    own = wide(q_ref[128:144, 0:128].astype(F32)[0:1, :])

    @pl.loop(0, GROUP)
    def _(b):
        k = keys[b, 0:SPAN, :]
        vt = jnp.transpose(keys[b, SPAN : 2 * SPAN, :].astype(F32)).astype(BF16)
        info = wide(keys[b, 2 * SPAN : 2 * SPAN + 16, :].astype(F32)[0:1, :])
        low = dot(k[:, :HD], q_ref[HD:128, :]) * SCALE
        shift = raise_shift(1, jnp.max(low, axis=0, keepdims=True))
        add(1, vt[:HD], jnp.exp2(low - shift))
        for half, seen in ((0, info < own), (1, info > own)):
            part = slice(half * HD, (half + 1) * HD)
            s = dot(k[:, part], q_ref[part, :]) * SCALE
            top = jnp.where(seen, jnp.max(s, axis=0, keepdims=True), -1e30)
            shift = raise_shift(half, top)
            add(half, vt[part], jnp.where(seen, jnp.exp2(s - shift), 0.0))


def finish(held, sent, sink_ref, *refs):
    parts, out_ref = refs[: held + sent], refs[held + sent]
    swapped = jnp.broadcast_to(refs[0][PART : PART + 1, 0:128], (SPAN, 128)) > 0.5
    results = []
    for half in range(2):
        part = slice(half * HD, (half + 1) * HD)
        terms = [
            (p[144 + 8 * half : 145 + 8 * half, :], p[128 + 8 * half : 129 + 8 * half, :], p[part, :])
            for p in parts[:held]
        ]
        for p in parts[held:]:
            stats = p[128:144, :].astype(F32)
            total = stats[2 * half : 2 * half + 1] + stats[2 * half + 1 : 2 * half + 2]
            terms.append((stats[4 + half : 5 + half], total, p[part, :].astype(F32)))
        top = functools.reduce(jnp.maximum, [shift for shift, _, _ in terms])
        total = jnp.exp2(sink_ref[0:1, :] * LOG2E - top)
        sums = jnp.zeros((HD, ROWS), F32)
        for shift, some, weighted in terms:
            factor = jnp.exp2(shift - top)
            total = total + some * factor
            sums = sums + weighted * factor
        results.append(sums / total)
    both = jnp.transpose(jnp.concatenate(results, axis=0))
    for g in range(HEADS // 2):
        even, odd = both[2 * g * SPAN : (2 * g + 1) * SPAN], both[(2 * g + 1) * SPAN : (2 * g + 2) * SPAN]
        lo = jnp.concatenate([even[:, :HD], odd[:, :HD]], axis=1)
        up = jnp.concatenate([even[:, HD:], odd[:, HD:]], axis=1)
        lanes = slice(128 * g, 128 * (g + 1))
        out_ref[0:SPAN, lanes] = jnp.where(swapped, up, lo).astype(BF16)
        out_ref[SPAN : 2 * SPAN, lanes] = jnp.where(swapped, lo, up).astype(BF16)


def partials(queries, chunks, old=None, at=None, packed=False):
    nq, nc = len(queries), len(chunks)
    pairs = nq * nc * 2 * CHUNK * ROWS
    keys = [part for chunk in chunks for part in chunk]
    operands = [*queries, *keys, *([] if at is None else [old])]
    sums = (nq, PART, ROWS)
    shape = jax.ShapeDtypeStruct(sums, F32)
    if packed:
        shape = jax.ShapeDtypeStruct((QMSG, ROWS), BF16)
    return pl.pallas_call(
        functools.partial(attend, nq, nc, at, packed),
        out_shape=shape,
        in_specs=[VMEM] * len(operands),
        out_specs=VMEM,
        scratch_shapes=([pltpu.VMEM(sums, F32)] if packed else [])
        + [pltpu.VMEM((nq, QMSG, ROWS), BF16), pltpu.VMEM((nc, GROUP, MSG, 128), BF16)],
        compiler_params=PARAMS,
        cost_estimate=pl.CostEstimate(
            flops=pairs * 16, bytes_accessed=nc * 2**14, transcendentals=0
        ),
        name="attend",
    )(*operands)


def simple(kernel, shape, name, *operands):
    return pl.pallas_call(
        kernel,
        out_shape=shape,
        in_specs=[VMEM] * len(operands),
        out_specs=VMEM,
        compiler_params=PARAMS,
        name=name,
    )(*operands)


def place(index):
    inner, outer = divmod(index, 16)
    return inner % 4, inner // 4 * 2 + outer // 2 % 2, outer // 4, outer % 2


def index_of(x, y, z, core):
    return (y // 2 * 4 + x) * 16 + z * 4 + y % 2 * 2 + core


def permute(array, target):
    pairs = []
    for source in range(128):
        x, y, z, core = place(source)
        x, y, z, core = target(x, y, z, core)
        pairs.append((source, index_of(x % 4, y % 4, z % 4, core % 2)))
    return lax.ppermute(array, ("inner", "outer"), pairs)


def along_first(array, d):
    return permute(array, lambda x, y, z, c: (x, y, z + d, c) if c else (x + d, y, z, c))


def along_second(array, d):
    return permute(array, lambda x, y, z, c: (x + d, y, z, c) if c else (x, y, z + d, c))


def along_y(array, d):
    return permute(array, lambda x, y, z, c: (x, y + d, z, c))


def other_core(array):
    return permute(array, lambda x, y, z, c: (x, y, z, c + 1))


def after(array, *others):
    return lax.optimization_barrier((array, *others))[0]


def prepared(kernel, name, positions, rows, *shapes):
    return pl.pallas_call(
        kernel,
        out_shape=shapes,
        in_specs=[HBM, HBM],
        out_specs=(VMEM,) * len(shapes),
        scratch_shapes=[
            pltpu.SMEM(positions.shape, jnp.int32),
            pltpu.VMEM(rows.shape, BF16),
            pltpu.SemaphoreType.DMA((2,)),
        ],
        compiler_params=pltpu.CompilerParams(vmem_limit_bytes=63 << 20),
        name=name,
    )(positions, rows)


def shards(queries, key_value, positions, sinks):
    (km,) = prepared(
        prepare_keys,
        "prepare_keys",
        positions,
        key_value,
        jax.ShapeDtypeStruct((1, MSG, 128), BF16),
    )
    qm, flag = prepared(
        prepare_queries,
        "prepare_queries",
        positions,
        after(queries, km),
        jax.ShapeDtypeStruct((QMSG, ROWS), BF16),
        jax.ShapeDtypeStruct((8, ROWS), F32),
    )
    right = along_first(km, 1)
    row = jnp.concatenate([after(km, qm), right, along_first(km, -1), along_first(km, 2)], axis=0)
    asked = after(qm, right)
    up, down, over = along_y(asked, 1), along_y(asked, -1), along_y(asked, 2)
    chunks = [(row, other_core(row))]
    own = partials([qm], chunks)
    diag = simple(
        diagonal, jax.ShapeDtypeStruct((PART + 8, ROWS), F32), "diagonal", after(qm, own), km, flag
    )
    for d in (1, -1, 2):
        group = along_second(row, d)
        chunks.append((group, other_core(after(group, diag))))
    two = partials([after(up, own), down], chunks[:1])
    two = partials([after(up, two), down], chunks[1:2], two, 0)
    sent = [partials([after(over, two)], chunks, packed=True)]
    back = [along_y(sent[0], -2)]
    for at, query, d in ((0, up, -1), (1, down, 1)):
        sent.append(partials([after(query, sent[-1])], chunks[2:], two, at, packed=True))
        back.append(along_y(sent[-1], d))
    own = partials([after(qm, sent[-1])], chunks[1:2], own, 0)
    own = partials([after(qm, own, back[0])], chunks[2:3], own, 0)
    own = partials([after(qm, own, back[1])], chunks[3:], own, 0)
    sink_row = jnp.broadcast_to(jnp.repeat(sinks, SPAN)[None], (8, ROWS))
    return simple(
        functools.partial(finish, 2, 3),
        jax.ShapeDtypeStruct(queries.shape, BF16),
        "finish",
        sink_row,
        diag,
        own.reshape(PART, ROWS),
        *back,
    )


def solution(mesh):
    return jax.shard_map(
        shards,
        mesh=mesh,
        in_specs=(
            P(("inner", "outer"), None),
            P(("inner", "outer"), None),
            P(("inner", "outer")),
            P(),
        ),
        out_specs=P(("inner", "outer"), None),
        check_vma=False,
    )
```

```python
import functools

import jax
import jax.numpy as jnp
from jax import lax
from jax.experimental import pallas as pl
from jax.experimental.pallas import tpu as pltpu
from jax.sharding import PartitionSpec as P

HEADS = 8
HD = 64
SPAN = 96
ROWS = HEADS * SPAN
GROUP = 8
CHUNK = GROUP * SPAN
MSG = 208
QMSG = 144
PART = 160
LOG2E = 1.4426950408889634
SCALE = HD**-0.5 * LOG2E
LIMIT = 1e36
F32 = jnp.float32
BF16 = jnp.bfloat16
VMEM = pl.BlockSpec(memory_space=pltpu.VMEM)
HBM = pl.BlockSpec(memory_space=pltpu.HBM)
PARAMS = pltpu.CompilerParams(vmem_limit_bytes=20 << 20)


def dot(a, b):
    return jnp.dot(a, b, preferred_element_type=F32)


def load(pairs, sems):
    copies = [
        pltpu.make_async_copy(source, target, sems.at[n]) for n, (source, target) in enumerate(pairs)
    ]
    for copy in copies:
        copy.start()
    for copy in copies:
        copy.wait()


def order(pos_ref, ref):
    run = pos_ref[0] // SPAN
    swapped = run >= 128
    first, second = ref[0:SPAN, :], ref[SPAN : 2 * SPAN, :]
    lower = jnp.where(swapped, 255 - run, run).astype(F32)
    return swapped, lower, jnp.where(swapped, second, first), jnp.where(swapped, first, second)


def prepare_keys(pos_hbm, kv_hbm, km_ref, pos_ref, kv_ref, sems):
    load(((pos_hbm, pos_ref), (kv_hbm, kv_ref)), sems)
    _, lower, lo, up = order(pos_ref, kv_ref)
    km_ref[0, 0:SPAN, :] = jnp.concatenate([lo[:, :HD], up[:, :HD]], axis=1)
    km_ref[0, SPAN : 2 * SPAN, :] = jnp.concatenate([lo[:, HD:], up[:, HD:]], axis=1)
    km_ref[0, 2 * SPAN :, :] = jnp.full((MSG - 2 * SPAN, 128), lower, F32).astype(BF16)


def prepare_queries(pos_hbm, q_hbm, qm_ref, flag_ref, pos_ref, q_ref, sems):
    load(((pos_hbm, pos_ref), (q_hbm, q_ref)), sems)
    swapped, lower, lo, up = order(pos_ref, q_ref)
    stacked = jnp.concatenate(
        [
            jnp.concatenate([lo[:, h * HD : (h + 1) * HD], up[:, h * HD : (h + 1) * HD]], axis=1)
            for h in range(HEADS)
        ],
        axis=0,
    )
    qm_ref[0:128, :] = jnp.transpose(stacked)
    qm_ref[128:, :] = jnp.full((QMSG - 128, ROWS), lower, F32).astype(BF16)
    flag_ref[...] = jnp.full((8, ROWS), jnp.where(swapped, 1.0, 0.0), F32)


def diagonal(qm_ref, km_ref, flag_ref, out_ref):
    out_ref[PART:, :] = flag_ref[...]
    keys = lax.broadcasted_iota(jnp.int32, (SPAN, ROWS), 0)
    rows = lax.broadcasted_iota(jnp.int32, (SPAN, ROWS), 1)
    mine = rows
    for h in range(1, HEADS):
        mine = jnp.where(rows >= h * SPAN, rows - h * SPAN, mine)
    visible = keys <= mine
    k = km_ref[0, 0:SPAN, :]
    v = jnp.transpose(km_ref[0, SPAN : 2 * SPAN, :].astype(F32)).astype(BF16)
    for half in range(2):
        part = slice(half * HD, (half + 1) * HD)
        s = dot(k[:, part], qm_ref[part, :]) * SCALE
        s = jnp.where(visible, s, -1e30)
        shift = jnp.maximum(jnp.max(s, axis=0, keepdims=True), 0.0)
        p = jnp.where(visible, jnp.exp2(s - shift), 0.0)
        out_ref[part, :] = dot(v[part, :], p.astype(BF16))
        total = jnp.sum(p, axis=0, keepdims=True)
        out_ref[128 + 8 * half : 136 + 8 * half, :] = jnp.broadcast_to(total, (8, ROWS))
        out_ref[144 + 8 * half : 152 + 8 * half, :] = jnp.broadcast_to(shift, (8, ROWS))


def chunk_masks(keys, q_ref):
    info = keys[:, 2 * SPAN : 2 * SPAN + 16, :].astype(F32)[:, 0:1, :]
    own = q_ref[128:144, 0:128].astype(F32)[0:1, :]
    below = jnp.where(info < own[None], 1.0, 0.0)
    above = jnp.where(info > own[None], 1.0, 0.0)
    return below, above


def along_lanes(mask):
    lanes = lax.broadcasted_iota(jnp.int32, (16, CHUNK), 1)
    wide = [
        jnp.concatenate([jnp.broadcast_to(mask[b], (16, 128))] * (CHUNK // 128), axis=1)
        for b in range(GROUP)
    ]
    out = wide[0]
    for b in range(1, GROUP):
        out = jnp.where(lanes >= b * SPAN, wide[b], out)
    return out


def transposed_values(keys):
    return jnp.transpose(keys[:, SPAN : 2 * SPAN, :].reshape(CHUNK, 128))


def chunk_operands(keys, q_ref, vt):
    below, above = chunk_masks(keys, q_ref)
    k = keys[:, 0:SPAN, :]
    lanes = lax.broadcasted_iota(jnp.int32, (GROUP, 1, 128), 2)
    keep = jnp.where(lanes < HD, below, above).astype(BF16)
    chosen = (k * keep).reshape(CHUNK, 128)
    low, high = along_lanes(below), along_lanes(above)
    rows = lax.broadcasted_iota(jnp.int32, (16, CHUNK), 0)
    ones = jnp.where(rows < 8, low, high).astype(BF16)
    low, high = low[0:1].astype(BF16), high[0:1].astype(BF16)
    values = jnp.concatenate([vt[:HD] * low, vt[HD:] * high, ones], axis=0)
    return k.reshape(CHUNK, 128), chosen, values


def each(count, body):
    if count == 1:
        body(0)
    else:
        pl.loop(0, count)(body)


def attend(nq, nc, at, packed, *refs):
    q_refs, refs = refs[:nq], refs[nq:]
    key_refs, refs = refs[: 2 * nc], refs[2 * nc :]
    if at is not None:
        old_ref, refs = refs[0], refs[1:]
    out_ref, refs = refs[0], refs[1:]
    sums = refs[0] if packed else out_ref
    queries, keys = refs[-2], refs[-1]
    for q in range(nq):
        queries[q] = q_refs[q][...]
        sums[q] = jnp.zeros((PART, ROWS), F32) if at is None else old_ref[at + q]
    for c in range(nc):
        keys[c, 0 : GROUP // 2] = key_refs[2 * c][...]
        keys[c, GROUP // 2 :] = key_refs[2 * c + 1][...]

    def add(c):
        chunk = keys[c]
        vt = transposed_values(chunk)
        first = jnp.concatenate([vt[:HD], jnp.ones((16, CHUNK), BF16)], axis=0)

        def one(q):
            q_ref = queries.at[q]
            k, chosen, values = chunk_operands(chunk, q_ref, vt)
            a = dot(k[:, :HD], q_ref[HD:128, :])
            b = dot(chosen, q_ref[0:128, :])
            pa = jnp.exp2(a * SCALE).astype(BF16)
            pb = jnp.exp2(b * SCALE).astype(BF16)
            oa = dot(first, pa)
            ob = dot(values, pb)
            sums[q, 0:HD, :] += ob[:HD]
            sums[q, HD:128, :] += oa[:HD] + ob[HD:128]
            sums[q, 128:136, :] += ob[128:136]
            sums[q, 136:144, :] += oa[HD : HD + 8] + ob[136:144]

        each(nq, one)

    each(nc, add)

    def check(q):
        bad = jnp.sum(jnp.where(sums[q, 128:144, :] < LIMIT, 0.0, 1.0))
        bad = bad + jnp.sum(sums[q, 144:160, :])

        @pl.when(bad > 0.0)
        def _():
            for k in range(nq):

                @pl.when(q == k)
                def _():
                    sums[k] = jnp.zeros((PART, ROWS), F32) if at is None else old_ref[at + k]

            @pl.loop(0, nc)
            def _(c):
                careful(keys.at[c], queries.at[q], sums.at[q])

    each(nq, check)

    if packed:
        for q in range(nq):
            out_ref[0:128, :] = sums[q, 0:128, :].astype(BF16)
            rows = lax.broadcasted_iota(jnp.int32, (16, ROWS), 0)
            stats = jnp.zeros((16, ROWS), F32)
            for row, start in ((0, 128), (2, 136)):
                total = jnp.broadcast_to(sums[q, start : start + 1, :], (16, ROWS))
                high = total.astype(BF16).astype(F32)
                stats = jnp.where(rows == row, high, stats)
                stats = jnp.where(rows == row + 1, total - high, stats)
            for row, start in ((4, 144), (5, 152)):
                shift = jnp.broadcast_to(sums[q, start : start + 1, :], (16, ROWS))
                stats = jnp.where(rows == row, shift, stats)
            out_ref[128:144, :] = stats.astype(BF16)


def careful(keys, q_ref, out_ref):
    def raise_shift(half, top):
        old = out_ref[144 + 8 * half : 145 + 8 * half, :]
        new = jnp.maximum(old, jnp.maximum(top, 0.0).astype(BF16).astype(F32))
        factor = jnp.exp2(old - new)
        out_ref[half * HD : (half + 1) * HD, :] *= factor
        out_ref[128 + 8 * half : 136 + 8 * half, :] *= factor
        out_ref[144 + 8 * half : 152 + 8 * half, :] = jnp.broadcast_to(new, (8, ROWS))
        return new

    def add(half, values, p):
        p = p.astype(BF16)
        out_ref[half * HD : (half + 1) * HD, :] += dot(values, p)
        out_ref[128 + 8 * half : 136 + 8 * half, :] += dot(jnp.ones((16, SPAN), BF16), p)[:8]

    def wide(row):
        return jnp.concatenate([row] * (ROWS // 128), axis=1)

    own = wide(q_ref[128:144, 0:128].astype(F32)[0:1, :])

    @pl.loop(0, GROUP)
    def _(b):
        k = keys[b, 0:SPAN, :]
        vt = jnp.transpose(keys[b, SPAN : 2 * SPAN, :].astype(F32)).astype(BF16)
        info = wide(keys[b, 2 * SPAN : 2 * SPAN + 16, :].astype(F32)[0:1, :])
        low = dot(k[:, :HD], q_ref[HD:128, :]) * SCALE
        shift = raise_shift(1, jnp.max(low, axis=0, keepdims=True))
        add(1, vt[:HD], jnp.exp2(low - shift))
        for half, seen in ((0, info < own), (1, info > own)):
            part = slice(half * HD, (half + 1) * HD)
            s = dot(k[:, part], q_ref[part, :]) * SCALE
            top = jnp.where(seen, jnp.max(s, axis=0, keepdims=True), -1e30)
            shift = raise_shift(half, top)
            add(half, vt[part], jnp.where(seen, jnp.exp2(s - shift), 0.0))


def finish(held, sent, sink_ref, *refs):
    parts, out_ref = refs[: held + sent], refs[held + sent]
    swapped = jnp.broadcast_to(refs[0][PART : PART + 1, 0:128], (SPAN, 128)) > 0.5
    results = []
    for half in range(2):
        part = slice(half * HD, (half + 1) * HD)
        terms = [
            (p[144 + 8 * half : 145 + 8 * half, :], p[128 + 8 * half : 129 + 8 * half, :], p[part, :])
            for p in parts[:held]
        ]
        for p in parts[held:]:
            stats = p[128:144, :].astype(F32)
            total = stats[2 * half : 2 * half + 1] + stats[2 * half + 1 : 2 * half + 2]
            terms.append((stats[4 + half : 5 + half], total, p[part, :].astype(F32)))
        top = functools.reduce(jnp.maximum, [shift for shift, _, _ in terms])
        total = jnp.exp2(sink_ref[0:1, :] * LOG2E - top)
        sums = jnp.zeros((HD, ROWS), F32)
        for shift, some, weighted in terms:
            factor = jnp.exp2(shift - top)
            total = total + some * factor
            sums = sums + weighted * factor
        results.append(sums / total)
    both = jnp.transpose(jnp.concatenate(results, axis=0))
    for g in range(HEADS // 2):
        even, odd = both[2 * g * SPAN : (2 * g + 1) * SPAN], both[(2 * g + 1) * SPAN : (2 * g + 2) * SPAN]
        lo = jnp.concatenate([even[:, :HD], odd[:, :HD]], axis=1)
        up = jnp.concatenate([even[:, HD:], odd[:, HD:]], axis=1)
        lanes = slice(128 * g, 128 * (g + 1))
        out_ref[0:SPAN, lanes] = jnp.where(swapped, up, lo).astype(BF16)
        out_ref[SPAN : 2 * SPAN, lanes] = jnp.where(swapped, lo, up).astype(BF16)


def partials(queries, chunks, old=None, at=None, packed=False):
    nq, nc = len(queries), len(chunks)
    pairs = nq * nc * 2 * CHUNK * ROWS
    keys = [part for chunk in chunks for part in chunk]
    operands = [*queries, *keys, *([] if at is None else [old])]
    sums = (nq, PART, ROWS)
    shape = jax.ShapeDtypeStruct(sums, F32)
    if packed:
        shape = jax.ShapeDtypeStruct((QMSG, ROWS), BF16)
    return pl.pallas_call(
        functools.partial(attend, nq, nc, at, packed),
        out_shape=shape,
        in_specs=[VMEM] * len(operands),
        out_specs=VMEM,
        scratch_shapes=([pltpu.VMEM(sums, F32)] if packed else [])
        + [pltpu.VMEM((nq, QMSG, ROWS), BF16), pltpu.VMEM((nc, GROUP, MSG, 128), BF16)],
        compiler_params=PARAMS,
        cost_estimate=pl.CostEstimate(
            flops=pairs * 16, bytes_accessed=nc * 2**14, transcendentals=0
        ),
        name="attend",
    )(*operands)


def simple(kernel, shape, name, *operands):
    return pl.pallas_call(
        kernel,
        out_shape=shape,
        in_specs=[VMEM] * len(operands),
        out_specs=VMEM,
        compiler_params=PARAMS,
        name=name,
    )(*operands)


def place(index):
    inner, outer = divmod(index, 16)
    return inner % 4, inner // 4 * 2 + outer // 2 % 2, outer // 4, outer % 2


def index_of(x, y, z, core):
    return (y // 2 * 4 + x) * 16 + z * 4 + y % 2 * 2 + core


def permute(array, target):
    pairs = []
    for source in range(128):
        x, y, z, core = place(source)
        x, y, z, core = target(x, y, z, core)
        pairs.append((source, index_of(x % 4, y % 4, z % 4, core % 2)))
    return lax.ppermute(array, ("inner", "outer"), pairs)


def along_first(array, d):
    return permute(array, lambda x, y, z, c: (x, y, z + d, c) if c else (x + d, y, z, c))


def along_second(array, d):
    return permute(array, lambda x, y, z, c: (x + d, y, z, c) if c else (x, y, z + d, c))


def along_y(array, d):
    return permute(array, lambda x, y, z, c: (x, y + d, z, c))


def other_core(array):
    return permute(array, lambda x, y, z, c: (x, y, z, c + 1))


def after(array, *others):
    return lax.optimization_barrier((array, *others))[0]


def prepared(kernel, name, positions, rows, *shapes):
    return pl.pallas_call(
        kernel,
        out_shape=shapes,
        in_specs=[HBM, HBM],
        out_specs=(VMEM,) * len(shapes),
        scratch_shapes=[
            pltpu.SMEM(positions.shape, jnp.int32),
            pltpu.VMEM(rows.shape, BF16),
            pltpu.SemaphoreType.DMA((2,)),
        ],
        compiler_params=pltpu.CompilerParams(vmem_limit_bytes=63 << 20),
        name=name,
    )(positions, rows)


def shards(queries, key_value, positions, sinks):
    (km,) = prepared(
        prepare_keys,
        "prepare_keys",
        positions,
        key_value,
        jax.ShapeDtypeStruct((1, MSG, 128), BF16),
    )
    qm, flag = prepared(
        prepare_queries,
        "prepare_queries",
        positions,
        after(queries, km),
        jax.ShapeDtypeStruct((QMSG, ROWS), BF16),
        jax.ShapeDtypeStruct((8, ROWS), F32),
    )
    right = along_first(km, 1)
    row = jnp.concatenate([after(km, qm), right, along_first(km, -1), along_first(km, 2)], axis=0)
    asked = after(qm, right)
    up, down, over = along_y(asked, 1), along_y(asked, -1), along_y(asked, 2)
    chunks = [(row, other_core(row))]
    own = partials([qm], chunks)
    diag = simple(
        diagonal, jax.ShapeDtypeStruct((PART + 8, ROWS), F32), "diagonal", after(qm, own), km, flag
    )
    for d in (1, -1, 2):
        group = along_second(row, d)
        chunks.append((group, other_core(after(group, diag))))
    back, last = [], own
    for query, d in ((up, -1), (over, -2), (down, 1)):
        last = partials([after(query, last)], chunks, packed=True)
        back.append(along_y(last, d))
    own = partials([after(qm, last)], chunks[1:2], own, 0)
    own = partials([after(qm, own, back[0])], chunks[2:3], own, 0)
    own = partials([after(qm, own, back[1])], chunks[3:], own, 0)
    sink_row = jnp.broadcast_to(jnp.repeat(sinks, SPAN)[None], (8, ROWS))
    return simple(
        functools.partial(finish, 2, 3),
        jax.ShapeDtypeStruct(queries.shape, BF16),
        "finish",
        sink_row,
        diag,
        own.reshape(PART, ROWS),
        *back,
    )


def solution(mesh):
    return jax.shard_map(
        shards,
        mesh=mesh,
        in_specs=(
            P(("inner", "outer"), None),
            P(("inner", "outer"), None),
            P(("inner", "outer")),
            P(),
        ),
        out_specs=P(("inner", "outer"), None),
        check_vma=False,
    )
```

```python
import functools

import jax
import jax.numpy as jnp
from jax import lax
from jax.experimental import pallas as pl
from jax.experimental.pallas import tpu as pltpu
from jax.sharding import PartitionSpec as P

HEADS = 8
HD = 64
SPAN = 96
ROWS = HEADS * SPAN
GROUP = 8
CHUNK = GROUP * SPAN
MSG = 208
QMSG = 144
PART = 160
LOG2E = 1.4426950408889634
SCALE = HD**-0.5 * LOG2E
LIMIT = 1e36
F32 = jnp.float32
BF16 = jnp.bfloat16
VMEM = pl.BlockSpec(memory_space=pltpu.VMEM)
HBM = pl.BlockSpec(memory_space=pltpu.HBM)
PARAMS = pltpu.CompilerParams(vmem_limit_bytes=20 << 20)


def dot(a, b):
    return jnp.dot(a, b, preferred_element_type=F32)


def load(pairs, sems):
    copies = [
        pltpu.make_async_copy(source, target, sems.at[n]) for n, (source, target) in enumerate(pairs)
    ]
    for copy in copies:
        copy.start()
    for copy in copies:
        copy.wait()


def order(pos_ref, ref):
    run = pos_ref[0] // SPAN
    swapped = run >= 128
    first, second = ref[0:SPAN, :], ref[SPAN : 2 * SPAN, :]
    lower = jnp.where(swapped, 255 - run, run).astype(F32)
    return swapped, lower, jnp.where(swapped, second, first), jnp.where(swapped, first, second)


def prepare_keys(pos_hbm, kv_hbm, km_ref, pos_ref, kv_ref, sems):
    load(((pos_hbm, pos_ref), (kv_hbm, kv_ref)), sems)
    _, lower, lo, up = order(pos_ref, kv_ref)
    km_ref[0, 0:SPAN, :] = jnp.concatenate([lo[:, :HD], up[:, :HD]], axis=1)
    km_ref[0, SPAN : 2 * SPAN, :] = jnp.concatenate([lo[:, HD:], up[:, HD:]], axis=1)
    km_ref[0, 2 * SPAN :, :] = jnp.full((MSG - 2 * SPAN, 128), lower, F32).astype(BF16)


def prepare_queries(pos_hbm, q_hbm, qm_ref, flag_ref, pos_ref, q_ref, sems):
    load(((pos_hbm, pos_ref), (q_hbm, q_ref)), sems)
    swapped, lower, lo, up = order(pos_ref, q_ref)
    stacked = jnp.concatenate(
        [
            jnp.concatenate([lo[:, h * HD : (h + 1) * HD], up[:, h * HD : (h + 1) * HD]], axis=1)
            for h in range(HEADS)
        ],
        axis=0,
    )
    qm_ref[0:128, :] = jnp.transpose(stacked)
    qm_ref[128:, :] = jnp.full((QMSG - 128, ROWS), lower, F32).astype(BF16)
    flag_ref[...] = jnp.full((8, ROWS), jnp.where(swapped, 1.0, 0.0), F32)


def diagonal(qm_ref, km_ref, flag_ref, out_ref):
    out_ref[PART:, :] = flag_ref[...]
    keys = lax.broadcasted_iota(jnp.int32, (SPAN, ROWS), 0)
    rows = lax.broadcasted_iota(jnp.int32, (SPAN, ROWS), 1)
    mine = rows
    for h in range(1, HEADS):
        mine = jnp.where(rows >= h * SPAN, rows - h * SPAN, mine)
    visible = keys <= mine
    k = km_ref[0, 0:SPAN, :]
    v = jnp.transpose(km_ref[0, SPAN : 2 * SPAN, :].astype(F32)).astype(BF16)
    for half in range(2):
        part = slice(half * HD, (half + 1) * HD)
        s = dot(k[:, part], qm_ref[part, :]) * SCALE
        s = jnp.where(visible, s, -1e30)
        shift = jnp.maximum(jnp.max(s, axis=0, keepdims=True), 0.0)
        p = jnp.where(visible, jnp.exp2(s - shift), 0.0)
        out_ref[part, :] = dot(v[part, :], p.astype(BF16))
        total = jnp.sum(p, axis=0, keepdims=True)
        out_ref[128 + 8 * half : 136 + 8 * half, :] = jnp.broadcast_to(total, (8, ROWS))
        out_ref[144 + 8 * half : 152 + 8 * half, :] = jnp.broadcast_to(shift, (8, ROWS))


def chunk_masks(keys, q_ref):
    info = keys[:, 2 * SPAN : 2 * SPAN + 16, :].astype(F32)[:, 0:1, :]
    own = q_ref[128:144, 0:128].astype(F32)[0:1, :]
    below = jnp.where(info < own[None], 1.0, 0.0)
    above = jnp.where(info > own[None], 1.0, 0.0)
    return below, above


def along_lanes(mask):
    lanes = lax.broadcasted_iota(jnp.int32, (16, CHUNK), 1)
    wide = [
        jnp.concatenate([jnp.broadcast_to(mask[b], (16, 128))] * (CHUNK // 128), axis=1)
        for b in range(GROUP)
    ]
    out = wide[0]
    for b in range(1, GROUP):
        out = jnp.where(lanes >= b * SPAN, wide[b], out)
    return out


def transposed_values(keys):
    return jnp.transpose(keys[:, SPAN : 2 * SPAN, :].reshape(CHUNK, 128))


def chunk_operands(keys, q_ref, vt):
    below, above = chunk_masks(keys, q_ref)
    k = keys[:, 0:SPAN, :]
    lanes = lax.broadcasted_iota(jnp.int32, (GROUP, 1, 128), 2)
    keep = jnp.where(lanes < HD, below, above).astype(BF16)
    chosen = (k * keep).reshape(CHUNK, 128)
    low, high = along_lanes(below), along_lanes(above)
    rows = lax.broadcasted_iota(jnp.int32, (16, CHUNK), 0)
    ones = jnp.where(rows < 8, low, high).astype(BF16)
    low, high = low[0:1].astype(BF16), high[0:1].astype(BF16)
    values = jnp.concatenate([vt[:HD] * low, vt[HD:] * high, ones], axis=0)
    return k.reshape(CHUNK, 128), chosen, values


def each(count, body):
    if count == 1:
        body(0)
    else:
        pl.loop(0, count)(body)


def attend(nq, nc, at, packed, *refs):
    q_refs, refs = refs[:nq], refs[nq:]
    key_refs, refs = refs[:nc], refs[nc:]
    if at is not None:
        old_ref, refs = refs[0], refs[1:]
    out_ref, refs = refs[0], refs[1:]
    sums = refs[0] if packed else out_ref
    queries, keys = refs[-2], refs[-1]
    for q in range(nq):
        queries[q] = q_refs[q][...]
        sums[q] = jnp.zeros((PART, ROWS), F32) if at is None else old_ref[at + q]
    for c in range(nc):
        keys[c] = key_refs[c][...]

    def add(c):
        chunk = keys[c]
        vt = transposed_values(chunk)
        first = jnp.concatenate([vt[:HD], jnp.ones((16, CHUNK), BF16)], axis=0)

        def one(q):
            q_ref = queries.at[q]
            k, chosen, values = chunk_operands(chunk, q_ref, vt)
            a = dot(k[:, :HD], q_ref[HD:128, :])
            b = dot(chosen, q_ref[0:128, :])
            pa = jnp.exp2(a * SCALE).astype(BF16)
            pb = jnp.exp2(b * SCALE).astype(BF16)
            oa = dot(first, pa)
            ob = dot(values, pb)
            sums[q, 0:HD, :] += ob[:HD]
            sums[q, HD:128, :] += oa[:HD] + ob[HD:128]
            sums[q, 128:136, :] += ob[128:136]
            sums[q, 136:144, :] += oa[HD : HD + 8] + ob[136:144]

        each(nq, one)

    each(nc, add)

    def check(q):
        bad = jnp.sum(jnp.where(sums[q, 128:144, :] < LIMIT, 0.0, 1.0))
        bad = bad + jnp.sum(sums[q, 144:160, :])

        @pl.when(bad > 0.0)
        def _():
            for k in range(nq):

                @pl.when(q == k)
                def _():
                    sums[k] = jnp.zeros((PART, ROWS), F32) if at is None else old_ref[at + k]

            @pl.loop(0, nc)
            def _(c):
                careful(keys.at[c], queries.at[q], sums.at[q])

    each(nq, check)

    if packed:
        for q in range(nq):
            out_ref[0:128, :] = sums[q, 0:128, :].astype(BF16)
            rows = lax.broadcasted_iota(jnp.int32, (16, ROWS), 0)
            stats = jnp.zeros((16, ROWS), F32)
            for row, start in ((0, 128), (2, 136)):
                total = jnp.broadcast_to(sums[q, start : start + 1, :], (16, ROWS))
                high = total.astype(BF16).astype(F32)
                stats = jnp.where(rows == row, high, stats)
                stats = jnp.where(rows == row + 1, total - high, stats)
            for row, start in ((4, 144), (5, 152)):
                shift = jnp.broadcast_to(sums[q, start : start + 1, :], (16, ROWS))
                stats = jnp.where(rows == row, shift, stats)
            out_ref[128:144, :] = stats.astype(BF16)


def careful(keys, q_ref, out_ref):
    def raise_shift(half, top):
        old = out_ref[144 + 8 * half : 145 + 8 * half, :]
        new = jnp.maximum(old, jnp.maximum(top, 0.0).astype(BF16).astype(F32))
        factor = jnp.exp2(old - new)
        out_ref[half * HD : (half + 1) * HD, :] *= factor
        out_ref[128 + 8 * half : 136 + 8 * half, :] *= factor
        out_ref[144 + 8 * half : 152 + 8 * half, :] = jnp.broadcast_to(new, (8, ROWS))
        return new

    def add(half, values, p):
        p = p.astype(BF16)
        out_ref[half * HD : (half + 1) * HD, :] += dot(values, p)
        out_ref[128 + 8 * half : 136 + 8 * half, :] += dot(jnp.ones((16, SPAN), BF16), p)[:8]

    def wide(row):
        return jnp.concatenate([row] * (ROWS // 128), axis=1)

    own = wide(q_ref[128:144, 0:128].astype(F32)[0:1, :])

    @pl.loop(0, GROUP)
    def _(b):
        k = keys[b, 0:SPAN, :]
        vt = jnp.transpose(keys[b, SPAN : 2 * SPAN, :].astype(F32)).astype(BF16)
        info = wide(keys[b, 2 * SPAN : 2 * SPAN + 16, :].astype(F32)[0:1, :])
        low = dot(k[:, :HD], q_ref[HD:128, :]) * SCALE
        shift = raise_shift(1, jnp.max(low, axis=0, keepdims=True))
        add(1, vt[:HD], jnp.exp2(low - shift))
        for half, seen in ((0, info < own), (1, info > own)):
            part = slice(half * HD, (half + 1) * HD)
            s = dot(k[:, part], q_ref[part, :]) * SCALE
            top = jnp.where(seen, jnp.max(s, axis=0, keepdims=True), -1e30)
            shift = raise_shift(half, top)
            add(half, vt[part], jnp.where(seen, jnp.exp2(s - shift), 0.0))


def finish(held, sent, sink_ref, *refs):
    parts, out_ref = refs[: held + sent], refs[held + sent]
    swapped = jnp.broadcast_to(refs[0][PART : PART + 1, 0:128], (SPAN, 128)) > 0.5
    results = []
    for half in range(2):
        part = slice(half * HD, (half + 1) * HD)
        terms = [
            (p[144 + 8 * half : 145 + 8 * half, :], p[128 + 8 * half : 129 + 8 * half, :], p[part, :])
            for p in parts[:held]
        ]
        for p in parts[held:]:
            stats = p[128:144, :].astype(F32)
            total = stats[2 * half : 2 * half + 1] + stats[2 * half + 1 : 2 * half + 2]
            terms.append((stats[4 + half : 5 + half], total, p[part, :].astype(F32)))
        top = functools.reduce(jnp.maximum, [shift for shift, _, _ in terms])
        total = jnp.exp2(sink_ref[0:1, :] * LOG2E - top)
        sums = jnp.zeros((HD, ROWS), F32)
        for shift, some, weighted in terms:
            factor = jnp.exp2(shift - top)
            total = total + some * factor
            sums = sums + weighted * factor
        results.append(sums / total)
    both = jnp.transpose(jnp.concatenate(results, axis=0))
    for g in range(HEADS // 2):
        even, odd = both[2 * g * SPAN : (2 * g + 1) * SPAN], both[(2 * g + 1) * SPAN : (2 * g + 2) * SPAN]
        lo = jnp.concatenate([even[:, :HD], odd[:, :HD]], axis=1)
        up = jnp.concatenate([even[:, HD:], odd[:, HD:]], axis=1)
        lanes = slice(128 * g, 128 * (g + 1))
        out_ref[0:SPAN, lanes] = jnp.where(swapped, up, lo).astype(BF16)
        out_ref[SPAN : 2 * SPAN, lanes] = jnp.where(swapped, lo, up).astype(BF16)


def partials(queries, chunks, old=None, at=None, packed=False):
    nq, nc = len(queries), len(chunks)
    pairs = nq * nc * 2 * CHUNK * ROWS
    operands = [*queries, *chunks, *([] if at is None else [old])]
    sums = (nq, PART, ROWS)
    shape = jax.ShapeDtypeStruct(sums, F32)
    if packed:
        shape = jax.ShapeDtypeStruct((QMSG, ROWS), BF16)
    return pl.pallas_call(
        functools.partial(attend, nq, nc, at, packed),
        out_shape=shape,
        in_specs=[VMEM] * len(operands),
        out_specs=VMEM,
        scratch_shapes=([pltpu.VMEM(sums, F32)] if packed else [])
        + [pltpu.VMEM((nq, QMSG, ROWS), BF16), pltpu.VMEM((nc, GROUP, MSG, 128), BF16)],
        compiler_params=PARAMS,
        cost_estimate=pl.CostEstimate(
            flops=pairs * 16, bytes_accessed=nc * 2**14, transcendentals=0
        ),
        name="attend",
    )(*operands)


def simple(kernel, shape, name, *operands):
    return pl.pallas_call(
        kernel,
        out_shape=shape,
        in_specs=[VMEM] * len(operands),
        out_specs=VMEM,
        compiler_params=PARAMS,
        name=name,
    )(*operands)


def place(index):
    inner, outer = divmod(index, 16)
    return inner % 4, inner // 4 * 2 + outer // 2 % 2, outer // 4, outer % 2


def index_of(x, y, z, core):
    return (y // 2 * 4 + x) * 16 + z * 4 + y % 2 * 2 + core


def permute(array, target):
    pairs = []
    for source in range(128):
        x, y, z, core = place(source)
        x, y, z, core = target(x, y, z, core)
        pairs.append((source, index_of(x % 4, y % 4, z % 4, core % 2)))
    return lax.ppermute(array, ("inner", "outer"), pairs)


def along_first(array, d):
    return permute(array, lambda x, y, z, c: (x, y, z + d, c) if c else (x + d, y, z, c))


def along_second(array, d):
    return permute(array, lambda x, y, z, c: (x + d, y, z, c) if c else (x, y, z + d, c))


def y_neighbour(array):
    return permute(array, lambda x, y, z, c: (x, y ^ 1, z, c))


def y_opposite(array):
    return permute(array, lambda x, y, z, c: (x, y + 2, z, c))


def other_core(array):
    return permute(array, lambda x, y, z, c: (x, y, z, c + 1))


def after(array, *others):
    return lax.optimization_barrier((array, *others))[0]


def prepared(kernel, name, positions, rows, *shapes):
    return pl.pallas_call(
        kernel,
        out_shape=shapes,
        in_specs=[HBM, HBM],
        out_specs=(VMEM,) * len(shapes),
        scratch_shapes=[
            pltpu.SMEM(positions.shape, jnp.int32),
            pltpu.VMEM(rows.shape, BF16),
            pltpu.SemaphoreType.DMA((2,)),
        ],
        compiler_params=pltpu.CompilerParams(vmem_limit_bytes=63 << 20),
        name=name,
    )(positions, rows)


def shards(queries, key_value, positions, sinks):
    (km,) = prepared(
        prepare_keys,
        "prepare_keys",
        positions,
        key_value,
        jax.ShapeDtypeStruct((1, MSG, 128), BF16),
    )
    qm, flag = prepared(
        prepare_queries,
        "prepare_queries",
        positions,
        after(queries, km),
        jax.ShapeDtypeStruct((QMSG, ROWS), BF16),
        jax.ShapeDtypeStruct((8, ROWS), F32),
    )
    pair = jnp.concatenate([after(km, qm), y_neighbour(km)], axis=0)
    asked = y_opposite(qm)
    row = [pair, along_first(pair, 1), along_first(pair, -1), along_first(pair, 2)]
    group = jnp.concatenate([after(pair, asked), *row[1:]], axis=0)
    near = [group, other_core(group)]
    own = partials([qm], near[:1])
    sides = []
    for d in (1, -1, 2):
        side = along_second(group, d)
        sides.append([side, other_core(after(side, own))])
    mate = partials([after(asked, own)], near)
    diag = simple(
        diagonal, jax.ShapeDtypeStruct((PART + 8, ROWS), F32), "diagonal", after(qm, mate), km, flag
    )
    mate = partials([after(asked, diag)], sides[0], mate, 0)
    sent = partials([asked], sides[1] + sides[2], mate, 0, packed=True)
    back = y_opposite(sent)
    own = partials([after(qm, sent)], near[1:] + sides[0], own, 0)
    own = partials([qm], sides[1], own, 0)
    own = partials([qm], sides[2], own, 0)
    sink_row = jnp.broadcast_to(jnp.repeat(sinks, SPAN)[None], (8, ROWS))
    return simple(
        functools.partial(finish, 2, 1),
        jax.ShapeDtypeStruct(queries.shape, BF16),
        "finish",
        sink_row,
        diag,
        own.reshape(PART, ROWS),
        back,
    )


def solution(mesh):
    return jax.shard_map(
        shards,
        mesh=mesh,
        in_specs=(
            P(("inner", "outer"), None),
            P(("inner", "outer"), None),
            P(("inner", "outer")),
            P(),
        ),
        out_specs=P(("inner", "outer"), None),
        check_vma=False,
    )
```

```python
import functools

import jax
import jax.numpy as jnp
from jax import lax
from jax.experimental import pallas as pl
from jax.experimental.pallas import tpu as pltpu
from jax.sharding import PartitionSpec as P

HEADS = 8
HD = 64
SPAN = 96
ROWS = HEADS * SPAN
GROUP = 8
CHUNK = GROUP * SPAN
MSG = 208
QMSG = 144
PART = 160
LOG2E = 1.4426950408889634
SCALE = HD**-0.5 * LOG2E
LIMIT = 1e36
F32 = jnp.float32
BF16 = jnp.bfloat16
VMEM = pl.BlockSpec(memory_space=pltpu.VMEM)
HBM = pl.BlockSpec(memory_space=pltpu.HBM)
PARAMS = pltpu.CompilerParams(vmem_limit_bytes=20 << 20)


def dot(a, b):
    return jnp.dot(a, b, preferred_element_type=F32)


def load(pairs, sems):
    copies = [
        pltpu.make_async_copy(source, target, sems.at[n]) for n, (source, target) in enumerate(pairs)
    ]
    for copy in copies:
        copy.start()
    for copy in copies:
        copy.wait()


def order(pos_ref, ref):
    run = pos_ref[0] // SPAN
    swapped = run >= 128
    first, second = ref[0:SPAN, :], ref[SPAN : 2 * SPAN, :]
    lower = jnp.where(swapped, 255 - run, run).astype(F32)
    return swapped, lower, jnp.where(swapped, second, first), jnp.where(swapped, first, second)


def prepare_keys(pos_hbm, kv_hbm, km_ref, pos_ref, kv_ref, sems):
    load(((pos_hbm, pos_ref), (kv_hbm, kv_ref)), sems)
    _, lower, lo, up = order(pos_ref, kv_ref)
    km_ref[0, 0:SPAN, :] = jnp.concatenate([lo[:, :HD], up[:, :HD]], axis=1)
    km_ref[0, SPAN : 2 * SPAN, :] = jnp.concatenate([lo[:, HD:], up[:, HD:]], axis=1)
    km_ref[0, 2 * SPAN :, :] = jnp.full((MSG - 2 * SPAN, 128), lower, F32).astype(BF16)


def prepare_queries(pos_hbm, q_hbm, qm_ref, flag_ref, pos_ref, q_ref, sems):
    load(((pos_hbm, pos_ref), (q_hbm, q_ref)), sems)
    swapped, lower, lo, up = order(pos_ref, q_ref)
    stacked = jnp.concatenate(
        [
            jnp.concatenate([lo[:, h * HD : (h + 1) * HD], up[:, h * HD : (h + 1) * HD]], axis=1)
            for h in range(HEADS)
        ],
        axis=0,
    )
    qm_ref[0:128, :] = jnp.transpose(stacked)
    qm_ref[128:, :] = jnp.full((QMSG - 128, ROWS), lower, F32).astype(BF16)
    flag_ref[...] = jnp.full((8, ROWS), jnp.where(swapped, 1.0, 0.0), F32)


def diagonal(qm_ref, km_ref, flag_ref, out_ref):
    out_ref[PART:, :] = flag_ref[...]
    keys = lax.broadcasted_iota(jnp.int32, (SPAN, ROWS), 0)
    rows = lax.broadcasted_iota(jnp.int32, (SPAN, ROWS), 1)
    mine = rows
    for h in range(1, HEADS):
        mine = jnp.where(rows >= h * SPAN, rows - h * SPAN, mine)
    visible = keys <= mine
    k = km_ref[0, 0:SPAN, :]
    v = jnp.transpose(km_ref[0, SPAN : 2 * SPAN, :].astype(F32)).astype(BF16)
    for half in range(2):
        part = slice(half * HD, (half + 1) * HD)
        s = dot(k[:, part], qm_ref[part, :]) * SCALE
        s = jnp.where(visible, s, -1e30)
        shift = jnp.maximum(jnp.max(s, axis=0, keepdims=True), 0.0)
        p = jnp.where(visible, jnp.exp2(s - shift), 0.0)
        out_ref[part, :] = dot(v[part, :], p.astype(BF16))
        total = jnp.sum(p, axis=0, keepdims=True)
        out_ref[128 + 8 * half : 136 + 8 * half, :] = jnp.broadcast_to(total, (8, ROWS))
        out_ref[144 + 8 * half : 152 + 8 * half, :] = jnp.broadcast_to(shift, (8, ROWS))


def chunk_masks(keys, q_ref):
    info = keys[:, 2 * SPAN : 2 * SPAN + 16, :].astype(F32)[:, 0:1, :]
    own = q_ref[128:144, 0:128].astype(F32)[0:1, :]
    below = jnp.where(info < own[None], 1.0, 0.0)
    above = jnp.where(info > own[None], 1.0, 0.0)
    return below, above


def along_lanes(mask):
    lanes = lax.broadcasted_iota(jnp.int32, (16, CHUNK), 1)
    wide = [
        jnp.concatenate([jnp.broadcast_to(mask[b], (16, 128))] * (CHUNK // 128), axis=1)
        for b in range(GROUP)
    ]
    out = wide[0]
    for b in range(1, GROUP):
        out = jnp.where(lanes >= b * SPAN, wide[b], out)
    return out


def transposed_values(keys):
    return jnp.transpose(keys[:, SPAN : 2 * SPAN, :].reshape(CHUNK, 128))


def chunk_operands(keys, q_ref, vt):
    below, above = chunk_masks(keys, q_ref)
    k = keys[:, 0:SPAN, :]
    lanes = lax.broadcasted_iota(jnp.int32, (GROUP, 1, 128), 2)
    keep = jnp.where(lanes < HD, below, above).astype(BF16)
    chosen = (k * keep).reshape(CHUNK, 128)
    low, high = along_lanes(below), along_lanes(above)
    rows = lax.broadcasted_iota(jnp.int32, (16, CHUNK), 0)
    ones = jnp.where(rows < 8, low, high).astype(BF16)
    low, high = low[0:1].astype(BF16), high[0:1].astype(BF16)
    values = jnp.concatenate([vt[:HD] * low, vt[HD:] * high, ones], axis=0)
    return k.reshape(CHUNK, 128), chosen, values


def each(count, body):
    if count == 1:
        body(0)
    else:
        pl.loop(0, count)(body)


def attend(nq, nc, at, packed, *refs):
    q_refs, refs = refs[:nq], refs[nq:]
    key_refs, refs = refs[:nc], refs[nc:]
    if at is not None:
        old_ref, refs = refs[0], refs[1:]
    out_ref, refs = refs[0], refs[1:]
    sums = refs[0] if packed else out_ref
    queries, keys = refs[-2], refs[-1]
    for q in range(nq):
        queries[q] = q_refs[q][...]
        sums[q] = jnp.zeros((PART, ROWS), F32) if at is None else old_ref[at + q]
    for c in range(nc):
        keys[c] = key_refs[c][...]

    def add(c):
        chunk = keys[c]
        vt = transposed_values(chunk)
        first = jnp.concatenate([vt[:HD], jnp.ones((16, CHUNK), BF16)], axis=0)

        def one(q):
            q_ref = queries.at[q]
            k, chosen, values = chunk_operands(chunk, q_ref, vt)
            a = dot(k[:, :HD], q_ref[HD:128, :])
            b = dot(chosen, q_ref[0:128, :])
            pa = jnp.exp2(a * SCALE).astype(BF16)
            pb = jnp.exp2(b * SCALE).astype(BF16)
            oa = dot(first, pa)
            ob = dot(values, pb)
            sums[q, 0:HD, :] += ob[:HD]
            sums[q, HD:128, :] += oa[:HD] + ob[HD:128]
            sums[q, 128:136, :] += ob[128:136]
            sums[q, 136:144, :] += oa[HD : HD + 8] + ob[136:144]

        each(nq, one)

    each(nc, add)

    def check(q):
        bad = jnp.sum(jnp.where(sums[q, 128:144, :] < LIMIT, 0.0, 1.0))
        bad = bad + jnp.sum(sums[q, 144:160, :])

        @pl.when(bad > 0.0)
        def _():
            for k in range(nq):

                @pl.when(q == k)
                def _():
                    sums[k] = jnp.zeros((PART, ROWS), F32) if at is None else old_ref[at + k]

            @pl.loop(0, nc)
            def _(c):
                careful(keys.at[c], queries.at[q], sums.at[q])

    each(nq, check)

    if packed:
        for q in range(nq):
            out_ref[0:128, :] = sums[q, 0:128, :].astype(BF16)
            rows = lax.broadcasted_iota(jnp.int32, (16, ROWS), 0)
            stats = jnp.zeros((16, ROWS), F32)
            for row, start in ((0, 128), (2, 136)):
                total = jnp.broadcast_to(sums[q, start : start + 1, :], (16, ROWS))
                high = total.astype(BF16).astype(F32)
                stats = jnp.where(rows == row, high, stats)
                stats = jnp.where(rows == row + 1, total - high, stats)
            for row, start in ((4, 144), (5, 152)):
                shift = jnp.broadcast_to(sums[q, start : start + 1, :], (16, ROWS))
                stats = jnp.where(rows == row, shift, stats)
            out_ref[128:144, :] = stats.astype(BF16)


def careful(keys, q_ref, out_ref):
    def raise_shift(half, top):
        old = out_ref[144 + 8 * half : 145 + 8 * half, :]
        new = jnp.maximum(old, jnp.maximum(top, 0.0).astype(BF16).astype(F32))
        factor = jnp.exp2(old - new)
        out_ref[half * HD : (half + 1) * HD, :] *= factor
        out_ref[128 + 8 * half : 136 + 8 * half, :] *= factor
        out_ref[144 + 8 * half : 152 + 8 * half, :] = jnp.broadcast_to(new, (8, ROWS))
        return new

    def add(half, values, p):
        p = p.astype(BF16)
        out_ref[half * HD : (half + 1) * HD, :] += dot(values, p)
        out_ref[128 + 8 * half : 136 + 8 * half, :] += dot(jnp.ones((16, SPAN), BF16), p)[:8]

    def wide(row):
        return jnp.concatenate([row] * (ROWS // 128), axis=1)

    own = wide(q_ref[128:144, 0:128].astype(F32)[0:1, :])

    @pl.loop(0, GROUP)
    def _(b):
        k = keys[b, 0:SPAN, :]
        vt = jnp.transpose(keys[b, SPAN : 2 * SPAN, :].astype(F32)).astype(BF16)
        info = wide(keys[b, 2 * SPAN : 2 * SPAN + 16, :].astype(F32)[0:1, :])
        low = dot(k[:, :HD], q_ref[HD:128, :]) * SCALE
        shift = raise_shift(1, jnp.max(low, axis=0, keepdims=True))
        add(1, vt[:HD], jnp.exp2(low - shift))
        for half, seen in ((0, info < own), (1, info > own)):
            part = slice(half * HD, (half + 1) * HD)
            s = dot(k[:, part], q_ref[part, :]) * SCALE
            top = jnp.where(seen, jnp.max(s, axis=0, keepdims=True), -1e30)
            shift = raise_shift(half, top)
            add(half, vt[part], jnp.where(seen, jnp.exp2(s - shift), 0.0))


def finish(held, sent, sink_ref, *refs):
    parts, out_ref = refs[: held + sent], refs[held + sent]
    swapped = jnp.broadcast_to(refs[0][PART : PART + 1, 0:128], (SPAN, 128)) > 0.5
    results = []
    for half in range(2):
        part = slice(half * HD, (half + 1) * HD)
        terms = [
            (p[144 + 8 * half : 145 + 8 * half, :], p[128 + 8 * half : 129 + 8 * half, :], p[part, :])
            for p in parts[:held]
        ]
        for p in parts[held:]:
            stats = p[128:144, :].astype(F32)
            total = stats[2 * half : 2 * half + 1] + stats[2 * half + 1 : 2 * half + 2]
            terms.append((stats[4 + half : 5 + half], total, p[part, :].astype(F32)))
        top = functools.reduce(jnp.maximum, [shift for shift, _, _ in terms])
        total = jnp.exp2(sink_ref[0:1, :] * LOG2E - top)
        sums = jnp.zeros((HD, ROWS), F32)
        for shift, some, weighted in terms:
            factor = jnp.exp2(shift - top)
            total = total + some * factor
            sums = sums + weighted * factor
        results.append(sums / total)
    both = jnp.transpose(jnp.concatenate(results, axis=0))
    for g in range(HEADS // 2):
        even, odd = both[2 * g * SPAN : (2 * g + 1) * SPAN], both[(2 * g + 1) * SPAN : (2 * g + 2) * SPAN]
        lo = jnp.concatenate([even[:, :HD], odd[:, :HD]], axis=1)
        up = jnp.concatenate([even[:, HD:], odd[:, HD:]], axis=1)
        lanes = slice(128 * g, 128 * (g + 1))
        out_ref[0:SPAN, lanes] = jnp.where(swapped, up, lo).astype(BF16)
        out_ref[SPAN : 2 * SPAN, lanes] = jnp.where(swapped, lo, up).astype(BF16)


def partials(queries, chunks, old=None, at=None, packed=False):
    nq, nc = len(queries), len(chunks)
    pairs = nq * nc * 2 * CHUNK * ROWS
    operands = [*queries, *chunks, *([] if at is None else [old])]
    sums = (nq, PART, ROWS)
    shape = jax.ShapeDtypeStruct(sums, F32)
    if packed:
        shape = jax.ShapeDtypeStruct((QMSG, ROWS), BF16)
    return pl.pallas_call(
        functools.partial(attend, nq, nc, at, packed),
        out_shape=shape,
        in_specs=[VMEM] * len(operands),
        out_specs=VMEM,
        scratch_shapes=([pltpu.VMEM(sums, F32)] if packed else [])
        + [pltpu.VMEM((nq, QMSG, ROWS), BF16), pltpu.VMEM((nc, GROUP, MSG, 128), BF16)],
        compiler_params=PARAMS,
        cost_estimate=pl.CostEstimate(
            flops=pairs * 16, bytes_accessed=nc * 2**14, transcendentals=0
        ),
        name="attend",
    )(*operands)


def simple(kernel, shape, name, *operands):
    return pl.pallas_call(
        kernel,
        out_shape=shape,
        in_specs=[VMEM] * len(operands),
        out_specs=VMEM,
        compiler_params=PARAMS,
        name=name,
    )(*operands)


def place(index):
    inner, outer = divmod(index, 16)
    return inner % 4, inner // 4 * 2 + outer // 2 % 2, outer // 4, outer % 2


def index_of(x, y, z, core):
    return (y // 2 * 4 + x) * 16 + z * 4 + y % 2 * 2 + core


def permute(array, target):
    pairs = []
    for source in range(128):
        x, y, z, core = place(source)
        x, y, z, core = target(x, y, z, core)
        pairs.append((source, index_of(x % 4, y % 4, z % 4, core % 2)))
    return lax.ppermute(array, ("inner", "outer"), pairs)


def along_first(array, d):
    return permute(array, lambda x, y, z, c: (x, y, z + d, c) if c else (x + d, y, z, c))


def along_second(array, d):
    return permute(array, lambda x, y, z, c: (x + d, y, z, c) if c else (x, y, z + d, c))


def y_neighbour(array):
    return permute(array, lambda x, y, z, c: (x, y ^ 1, z, c))


def y_opposite(array):
    return permute(array, lambda x, y, z, c: (x, y + 2, z, c))


def other_core(array):
    return permute(array, lambda x, y, z, c: (x, y, z, c + 1))


def after(array, *others):
    return lax.optimization_barrier((array, *others))[0]


def prepared(kernel, name, positions, rows, *shapes):
    return pl.pallas_call(
        kernel,
        out_shape=shapes,
        in_specs=[HBM, HBM],
        out_specs=(VMEM,) * len(shapes),
        scratch_shapes=[
            pltpu.SMEM(positions.shape, jnp.int32),
            pltpu.VMEM(rows.shape, BF16),
            pltpu.SemaphoreType.DMA((2,)),
        ],
        compiler_params=pltpu.CompilerParams(vmem_limit_bytes=63 << 20),
        name=name,
    )(positions, rows)


def shards(queries, key_value, positions, sinks):
    (km,) = prepared(
        prepare_keys,
        "prepare_keys",
        positions,
        key_value,
        jax.ShapeDtypeStruct((1, MSG, 128), BF16),
    )
    qm, flag = prepared(
        prepare_queries,
        "prepare_queries",
        positions,
        after(queries, km),
        jax.ShapeDtypeStruct((QMSG, ROWS), BF16),
        jax.ShapeDtypeStruct((8, ROWS), F32),
    )
    pair = jnp.concatenate([after(km, qm), y_neighbour(km)], axis=0)
    asked = y_opposite(qm)
    row = [pair, along_first(pair, 1), along_first(pair, -1), along_first(pair, 2)]
    group = jnp.concatenate([after(pair, asked), *row[1:]], axis=0)
    near, near2 = group, other_core(group)
    side1, side2, side3 = [along_second(group, d) for d in (1, -1, 2)]
    own = partials([qm], [near])
    mate = partials([after(asked, own)], [near, near2])
    own = partials([after(qm, mate)], [near2], own, 0)
    diag = simple(
        diagonal, jax.ShapeDtypeStruct((PART + 8, ROWS), F32), "diagonal", after(qm, own), km, flag
    )
    swap1, swap2 = other_core(after(side1, diag)), other_core(after(side2, diag))
    mate = partials([after(asked, diag)], [side1], mate, 0)
    swap3 = other_core(after(side3, mate))
    mate = partials([asked], [side2, swap1], mate, 0)
    sent = partials([asked], [side3, swap2, swap3], mate, 0, packed=True)
    back = y_opposite(sent)
    own = partials([after(qm, sent)], [side1, swap1], own, 0)
    own = partials([qm], [side2, swap2], own, 0)
    own = partials([qm], [side3, swap3], own, 0)
    sink_row = jnp.broadcast_to(jnp.repeat(sinks, SPAN)[None], (8, ROWS))
    return simple(
        functools.partial(finish, 2, 1),
        jax.ShapeDtypeStruct(queries.shape, BF16),
        "finish",
        sink_row,
        diag,
        own.reshape(PART, ROWS),
        back,
    )


def solution(mesh):
    return jax.shard_map(
        shards,
        mesh=mesh,
        in_specs=(
            P(("inner", "outer"), None),
            P(("inner", "outer"), None),
            P(("inner", "outer")),
            P(),
        ),
        out_specs=P(("inner", "outer"), None),
        check_vma=False,
    )
```

```python
import functools

import jax
import jax.numpy as jnp
from jax import lax
from jax.experimental import pallas as pl
from jax.experimental.pallas import tpu as pltpu
from jax.sharding import PartitionSpec as P

HEADS = 8
HD = 64
SPAN = 96
ROWS = HEADS * SPAN
GROUP = 8
CHUNK = GROUP * SPAN
MSG = 208
QMSG = 144
PART = 160
LOG2E = 1.4426950408889634
SCALE = HD**-0.5 * LOG2E
LIMIT = 1e36
F32 = jnp.float32
BF16 = jnp.bfloat16
VMEM = pl.BlockSpec(memory_space=pltpu.VMEM)
HBM = pl.BlockSpec(memory_space=pltpu.HBM)
PARAMS = pltpu.CompilerParams(vmem_limit_bytes=20 << 20)


def dot(a, b):
    return jnp.dot(a, b, preferred_element_type=F32)


def load(pairs, sems):
    copies = [
        pltpu.make_async_copy(source, target, sems.at[n]) for n, (source, target) in enumerate(pairs)
    ]
    for copy in copies:
        copy.start()
    for copy in copies:
        copy.wait()


def order(pos_ref, ref):
    run = pos_ref[0] // SPAN
    swapped = run >= 128
    first, second = ref[0:SPAN, :], ref[SPAN : 2 * SPAN, :]
    lower = jnp.where(swapped, 255 - run, run).astype(F32)
    return swapped, lower, jnp.where(swapped, second, first), jnp.where(swapped, first, second)


def prepare_keys(pos_hbm, kv_hbm, km_ref, pos_ref, kv_ref, sems):
    load(((pos_hbm, pos_ref), (kv_hbm, kv_ref)), sems)
    _, lower, lo, up = order(pos_ref, kv_ref)
    km_ref[0, 0:SPAN, :] = jnp.concatenate([lo[:, :HD], up[:, :HD]], axis=1)
    km_ref[0, SPAN : 2 * SPAN, :] = jnp.concatenate([lo[:, HD:], up[:, HD:]], axis=1)
    km_ref[0, 2 * SPAN :, :] = jnp.full((MSG - 2 * SPAN, 128), lower, F32).astype(BF16)


def prepare_queries(pos_hbm, q_hbm, qm_ref, flag_ref, pos_ref, q_ref, sems):
    load(((pos_hbm, pos_ref), (q_hbm, q_ref)), sems)
    swapped, lower, lo, up = order(pos_ref, q_ref)
    stacked = jnp.concatenate(
        [
            jnp.concatenate([lo[:, h * HD : (h + 1) * HD], up[:, h * HD : (h + 1) * HD]], axis=1)
            for h in range(HEADS)
        ],
        axis=0,
    )
    qm_ref[0:128, :] = jnp.transpose(stacked)
    qm_ref[128:, :] = jnp.full((QMSG - 128, ROWS), lower, F32).astype(BF16)
    flag_ref[...] = jnp.full((8, ROWS), jnp.where(swapped, 1.0, 0.0), F32)


def diagonal(qm_ref, km_ref, flag_ref, out_ref):
    out_ref[PART:, :] = flag_ref[...]
    keys = lax.broadcasted_iota(jnp.int32, (SPAN, ROWS), 0)
    rows = lax.broadcasted_iota(jnp.int32, (SPAN, ROWS), 1)
    mine = rows
    for h in range(1, HEADS):
        mine = jnp.where(rows >= h * SPAN, rows - h * SPAN, mine)
    visible = keys <= mine
    k = km_ref[0, 0:SPAN, :]
    v = jnp.transpose(km_ref[0, SPAN : 2 * SPAN, :].astype(F32)).astype(BF16)
    for half in range(2):
        part = slice(half * HD, (half + 1) * HD)
        s = dot(k[:, part], qm_ref[part, :]) * SCALE
        s = jnp.where(visible, s, -1e30)
        shift = jnp.maximum(jnp.max(s, axis=0, keepdims=True), 0.0)
        p = jnp.where(visible, jnp.exp2(s - shift), 0.0)
        out_ref[part, :] = dot(v[part, :], p.astype(BF16))
        total = jnp.sum(p, axis=0, keepdims=True)
        out_ref[128 + 8 * half : 136 + 8 * half, :] = jnp.broadcast_to(total, (8, ROWS))
        out_ref[144 + 8 * half : 152 + 8 * half, :] = jnp.broadcast_to(shift, (8, ROWS))


def chunk_masks(keys, q_ref):
    info = keys[:, 2 * SPAN : 2 * SPAN + 16, :].astype(F32)[:, 0:1, :]
    own = q_ref[128:144, 0:128].astype(F32)[0:1, :]
    below = jnp.where(info < own[None], 1.0, 0.0)
    above = jnp.where(info > own[None], 1.0, 0.0)
    return below, above


def along_lanes(mask):
    lanes = lax.broadcasted_iota(jnp.int32, (16, CHUNK), 1)
    wide = [
        jnp.concatenate([jnp.broadcast_to(mask[b], (16, 128))] * (CHUNK // 128), axis=1)
        for b in range(GROUP)
    ]
    out = wide[0]
    for b in range(1, GROUP):
        out = jnp.where(lanes >= b * SPAN, wide[b], out)
    return out


def transposed_values(keys):
    return jnp.transpose(keys[:, SPAN : 2 * SPAN, :].reshape(CHUNK, 128))


def chunk_operands(keys, q_ref, vt):
    below, above = chunk_masks(keys, q_ref)
    k = keys[:, 0:SPAN, :]
    lanes = lax.broadcasted_iota(jnp.int32, (GROUP, 1, 128), 2)
    keep = jnp.where(lanes < HD, below, above).astype(BF16)
    chosen = (k * keep).reshape(CHUNK, 128)
    low, high = along_lanes(below), along_lanes(above)
    rows = lax.broadcasted_iota(jnp.int32, (16, CHUNK), 0)
    ones = jnp.where(rows < 8, low, high).astype(BF16)
    low, high = low[0:1].astype(BF16), high[0:1].astype(BF16)
    values = jnp.concatenate([vt[:HD] * low, vt[HD:] * high, ones], axis=0)
    return k.reshape(CHUNK, 128), chosen, values


def each(count, body):
    if count == 1:
        body(0)
    else:
        pl.loop(0, count)(body)


def attend(nq, nc, at, packed, *refs):
    q_refs, refs = refs[:nq], refs[nq:]
    key_refs, refs = refs[:nc], refs[nc:]
    if at is not None:
        old_ref, refs = refs[0], refs[1:]
    out_ref, refs = refs[0], refs[1:]
    sums = refs[0] if packed else out_ref
    queries, keys = refs[-2], refs[-1]
    for q in range(nq):
        queries[q] = q_refs[q][...]
        sums[q] = jnp.zeros((PART, ROWS), F32) if at is None else old_ref[at + q]
    for c in range(nc):
        keys[c] = key_refs[c][...]

    def add(c):
        chunk = keys[c]
        vt = transposed_values(chunk)
        first = jnp.concatenate([vt[:HD], jnp.ones((16, CHUNK), BF16)], axis=0)

        def one(q):
            q_ref = queries.at[q]
            k, chosen, values = chunk_operands(chunk, q_ref, vt)
            a = dot(k[:, :HD], q_ref[HD:128, :])
            b = dot(chosen, q_ref[0:128, :])
            pa = jnp.exp2(a * SCALE).astype(BF16)
            pb = jnp.exp2(b * SCALE).astype(BF16)
            oa = dot(first, pa)
            ob = dot(values, pb)
            sums[q, 0:HD, :] += ob[:HD]
            sums[q, HD:128, :] += oa[:HD] + ob[HD:128]
            sums[q, 128:136, :] += ob[128:136]
            sums[q, 136:144, :] += oa[HD : HD + 8] + ob[136:144]

        each(nq, one)

    each(nc, add)

    def check(q):
        bad = jnp.sum(jnp.where(sums[q, 128:144, :] < LIMIT, 0.0, 1.0))
        bad = bad + jnp.sum(sums[q, 144:160, :])

        @pl.when(bad > 0.0)
        def _():
            for k in range(nq):

                @pl.when(q == k)
                def _():
                    sums[k] = jnp.zeros((PART, ROWS), F32) if at is None else old_ref[at + k]

            @pl.loop(0, nc)
            def _(c):
                careful(keys.at[c], queries.at[q], sums.at[q])

    each(nq, check)

    if packed:
        for q in range(nq):
            out_ref[0:128, :] = sums[q, 0:128, :].astype(BF16)
            rows = lax.broadcasted_iota(jnp.int32, (16, ROWS), 0)
            stats = jnp.zeros((16, ROWS), F32)
            for row, start in ((0, 128), (2, 136)):
                total = jnp.broadcast_to(sums[q, start : start + 1, :], (16, ROWS))
                high = total.astype(BF16).astype(F32)
                stats = jnp.where(rows == row, high, stats)
                stats = jnp.where(rows == row + 1, total - high, stats)
            for row, start in ((4, 144), (5, 152)):
                shift = jnp.broadcast_to(sums[q, start : start + 1, :], (16, ROWS))
                stats = jnp.where(rows == row, shift, stats)
            out_ref[128:144, :] = stats.astype(BF16)


def careful(keys, q_ref, out_ref):
    def raise_shift(half, top):
        old = out_ref[144 + 8 * half : 145 + 8 * half, :]
        new = jnp.maximum(old, jnp.maximum(top, 0.0).astype(BF16).astype(F32))
        factor = jnp.exp2(old - new)
        out_ref[half * HD : (half + 1) * HD, :] *= factor
        out_ref[128 + 8 * half : 136 + 8 * half, :] *= factor
        out_ref[144 + 8 * half : 152 + 8 * half, :] = jnp.broadcast_to(new, (8, ROWS))
        return new

    def add(half, values, p):
        p = p.astype(BF16)
        out_ref[half * HD : (half + 1) * HD, :] += dot(values, p)
        out_ref[128 + 8 * half : 136 + 8 * half, :] += dot(jnp.ones((16, SPAN), BF16), p)[:8]

    def wide(row):
        return jnp.concatenate([row] * (ROWS // 128), axis=1)

    own = wide(q_ref[128:144, 0:128].astype(F32)[0:1, :])

    @pl.loop(0, GROUP)
    def _(b):
        k = keys[b, 0:SPAN, :]
        vt = jnp.transpose(keys[b, SPAN : 2 * SPAN, :].astype(F32)).astype(BF16)
        info = wide(keys[b, 2 * SPAN : 2 * SPAN + 16, :].astype(F32)[0:1, :])
        low = dot(k[:, :HD], q_ref[HD:128, :]) * SCALE
        shift = raise_shift(1, jnp.max(low, axis=0, keepdims=True))
        add(1, vt[:HD], jnp.exp2(low - shift))
        for half, seen in ((0, info < own), (1, info > own)):
            part = slice(half * HD, (half + 1) * HD)
            s = dot(k[:, part], q_ref[part, :]) * SCALE
            top = jnp.where(seen, jnp.max(s, axis=0, keepdims=True), -1e30)
            shift = raise_shift(half, top)
            add(half, vt[part], jnp.where(seen, jnp.exp2(s - shift), 0.0))


def finish(sink_ref, diag_ref, own_ref, message_any, out_ref, message, sem):
    copy = pltpu.make_async_copy(message_any, message, sem)
    copy.start()
    swapped = jnp.broadcast_to(diag_ref[PART : PART + 1, 0:128], (SPAN, 128)) > 0.5
    held = []
    for half in range(2):
        part = slice(half * HD, (half + 1) * HD)
        stat = 128 + 8 * half
        shifts = [p[stat + 16 : stat + 17, :] for p in (diag_ref, own_ref)]
        top = jnp.maximum(*shifts)
        total = jnp.exp2(sink_ref[0:1, :] * LOG2E - top)
        sums = jnp.zeros((HD, ROWS), F32)
        for p, shift in zip((diag_ref, own_ref), shifts):
            factor = jnp.exp2(shift - top)
            total = total + p[stat : stat + 1, :] * factor
            sums = sums + p[part, :] * factor
        held.append((top, total, sums))
    copy.wait()
    stats = message[128:144, :].astype(F32)
    results = []
    for half, (top, total, sums) in enumerate(held):
        shift = stats[4 + half : 5 + half]
        new = jnp.maximum(top, shift)
        kept, added = jnp.exp2(top - new), jnp.exp2(shift - new)
        more = stats[2 * half : 2 * half + 1] + stats[2 * half + 1 : 2 * half + 2]
        scale = 1.0 / (total * kept + more * added)
        sent = message[half * HD : (half + 1) * HD, :].astype(F32)
        results.append(sums * (kept * scale) + sent * (added * scale))
    both = jnp.transpose(jnp.concatenate(results, axis=0))
    for g in range(HEADS // 2):
        even, odd = both[2 * g * SPAN : (2 * g + 1) * SPAN], both[(2 * g + 1) * SPAN : (2 * g + 2) * SPAN]
        lo = jnp.concatenate([even[:, :HD], odd[:, :HD]], axis=1)
        up = jnp.concatenate([even[:, HD:], odd[:, HD:]], axis=1)
        lanes = slice(128 * g, 128 * (g + 1))
        out_ref[0:SPAN, lanes] = jnp.where(swapped, up, lo).astype(BF16)
        out_ref[SPAN : 2 * SPAN, lanes] = jnp.where(swapped, lo, up).astype(BF16)


def partials(queries, chunks, old=None, at=None, packed=False):
    nq, nc = len(queries), len(chunks)
    pairs = nq * nc * 2 * CHUNK * ROWS
    operands = [*queries, *chunks, *([] if at is None else [old])]
    sums = (nq, PART, ROWS)
    shape = jax.ShapeDtypeStruct(sums, F32)
    if packed:
        shape = jax.ShapeDtypeStruct((QMSG, ROWS), BF16)
    return pl.pallas_call(
        functools.partial(attend, nq, nc, at, packed),
        out_shape=shape,
        in_specs=[VMEM] * len(operands),
        out_specs=VMEM,
        scratch_shapes=([pltpu.VMEM(sums, F32)] if packed else [])
        + [pltpu.VMEM((nq, QMSG, ROWS), BF16), pltpu.VMEM((nc, GROUP, MSG, 128), BF16)],
        compiler_params=PARAMS,
        cost_estimate=pl.CostEstimate(
            flops=pairs * 16, bytes_accessed=nc * 2**14, transcendentals=0
        ),
        name="attend",
    )(*operands)


def simple(kernel, shape, name, *operands):
    return pl.pallas_call(
        kernel,
        out_shape=shape,
        in_specs=[VMEM] * len(operands),
        out_specs=VMEM,
        compiler_params=PARAMS,
        name=name,
    )(*operands)


def place(index):
    inner, outer = divmod(index, 16)
    return inner % 4, inner // 4 * 2 + outer // 2 % 2, outer // 4, outer % 2


def index_of(x, y, z, core):
    return (y // 2 * 4 + x) * 16 + z * 4 + y % 2 * 2 + core


def permute(array, target):
    pairs = []
    for source in range(128):
        x, y, z, core = place(source)
        x, y, z, core = target(x, y, z, core)
        pairs.append((source, index_of(x % 4, y % 4, z % 4, core % 2)))
    return lax.ppermute(array, ("inner", "outer"), pairs)


def along_first(array, d):
    return permute(array, lambda x, y, z, c: (x, y, z + d, c) if c else (x + d, y, z, c))


def along_second(array, d):
    return permute(array, lambda x, y, z, c: (x + d, y, z, c) if c else (x, y, z + d, c))


def y_neighbour(array):
    return permute(array, lambda x, y, z, c: (x, y ^ 1, z, c))


def y_opposite(array):
    return permute(array, lambda x, y, z, c: (x, y + 2, z, c))


def other_core(array):
    return permute(array, lambda x, y, z, c: (x, y, z, c + 1))


def after(array, *others):
    return lax.optimization_barrier((array, *others))[0]


def prepared(kernel, name, positions, rows, *shapes):
    return pl.pallas_call(
        kernel,
        out_shape=shapes,
        in_specs=[HBM, HBM],
        out_specs=(VMEM,) * len(shapes),
        scratch_shapes=[
            pltpu.SMEM(positions.shape, jnp.int32),
            pltpu.VMEM(rows.shape, BF16),
            pltpu.SemaphoreType.DMA((2,)),
        ],
        compiler_params=pltpu.CompilerParams(vmem_limit_bytes=63 << 20),
        name=name,
    )(positions, rows)


def shards(queries, key_value, positions, sinks):
    (km,) = prepared(
        prepare_keys,
        "prepare_keys",
        positions,
        key_value,
        jax.ShapeDtypeStruct((1, MSG, 128), BF16),
    )
    qm, flag = prepared(
        prepare_queries,
        "prepare_queries",
        positions,
        after(queries, km),
        jax.ShapeDtypeStruct((QMSG, ROWS), BF16),
        jax.ShapeDtypeStruct((8, ROWS), F32),
    )
    pair = jnp.concatenate([after(km, qm), y_neighbour(km)], axis=0)
    asked = y_opposite(qm)
    far, right, left = [along_first(pair, d) for d in (2, 1, -1)]
    near = jnp.concatenate([after(pair, asked), far, right, left], axis=0)
    side3, side1, side2 = [along_second(near, d) for d in (2, 1, -1)]
    own = partials([qm], [near])
    near2 = other_core(near)
    mate = partials([after(asked, own)], [near])
    diag = simple(
        diagonal, jax.ShapeDtypeStruct((PART + 8, ROWS), F32), "diagonal", after(qm, mate), km, flag
    )
    mate = partials([after(asked, diag)], [near2], mate, 0)
    own = partials([after(qm, mate)], [near2], own, 0)
    mate = partials([after(asked, own)], [side1], mate, 0)
    mate = partials([asked], [side2], mate, 0)
    swap1, swap2, swap3 = [other_core(after(side, mate)) for side in (side1, side2, side3)]
    mate = partials([asked], [side3], mate, 0)
    sent = partials([asked], [swap1, swap2, swap3], mate, 0, packed=True)
    back = y_opposite(sent)
    own = partials([after(qm, sent)], [swap3, swap2], own, 0)
    own = partials([qm], [swap1, side3], own, 0)
    own = partials([qm], [side2, side1], own, 0)
    sink_row = jnp.broadcast_to(jnp.repeat(sinks, SPAN)[None], (8, ROWS))
    return pl.pallas_call(
        finish,
        out_shape=jax.ShapeDtypeStruct(queries.shape, BF16),
        in_specs=[VMEM] * 3 + [HBM],
        out_specs=VMEM,
        scratch_shapes=[pltpu.VMEM((QMSG, ROWS), BF16), pltpu.SemaphoreType.DMA],
        compiler_params=PARAMS,
        name="finish",
    )(sink_row, diag, own.reshape(PART, ROWS), back)


def solution(mesh):
    return jax.shard_map(
        shards,
        mesh=mesh,
        in_specs=(
            P(("inner", "outer"), None),
            P(("inner", "outer"), None),
            P(("inner", "outer")),
            P(),
        ),
        out_specs=P(("inner", "outer"), None),
        check_vma=False,
    )
```

```python
import functools

import jax
import jax.numpy as jnp
from jax import lax
from jax.experimental import pallas as pl
from jax.experimental.pallas import tpu as pltpu
from jax.sharding import PartitionSpec as P

HEADS = 8
HD = 64
SPAN = 96
ROWS = HEADS * SPAN
GROUP = 8
CHUNK = GROUP * SPAN
MSG = 208
QMSG = 144
PART = 160
LOG2E = 1.4426950408889634
SCALE = HD**-0.5 * LOG2E
LIMIT = 1e36
F32 = jnp.float32
BF16 = jnp.bfloat16
VMEM = pl.BlockSpec(memory_space=pltpu.VMEM)
HBM = pl.BlockSpec(memory_space=pltpu.HBM)
PARAMS = pltpu.CompilerParams(vmem_limit_bytes=20 << 20)


def dot(a, b):
    return jnp.dot(a, b, preferred_element_type=F32)


def load(pairs, sems):
    copies = [
        pltpu.make_async_copy(source, target, sems.at[n]) for n, (source, target) in enumerate(pairs)
    ]
    for copy in copies:
        copy.start()
    for copy in copies:
        copy.wait()


def order(pos_ref, ref):
    run = pos_ref[0] // SPAN
    swapped = run >= 128
    first, second = ref[0:SPAN, :], ref[SPAN : 2 * SPAN, :]
    lower = jnp.where(swapped, 255 - run, run).astype(F32)
    return swapped, lower, jnp.where(swapped, second, first), jnp.where(swapped, first, second)


def prepare_keys(pos_hbm, kv_hbm, km_ref, pos_ref, kv_ref, sems):
    load(((pos_hbm, pos_ref), (kv_hbm, kv_ref)), sems)
    _, lower, lo, up = order(pos_ref, kv_ref)
    km_ref[0, 0:SPAN, :] = jnp.concatenate([lo[:, :HD], up[:, :HD]], axis=1)
    km_ref[0, SPAN : 2 * SPAN, :] = jnp.concatenate([lo[:, HD:], up[:, HD:]], axis=1)
    km_ref[0, 2 * SPAN :, :] = jnp.full((MSG - 2 * SPAN, 128), lower, F32).astype(BF16)


def prepare_queries(pos_hbm, q_hbm, sink_hbm, qm_ref, flag_ref, pos_ref, q_ref, sink_ref, sems):
    load(((pos_hbm, pos_ref), (q_hbm, q_ref), (sink_hbm, sink_ref)), sems)
    swapped, lower, lo, up = order(pos_ref, q_ref)
    stacked = jnp.concatenate(
        [
            jnp.concatenate([lo[:, h * HD : (h + 1) * HD], up[:, h * HD : (h + 1) * HD]], axis=1)
            for h in range(HEADS)
        ],
        axis=0,
    )
    qm_ref[0:128, :] = jnp.transpose(stacked)
    qm_ref[128:, :] = jnp.full((QMSG - 128, ROWS), lower, F32).astype(BF16)
    flag_ref[0:8, :] = jnp.full((8, ROWS), jnp.where(swapped, 1.0, 0.0), F32)
    lanes = lax.broadcasted_iota(jnp.int32, (8, ROWS), 1)
    sinks = jnp.full((8, ROWS), sink_ref[0], F32)
    for h in range(1, HEADS):
        sinks = jnp.where(lanes >= h * SPAN, sink_ref[h], sinks)
    flag_ref[8:16, :] = sinks


def diagonal(qm_ref, km_ref, flag_ref, out_ref):
    out_ref[PART:, :] = flag_ref[...]
    keys = lax.broadcasted_iota(jnp.int32, (SPAN, ROWS), 0)
    rows = lax.broadcasted_iota(jnp.int32, (SPAN, ROWS), 1)
    mine = rows
    for h in range(1, HEADS):
        mine = jnp.where(rows >= h * SPAN, rows - h * SPAN, mine)
    visible = keys <= mine
    k = km_ref[0, 0:SPAN, :]
    v = jnp.transpose(km_ref[0, SPAN : 2 * SPAN, :].astype(F32)).astype(BF16)
    for half in range(2):
        part = slice(half * HD, (half + 1) * HD)
        s = dot(k[:, part], qm_ref[part, :]) * SCALE
        s = jnp.where(visible, s, -1e30)
        shift = jnp.maximum(jnp.max(s, axis=0, keepdims=True), 0.0)
        p = jnp.where(visible, jnp.exp2(s - shift), 0.0)
        out_ref[part, :] = dot(v[part, :], p.astype(BF16))
        total = jnp.sum(p, axis=0, keepdims=True)
        out_ref[128 + 8 * half : 136 + 8 * half, :] = jnp.broadcast_to(total, (8, ROWS))
        out_ref[144 + 8 * half : 152 + 8 * half, :] = jnp.broadcast_to(shift, (8, ROWS))


def chunk_masks(keys, q_ref):
    info = keys[:, 2 * SPAN : 2 * SPAN + 16, :].astype(F32)[:, 0:1, :]
    own = q_ref[128:144, 0:128].astype(F32)[0:1, :]
    below = jnp.where(info < own[None], 1.0, 0.0)
    above = jnp.where(info > own[None], 1.0, 0.0)
    return below, above


def along_lanes(mask):
    lanes = lax.broadcasted_iota(jnp.int32, (16, CHUNK), 1)
    wide = [
        jnp.concatenate([jnp.broadcast_to(mask[b], (16, 128))] * (CHUNK // 128), axis=1)
        for b in range(GROUP)
    ]
    out = wide[0]
    for b in range(1, GROUP):
        out = jnp.where(lanes >= b * SPAN, wide[b], out)
    return out


def transposed_values(keys):
    return jnp.transpose(keys[:, SPAN : 2 * SPAN, :].reshape(CHUNK, 128))


def chunk_operands(keys, q_ref, vt):
    below, above = chunk_masks(keys, q_ref)
    k = keys[:, 0:SPAN, :]
    lanes = lax.broadcasted_iota(jnp.int32, (GROUP, 1, 128), 2)
    keep = jnp.where(lanes < HD, below, above).astype(BF16)
    chosen = (k * keep).reshape(CHUNK, 128)
    low, high = along_lanes(below), along_lanes(above)
    rows = lax.broadcasted_iota(jnp.int32, (16, CHUNK), 0)
    ones = jnp.where(rows < 8, low, high).astype(BF16)
    low, high = low[0:1].astype(BF16), high[0:1].astype(BF16)
    values = jnp.concatenate([vt[:HD] * low, vt[HD:] * high, ones], axis=0)
    return k.reshape(CHUNK, 128), chosen, values


def each(count, body):
    if count == 1:
        body(0)
    else:
        pl.loop(0, count)(body)


def attend(nq, nc, at, packed, *refs):
    q_refs, refs = refs[:nq], refs[nq:]
    key_refs, refs = refs[:nc], refs[nc:]
    if at is not None:
        old_ref, refs = refs[0], refs[1:]
    out_ref, refs = refs[0], refs[1:]
    sums = refs[0] if packed else out_ref
    queries, keys = refs[-2], refs[-1]
    for q in range(nq):
        queries[q] = q_refs[q][...]
        sums[q] = jnp.zeros((PART, ROWS), F32) if at is None else old_ref[at + q]
    for c in range(nc):
        keys[c] = key_refs[c][...]

    def add(c):
        chunk = keys[c]
        vt = transposed_values(chunk)
        first = jnp.concatenate([vt[:HD], jnp.ones((16, CHUNK), BF16)], axis=0)

        def one(q):
            q_ref = queries.at[q]
            k, chosen, values = chunk_operands(chunk, q_ref, vt)
            a = dot(k[:, :HD], q_ref[HD:128, :])
            b = dot(chosen, q_ref[0:128, :])
            pa = jnp.exp2(a * SCALE).astype(BF16)
            pb = jnp.exp2(b * SCALE).astype(BF16)
            oa = dot(first, pa)
            ob = dot(values, pb)
            sums[q, 0:HD, :] += ob[:HD]
            sums[q, HD:128, :] += oa[:HD] + ob[HD:128]
            sums[q, 128:136, :] += ob[128:136]
            sums[q, 136:144, :] += oa[HD : HD + 8] + ob[136:144]

        each(nq, one)

    each(nc, add)

    def check(q):
        bad = jnp.sum(jnp.where(sums[q, 128:144, :] < LIMIT, 0.0, 1.0))
        bad = bad + jnp.sum(sums[q, 144:160, :])

        @pl.when(bad > 0.0)
        def _():
            for k in range(nq):

                @pl.when(q == k)
                def _():
                    sums[k] = jnp.zeros((PART, ROWS), F32) if at is None else old_ref[at + k]

            @pl.loop(0, nc)
            def _(c):
                careful(keys.at[c], queries.at[q], sums.at[q])

    each(nq, check)

    if packed:
        for q in range(nq):
            out_ref[0:128, :] = sums[q, 0:128, :].astype(BF16)
            rows = lax.broadcasted_iota(jnp.int32, (16, ROWS), 0)
            stats = jnp.zeros((16, ROWS), F32)
            for row, start in ((0, 128), (2, 136)):
                total = jnp.broadcast_to(sums[q, start : start + 1, :], (16, ROWS))
                high = total.astype(BF16).astype(F32)
                stats = jnp.where(rows == row, high, stats)
                stats = jnp.where(rows == row + 1, total - high, stats)
            for row, start in ((4, 144), (5, 152)):
                shift = jnp.broadcast_to(sums[q, start : start + 1, :], (16, ROWS))
                stats = jnp.where(rows == row, shift, stats)
            out_ref[128:144, :] = stats.astype(BF16)


def careful(keys, q_ref, out_ref):
    def raise_shift(half, top):
        old = out_ref[144 + 8 * half : 145 + 8 * half, :]
        new = jnp.maximum(old, jnp.maximum(top, 0.0).astype(BF16).astype(F32))
        factor = jnp.exp2(old - new)
        out_ref[half * HD : (half + 1) * HD, :] *= factor
        out_ref[128 + 8 * half : 136 + 8 * half, :] *= factor
        out_ref[144 + 8 * half : 152 + 8 * half, :] = jnp.broadcast_to(new, (8, ROWS))
        return new

    def add(half, values, p):
        p = p.astype(BF16)
        out_ref[half * HD : (half + 1) * HD, :] += dot(values, p)
        out_ref[128 + 8 * half : 136 + 8 * half, :] += dot(jnp.ones((16, SPAN), BF16), p)[:8]

    def wide(row):
        return jnp.concatenate([row] * (ROWS // 128), axis=1)

    own = wide(q_ref[128:144, 0:128].astype(F32)[0:1, :])

    @pl.loop(0, GROUP)
    def _(b):
        k = keys[b, 0:SPAN, :]
        vt = jnp.transpose(keys[b, SPAN : 2 * SPAN, :].astype(F32)).astype(BF16)
        info = wide(keys[b, 2 * SPAN : 2 * SPAN + 16, :].astype(F32)[0:1, :])
        low = dot(k[:, :HD], q_ref[HD:128, :]) * SCALE
        shift = raise_shift(1, jnp.max(low, axis=0, keepdims=True))
        add(1, vt[:HD], jnp.exp2(low - shift))
        for half, seen in ((0, info < own), (1, info > own)):
            part = slice(half * HD, (half + 1) * HD)
            s = dot(k[:, part], q_ref[part, :]) * SCALE
            top = jnp.where(seen, jnp.max(s, axis=0, keepdims=True), -1e30)
            shift = raise_shift(half, top)
            add(half, vt[part], jnp.where(seen, jnp.exp2(s - shift), 0.0))


def finish(diag_ref, own_ref, message, out_ref):
    swapped = jnp.broadcast_to(diag_ref[PART : PART + 1, 0:128], (SPAN, 128)) > 0.5
    held = []
    for half in range(2):
        part = slice(half * HD, (half + 1) * HD)
        stat = 128 + 8 * half
        shifts = [p[stat + 16 : stat + 17, :] for p in (diag_ref, own_ref)]
        top = jnp.maximum(*shifts)
        total = jnp.exp2(diag_ref[PART + 8 : PART + 9, :] * LOG2E - top)
        sums = jnp.zeros((HD, ROWS), F32)
        for p, shift in zip((diag_ref, own_ref), shifts):
            factor = jnp.exp2(shift - top)
            total = total + p[stat : stat + 1, :] * factor
            sums = sums + p[part, :] * factor
        held.append((top, total, sums))
    stats = message[128:144, :].astype(F32)
    results = []
    for half, (top, total, sums) in enumerate(held):
        shift = stats[4 + half : 5 + half]
        new = jnp.maximum(top, shift)
        kept, added = jnp.exp2(top - new), jnp.exp2(shift - new)
        more = stats[2 * half : 2 * half + 1] + stats[2 * half + 1 : 2 * half + 2]
        scale = 1.0 / (total * kept + more * added)
        sent = message[half * HD : (half + 1) * HD, :].astype(F32)
        results.append(sums * (kept * scale) + sent * (added * scale))
    both = jnp.transpose(jnp.concatenate(results, axis=0))
    for g in range(HEADS // 2):
        even, odd = both[2 * g * SPAN : (2 * g + 1) * SPAN], both[(2 * g + 1) * SPAN : (2 * g + 2) * SPAN]
        lo = jnp.concatenate([even[:, :HD], odd[:, :HD]], axis=1)
        up = jnp.concatenate([even[:, HD:], odd[:, HD:]], axis=1)
        lanes = slice(128 * g, 128 * (g + 1))
        out_ref[0:SPAN, lanes] = jnp.where(swapped, up, lo).astype(BF16)
        out_ref[SPAN : 2 * SPAN, lanes] = jnp.where(swapped, lo, up).astype(BF16)


def partials(queries, chunks, old=None, at=None, packed=False):
    nq, nc = len(queries), len(chunks)
    pairs = nq * nc * 2 * CHUNK * ROWS
    operands = [*queries, *chunks, *([] if at is None else [old])]
    sums = (nq, PART, ROWS)
    shape = jax.ShapeDtypeStruct(sums, F32)
    if packed:
        shape = jax.ShapeDtypeStruct((QMSG, ROWS), BF16)
    return pl.pallas_call(
        functools.partial(attend, nq, nc, at, packed),
        out_shape=shape,
        in_specs=[VMEM] * len(operands),
        out_specs=VMEM,
        scratch_shapes=([pltpu.VMEM(sums, F32)] if packed else [])
        + [pltpu.VMEM((nq, QMSG, ROWS), BF16), pltpu.VMEM((nc, GROUP, MSG, 128), BF16)],
        compiler_params=PARAMS,
        cost_estimate=pl.CostEstimate(
            flops=pairs * 16, bytes_accessed=nc * 2**14, transcendentals=0
        ),
        name="attend",
    )(*operands)


def simple(kernel, shape, name, *operands):
    return pl.pallas_call(
        kernel,
        out_shape=shape,
        in_specs=[VMEM] * len(operands),
        out_specs=VMEM,
        compiler_params=PARAMS,
        name=name,
    )(*operands)


def place(index):
    inner, outer = divmod(index, 16)
    return inner % 4, inner // 4 * 2 + outer // 2 % 2, outer // 4, outer % 2


def index_of(x, y, z, core):
    return (y // 2 * 4 + x) * 16 + z * 4 + y % 2 * 2 + core


def permute(array, target):
    pairs = []
    for source in range(128):
        x, y, z, core = place(source)
        x, y, z, core = target(x, y, z, core)
        pairs.append((source, index_of(x % 4, y % 4, z % 4, core % 2)))
    return lax.ppermute(array, ("inner", "outer"), pairs)


def along_first(array, d):
    return permute(array, lambda x, y, z, c: (x, y, z + d, c) if c else (x + d, y, z, c))


def along_second(array, d):
    return permute(array, lambda x, y, z, c: (x + d, y, z, c) if c else (x, y, z + d, c))


def y_neighbour(array):
    return permute(array, lambda x, y, z, c: (x, y ^ 1, z, c))


def y_opposite(array):
    return permute(array, lambda x, y, z, c: (x, y + 2, z, c))


def other_core(array):
    return permute(array, lambda x, y, z, c: (x, y, z, c + 1))


def after(array, *others):
    return lax.optimization_barrier((array, *others))[0]


def prepared(kernel, name, operands, scratch, *shapes):
    return pl.pallas_call(
        kernel,
        out_shape=shapes,
        in_specs=[HBM] * len(operands),
        out_specs=(VMEM,) * len(shapes),
        scratch_shapes=[*scratch, pltpu.SemaphoreType.DMA((len(operands),))],
        compiler_params=pltpu.CompilerParams(vmem_limit_bytes=63 << 20),
        name=name,
    )(*operands)


def shards(queries, key_value, positions, sinks):
    (km,) = prepared(
        prepare_keys,
        "prepare_keys",
        (positions, key_value),
        [pltpu.SMEM(positions.shape, jnp.int32), pltpu.VMEM(key_value.shape, BF16)],
        jax.ShapeDtypeStruct((1, MSG, 128), BF16),
    )
    qm, flag = prepared(
        prepare_queries,
        "prepare_queries",
        (positions, after(queries, km), sinks),
        [
            pltpu.SMEM(positions.shape, jnp.int32),
            pltpu.VMEM(queries.shape, BF16),
            pltpu.SMEM(sinks.shape, F32),
        ],
        jax.ShapeDtypeStruct((QMSG, ROWS), BF16),
        jax.ShapeDtypeStruct((16, ROWS), F32),
    )
    pair = jnp.concatenate([after(km, qm), y_neighbour(km)], axis=0)
    asked = y_opposite(qm)
    left, right, far = [along_first(pair, d) for d in (-1, 1, 2)]
    near = jnp.concatenate([after(pair, asked), left, right, far], axis=0)
    side3, side1, side2 = [along_second(near, d) for d in (2, 1, -1)]
    own = partials([qm], [near])
    near2 = other_core(near)
    mate = partials([after(asked, own)], [near])
    diag = simple(
        diagonal, jax.ShapeDtypeStruct((PART + 16, ROWS), F32), "diagonal", after(qm, mate), km, flag
    )
    mate = partials([after(asked, diag)], [near2], mate, 0)
    own = partials([after(qm, mate)], [near2], own, 0)
    mate = partials([after(asked, own)], [side1], mate, 0)
    own = partials([after(qm, mate)], [side1], own, 0)
    mate = partials([after(asked, own)], [side2], mate, 0)
    swap1, swap2, swap3 = [other_core(after(side, mate)) for side in (side1, side2, side3)]
    mate = partials([asked], [side3], mate, 0)
    sent = partials([asked], [swap1, swap2, swap3], mate, 0, packed=True)
    back = y_opposite(sent)
    own = partials([after(qm, sent)], [swap3, swap2], own, 0)
    own = partials([qm], [swap1, side3], own, 0)
    own = partials([qm], [side2], own, 0)
    return pl.pallas_call(
        finish,
        out_shape=jax.ShapeDtypeStruct(queries.shape, BF16),
        in_specs=[VMEM] * 3,
        out_specs=VMEM,
        compiler_params=PARAMS,
        name="finish",
    )(diag, own.reshape(PART, ROWS), back)


def solution(mesh):
    return jax.shard_map(
        shards,
        mesh=mesh,
        in_specs=(
            P(("inner", "outer"), None),
            P(("inner", "outer"), None),
            P(("inner", "outer")),
            P(),
        ),
        out_specs=P(("inner", "outer"), None),
        check_vma=False,
    )
```

```python
import functools

import jax
import jax.numpy as jnp
from jax import lax
from jax.experimental import pallas as pl
from jax.experimental.pallas import tpu as pltpu
from jax.sharding import PartitionSpec as P

HEADS = 8
HD = 64
SPAN = 96
ROWS = HEADS * SPAN
GROUP = 8
CHUNK = GROUP * SPAN
MSG = 208
QMSG = 144
PART = 160
LOG2E = 1.4426950408889634
SCALE = HD**-0.5 * LOG2E
LIMIT = 1e36
F32 = jnp.float32
BF16 = jnp.bfloat16
VMEM = pl.BlockSpec(memory_space=pltpu.VMEM)
HBM = pl.BlockSpec(memory_space=pltpu.HBM)
PARAMS = pltpu.CompilerParams(vmem_limit_bytes=20 << 20)


def dot(a, b):
    return jnp.dot(a, b, preferred_element_type=F32)


def load(pairs, sems):
    copies = [
        pltpu.make_async_copy(source, target, sems.at[n]) for n, (source, target) in enumerate(pairs)
    ]
    for copy in copies:
        copy.start()
    for copy in copies:
        copy.wait()


def order(pos_ref, ref):
    run = pos_ref[0] // SPAN
    swapped = run >= 128
    first, second = ref[0:SPAN, :], ref[SPAN : 2 * SPAN, :]
    lower = jnp.where(swapped, 255 - run, run).astype(F32)
    return swapped, lower, jnp.where(swapped, second, first), jnp.where(swapped, first, second)


def prepare_keys(pos_hbm, kv_hbm, km_ref, pos_ref, kv_ref, sems):
    load(((pos_hbm, pos_ref), (kv_hbm, kv_ref)), sems)
    _, lower, lo, up = order(pos_ref, kv_ref)
    km_ref[0, 0:SPAN, :] = jnp.concatenate([lo[:, :HD], up[:, :HD]], axis=1)
    km_ref[0, SPAN : 2 * SPAN, :] = jnp.concatenate([lo[:, HD:], up[:, HD:]], axis=1)
    km_ref[0, 2 * SPAN :, :] = jnp.full((MSG - 2 * SPAN, 128), lower, F32).astype(BF16)


def prepare_queries(pos_hbm, q_hbm, sink_hbm, qm_ref, flag_ref, pos_ref, q_ref, sink_ref, sems):
    load(((pos_hbm, pos_ref), (q_hbm, q_ref), (sink_hbm, sink_ref)), sems)
    swapped, lower, lo, up = order(pos_ref, q_ref)
    stacked = jnp.concatenate(
        [
            jnp.concatenate([lo[:, h * HD : (h + 1) * HD], up[:, h * HD : (h + 1) * HD]], axis=1)
            for h in range(HEADS)
        ],
        axis=0,
    )
    qm_ref[0:128, :] = jnp.transpose(stacked)
    qm_ref[128:, :] = jnp.full((QMSG - 128, ROWS), lower, F32).astype(BF16)
    flag_ref[0:8, :] = jnp.full((8, ROWS), jnp.where(swapped, 1.0, 0.0), F32)
    lanes = lax.broadcasted_iota(jnp.int32, (8, ROWS), 1)
    sinks = jnp.full((8, ROWS), sink_ref[0], F32)
    for h in range(1, HEADS):
        sinks = jnp.where(lanes >= h * SPAN, sink_ref[h], sinks)
    flag_ref[8:16, :] = sinks


def diagonal(qm_ref, km_ref, flag_ref, out_ref):
    out_ref[PART:, :] = flag_ref[...]
    keys = lax.broadcasted_iota(jnp.int32, (SPAN, ROWS), 0)
    rows = lax.broadcasted_iota(jnp.int32, (SPAN, ROWS), 1)
    mine = rows
    for h in range(1, HEADS):
        mine = jnp.where(rows >= h * SPAN, rows - h * SPAN, mine)
    visible = keys <= mine
    k = km_ref[0, 0:SPAN, :]
    v = jnp.transpose(km_ref[0, SPAN : 2 * SPAN, :].astype(F32)).astype(BF16)
    for half in range(2):
        part = slice(half * HD, (half + 1) * HD)
        s = dot(k[:, part], qm_ref[part, :]) * SCALE
        s = jnp.where(visible, s, -1e30)
        shift = jnp.maximum(jnp.max(s, axis=0, keepdims=True), 0.0)
        p = jnp.where(visible, jnp.exp2(s - shift), 0.0)
        out_ref[part, :] = dot(v[part, :], p.astype(BF16))
        total = jnp.sum(p, axis=0, keepdims=True)
        out_ref[128 + 8 * half : 136 + 8 * half, :] = jnp.broadcast_to(total, (8, ROWS))
        out_ref[144 + 8 * half : 152 + 8 * half, :] = jnp.broadcast_to(shift, (8, ROWS))


def chunk_masks(keys, q_ref):
    info = keys[:, 2 * SPAN : 2 * SPAN + 16, :].astype(F32)[:, 0:1, :]
    own = q_ref[128:144, 0:128].astype(F32)[0:1, :]
    below = jnp.where(info < own[None], 1.0, 0.0)
    above = jnp.where(info > own[None], 1.0, 0.0)
    return below, above


def along_lanes(mask):
    lanes = lax.broadcasted_iota(jnp.int32, (16, CHUNK), 1)
    wide = [
        jnp.concatenate([jnp.broadcast_to(mask[b], (16, 128))] * (CHUNK // 128), axis=1)
        for b in range(GROUP)
    ]
    out = wide[0]
    for b in range(1, GROUP):
        out = jnp.where(lanes >= b * SPAN, wide[b], out)
    return out


def transposed_values(keys):
    return jnp.transpose(keys[:, SPAN : 2 * SPAN, :].reshape(CHUNK, 128))


def chunk_operands(keys, q_ref, vt):
    below, above = chunk_masks(keys, q_ref)
    k = keys[:, 0:SPAN, :]
    lanes = lax.broadcasted_iota(jnp.int32, (GROUP, 1, 128), 2)
    keep = jnp.where(lanes < HD, below, above).astype(BF16)
    chosen = (k * keep).reshape(CHUNK, 128)
    low, high = along_lanes(below), along_lanes(above)
    rows = lax.broadcasted_iota(jnp.int32, (16, CHUNK), 0)
    ones = jnp.where(rows < 8, low, high).astype(BF16)
    low, high = low[0:1].astype(BF16), high[0:1].astype(BF16)
    values = jnp.concatenate([vt[:HD] * low, vt[HD:] * high, ones], axis=0)
    return k.reshape(CHUNK, 128), chosen, values


def each(count, body):
    if count == 1:
        body(0)
    else:
        pl.loop(0, count)(body)


def attend(nq, nc, at, packed, *refs):
    q_refs, refs = refs[:nq], refs[nq:]
    key_refs, refs = refs[:nc], refs[nc:]
    if at is not None:
        old_ref, refs = refs[0], refs[1:]
    out_ref, refs = refs[0], refs[1:]
    sums = refs[0] if packed else out_ref
    queries, keys = refs[-2], refs[-1]
    for q in range(nq):
        queries[q] = q_refs[q][...]
        sums[q] = jnp.zeros((PART, ROWS), F32) if at is None else old_ref[at + q]
    for c in range(nc):
        keys[c] = key_refs[c][...]

    def add(c):
        chunk = keys[c]
        vt = transposed_values(chunk)
        first = jnp.concatenate([vt[:HD], jnp.ones((16, CHUNK), BF16)], axis=0)

        def one(q):
            q_ref = queries.at[q]
            k, chosen, values = chunk_operands(chunk, q_ref, vt)
            a = dot(k[:, :HD], q_ref[HD:128, :])
            b = dot(chosen, q_ref[0:128, :])
            pa = jnp.exp2(a * SCALE).astype(BF16)
            pb = jnp.exp2(b * SCALE).astype(BF16)
            oa = dot(first, pa)
            ob = dot(values, pb)
            sums[q, 0:HD, :] += ob[:HD]
            sums[q, HD:128, :] += oa[:HD] + ob[HD:128]
            sums[q, 128:136, :] += ob[128:136]
            sums[q, 136:144, :] += oa[HD : HD + 8] + ob[136:144]

        each(nq, one)

    each(nc, add)

    def check(q):
        bad = jnp.sum(jnp.where(sums[q, 128:144, :] < LIMIT, 0.0, 1.0))
        bad = bad + jnp.sum(sums[q, 144:160, :])

        @pl.when(bad > 0.0)
        def _():
            for k in range(nq):

                @pl.when(q == k)
                def _():
                    sums[k] = jnp.zeros((PART, ROWS), F32) if at is None else old_ref[at + k]

            @pl.loop(0, nc)
            def _(c):
                careful(keys.at[c], queries.at[q], sums.at[q])

    each(nq, check)

    if packed:
        for q in range(nq):
            out_ref[0:128, :] = sums[q, 0:128, :].astype(BF16)
            rows = lax.broadcasted_iota(jnp.int32, (16, ROWS), 0)
            stats = jnp.zeros((16, ROWS), F32)
            for row, start in ((0, 128), (2, 136)):
                total = jnp.broadcast_to(sums[q, start : start + 1, :], (16, ROWS))
                high = total.astype(BF16).astype(F32)
                stats = jnp.where(rows == row, high, stats)
                stats = jnp.where(rows == row + 1, total - high, stats)
            for row, start in ((4, 144), (5, 152)):
                shift = jnp.broadcast_to(sums[q, start : start + 1, :], (16, ROWS))
                stats = jnp.where(rows == row, shift, stats)
            out_ref[128:144, :] = stats.astype(BF16)


def careful(keys, q_ref, out_ref):
    def raise_shift(half, top):
        old = out_ref[144 + 8 * half : 145 + 8 * half, :]
        new = jnp.maximum(old, jnp.maximum(top, 0.0).astype(BF16).astype(F32))
        factor = jnp.exp2(old - new)
        out_ref[half * HD : (half + 1) * HD, :] *= factor
        out_ref[128 + 8 * half : 136 + 8 * half, :] *= factor
        out_ref[144 + 8 * half : 152 + 8 * half, :] = jnp.broadcast_to(new, (8, ROWS))
        return new

    def add(half, values, p):
        p = p.astype(BF16)
        out_ref[half * HD : (half + 1) * HD, :] += dot(values, p)
        out_ref[128 + 8 * half : 136 + 8 * half, :] += dot(jnp.ones((16, SPAN), BF16), p)[:8]

    def wide(row):
        return jnp.concatenate([row] * (ROWS // 128), axis=1)

    own = wide(q_ref[128:144, 0:128].astype(F32)[0:1, :])

    @pl.loop(0, GROUP)
    def _(b):
        k = keys[b, 0:SPAN, :]
        vt = jnp.transpose(keys[b, SPAN : 2 * SPAN, :].astype(F32)).astype(BF16)
        info = wide(keys[b, 2 * SPAN : 2 * SPAN + 16, :].astype(F32)[0:1, :])
        low = dot(k[:, :HD], q_ref[HD:128, :]) * SCALE
        shift = raise_shift(1, jnp.max(low, axis=0, keepdims=True))
        add(1, vt[:HD], jnp.exp2(low - shift))
        for half, seen in ((0, info < own), (1, info > own)):
            part = slice(half * HD, (half + 1) * HD)
            s = dot(k[:, part], q_ref[part, :]) * SCALE
            top = jnp.where(seen, jnp.max(s, axis=0, keepdims=True), -1e30)
            shift = raise_shift(half, top)
            add(half, vt[part], jnp.where(seen, jnp.exp2(s - shift), 0.0))


def finish(diag_ref, own_ref, message, out_ref):
    swapped = jnp.broadcast_to(diag_ref[PART : PART + 1, 0:128], (SPAN, 128)) > 0.5
    held = []
    for half in range(2):
        part = slice(half * HD, (half + 1) * HD)
        stat = 128 + 8 * half
        shifts = [p[stat + 16 : stat + 17, :] for p in (diag_ref, own_ref)]
        top = jnp.maximum(*shifts)
        total = jnp.exp2(diag_ref[PART + 8 : PART + 9, :] * LOG2E - top)
        sums = jnp.zeros((HD, ROWS), F32)
        for p, shift in zip((diag_ref, own_ref), shifts):
            factor = jnp.exp2(shift - top)
            total = total + p[stat : stat + 1, :] * factor
            sums = sums + p[part, :] * factor
        held.append((top, total, sums))
    stats = message[128:144, :].astype(F32)
    results = []
    for half, (top, total, sums) in enumerate(held):
        shift = stats[4 + half : 5 + half]
        new = jnp.maximum(top, shift)
        kept, added = jnp.exp2(top - new), jnp.exp2(shift - new)
        more = stats[2 * half : 2 * half + 1] + stats[2 * half + 1 : 2 * half + 2]
        scale = 1.0 / (total * kept + more * added)
        sent = message[half * HD : (half + 1) * HD, :].astype(F32)
        results.append(sums * (kept * scale) + sent * (added * scale))
    both = jnp.transpose(jnp.concatenate(results, axis=0))
    for g in range(HEADS // 2):
        even, odd = both[2 * g * SPAN : (2 * g + 1) * SPAN], both[(2 * g + 1) * SPAN : (2 * g + 2) * SPAN]
        lo = jnp.concatenate([even[:, :HD], odd[:, :HD]], axis=1)
        up = jnp.concatenate([even[:, HD:], odd[:, HD:]], axis=1)
        lanes = slice(128 * g, 128 * (g + 1))
        out_ref[0:SPAN, lanes] = jnp.where(swapped, up, lo).astype(BF16)
        out_ref[SPAN : 2 * SPAN, lanes] = jnp.where(swapped, lo, up).astype(BF16)


def partials(queries, chunks, old=None, at=None, packed=False):
    nq, nc = len(queries), len(chunks)
    pairs = nq * nc * 2 * CHUNK * ROWS
    operands = [*queries, *chunks, *([] if at is None else [old])]
    sums = (nq, PART, ROWS)
    shape = jax.ShapeDtypeStruct(sums, F32)
    if packed:
        shape = jax.ShapeDtypeStruct((QMSG, ROWS), BF16)
    return pl.pallas_call(
        functools.partial(attend, nq, nc, at, packed),
        out_shape=shape,
        in_specs=[VMEM] * len(operands),
        out_specs=VMEM,
        scratch_shapes=([pltpu.VMEM(sums, F32)] if packed else [])
        + [pltpu.VMEM((nq, QMSG, ROWS), BF16), pltpu.VMEM((nc, GROUP, MSG, 128), BF16)],
        compiler_params=PARAMS,
        cost_estimate=pl.CostEstimate(
            flops=pairs * 16, bytes_accessed=nc * 2**14, transcendentals=0
        ),
        name="attend",
    )(*operands)


def simple(kernel, shape, name, *operands):
    return pl.pallas_call(
        kernel,
        out_shape=shape,
        in_specs=[VMEM] * len(operands),
        out_specs=VMEM,
        compiler_params=PARAMS,
        name=name,
    )(*operands)


def place(index):
    inner, outer = divmod(index, 16)
    return inner % 4, inner // 4 * 2 + outer // 2 % 2, outer // 4, outer % 2


def index_of(x, y, z, core):
    return (y // 2 * 4 + x) * 16 + z * 4 + y % 2 * 2 + core


def permute(array, target):
    pairs = []
    for source in range(128):
        x, y, z, core = place(source)
        x, y, z, core = target(x, y, z, core)
        pairs.append((source, index_of(x % 4, y % 4, z % 4, core % 2)))
    return lax.ppermute(array, ("inner", "outer"), pairs)


def along_first(array, d):
    return permute(array, lambda x, y, z, c: (x, y, z + d, c) if c else (x + d, y, z, c))


def along_second(array, d):
    return permute(array, lambda x, y, z, c: (x + d, y, z, c) if c else (x, y, z + d, c))


def y_neighbour(array):
    return permute(array, lambda x, y, z, c: (x, y ^ 1, z, c))


def y_opposite(array):
    return permute(array, lambda x, y, z, c: (x, y + 2, z, c))


def other_core(array):
    return permute(array, lambda x, y, z, c: (x, y, z, c + 1))


def after(array, *others):
    return lax.optimization_barrier((array, *others))[0]


def prepared(kernel, name, operands, scratch, *shapes):
    return pl.pallas_call(
        kernel,
        out_shape=shapes,
        in_specs=[HBM] * len(operands),
        out_specs=(VMEM,) * len(shapes),
        scratch_shapes=[*scratch, pltpu.SemaphoreType.DMA((len(operands),))],
        compiler_params=pltpu.CompilerParams(vmem_limit_bytes=63 << 20),
        name=name,
    )(*operands)


def shards(queries, key_value, positions, sinks):
    (km,) = prepared(
        prepare_keys,
        "prepare_keys",
        (positions, key_value),
        [pltpu.SMEM(positions.shape, jnp.int32), pltpu.VMEM(key_value.shape, BF16)],
        jax.ShapeDtypeStruct((1, MSG, 128), BF16),
    )
    qm, flag = prepared(
        prepare_queries,
        "prepare_queries",
        (positions, after(queries, km), sinks),
        [
            pltpu.SMEM(positions.shape, jnp.int32),
            pltpu.VMEM(queries.shape, BF16),
            pltpu.SMEM(sinks.shape, F32),
        ],
        jax.ShapeDtypeStruct((QMSG, ROWS), BF16),
        jax.ShapeDtypeStruct((16, ROWS), F32),
    )
    pair = jnp.concatenate([after(km, qm), y_opposite(km)], axis=0)
    asked = y_neighbour(qm)
    left, right, far = [along_first(pair, d) for d in (-1, 1, 2)]
    near = jnp.concatenate([after(pair, asked), left, right, far], axis=0)
    side3, side1, side2 = [along_second(near, d) for d in (2, 1, -1)]
    own = partials([qm], [near])
    near2 = other_core(near)
    mate = partials([after(asked, own)], [near])
    diag = simple(
        diagonal, jax.ShapeDtypeStruct((PART + 16, ROWS), F32), "diagonal", after(qm, mate), km, flag
    )
    mate = partials([after(asked, diag)], [near2], mate, 0)
    own = partials([after(qm, mate)], [near2], own, 0)
    mate = partials([after(asked, own)], [side1], mate, 0)
    own = partials([after(qm, mate)], [side1], own, 0)
    swap1 = other_core(after(side1, own))
    mate = partials([after(asked, own)], [side2], mate, 0)
    swap2, swap3 = [other_core(after(side, mate)) for side in (side2, side3)]
    mate = partials([asked], [side3, swap1], mate, 0)
    sent = partials([asked], [swap2, swap3], mate, 0, packed=True)
    back = y_neighbour(sent)
    own = partials([after(qm, sent)], [swap3, swap2], own, 0)
    own = partials([qm], [swap1, side3], own, 0)
    own = partials([qm], [side2], own, 0)
    return pl.pallas_call(
        finish,
        out_shape=jax.ShapeDtypeStruct(queries.shape, BF16),
        in_specs=[VMEM] * 3,
        out_specs=VMEM,
        compiler_params=PARAMS,
        name="finish",
    )(diag, own.reshape(PART, ROWS), back)


def solution(mesh):
    return jax.shard_map(
        shards,
        mesh=mesh,
        in_specs=(
            P(("inner", "outer"), None),
            P(("inner", "outer"), None),
            P(("inner", "outer")),
            P(),
        ),
        out_specs=P(("inner", "outer"), None),
        check_vma=False,
    )
```

```python
import functools

import jax
import jax.numpy as jnp
from jax import lax
from jax.experimental import pallas as pl
from jax.experimental.pallas import tpu as pltpu
from jax.sharding import PartitionSpec as P

HEADS = 8
HD = 64
SPAN = 96
ROWS = HEADS * SPAN
GROUP = 8
CHUNK = GROUP * SPAN
MSG = 208
QMSG = 144
PART = 160
LOG2E = 1.4426950408889634
SCALE = HD**-0.5 * LOG2E
LIMIT = 1e36
F32 = jnp.float32
BF16 = jnp.bfloat16
VMEM = pl.BlockSpec(memory_space=pltpu.VMEM)
HBM = pl.BlockSpec(memory_space=pltpu.HBM)
PARAMS = pltpu.CompilerParams(vmem_limit_bytes=20 << 20)


def dot(a, b):
    return jnp.dot(a, b, preferred_element_type=F32)


def load(pairs, sems):
    copies = [
        pltpu.make_async_copy(source, target, sems.at[n]) for n, (source, target) in enumerate(pairs)
    ]
    for copy in copies:
        copy.start()
    for copy in copies:
        copy.wait()


def order(pos_ref, ref):
    run = pos_ref[0] // SPAN
    swapped = run >= 128
    first, second = ref[0:SPAN, :], ref[SPAN : 2 * SPAN, :]
    lower = jnp.where(swapped, 255 - run, run).astype(F32)
    return swapped, lower, jnp.where(swapped, second, first), jnp.where(swapped, first, second)


def prepare_keys(pos_hbm, kv_hbm, km_ref, pos_ref, kv_ref, sems):
    load(((pos_hbm, pos_ref), (kv_hbm, kv_ref)), sems)
    _, lower, lo, up = order(pos_ref, kv_ref)
    km_ref[0, 0:SPAN, :] = jnp.concatenate([lo[:, :HD], up[:, :HD]], axis=1)
    km_ref[0, SPAN : 2 * SPAN, :] = jnp.concatenate([lo[:, HD:], up[:, HD:]], axis=1)
    km_ref[0, 2 * SPAN :, :] = jnp.full((MSG - 2 * SPAN, 128), lower, F32).astype(BF16)


def prepare_queries(pos_hbm, q_hbm, sink_hbm, qm_ref, flag_ref, pos_ref, q_ref, sink_ref, sems):
    load(((pos_hbm, pos_ref), (q_hbm, q_ref), (sink_hbm, sink_ref)), sems)
    swapped, lower, lo, up = order(pos_ref, q_ref)
    stacked = jnp.concatenate(
        [
            jnp.concatenate([lo[:, h * HD : (h + 1) * HD], up[:, h * HD : (h + 1) * HD]], axis=1)
            for h in range(HEADS)
        ],
        axis=0,
    )
    qm_ref[0:128, :] = jnp.transpose(stacked)
    qm_ref[128:, :] = jnp.full((QMSG - 128, ROWS), lower, F32).astype(BF16)
    flag_ref[0:8, :] = jnp.full((8, ROWS), jnp.where(swapped, 1.0, 0.0), F32)
    lanes = lax.broadcasted_iota(jnp.int32, (8, ROWS), 1)
    sinks = jnp.full((8, ROWS), sink_ref[0], F32)
    for h in range(1, HEADS):
        sinks = jnp.where(lanes >= h * SPAN, sink_ref[h], sinks)
    flag_ref[8:16, :] = sinks


def diagonal(qm_ref, km_ref, flag_ref, out_ref):
    out_ref[PART:, :] = flag_ref[...]
    keys = lax.broadcasted_iota(jnp.int32, (SPAN, ROWS), 0)
    rows = lax.broadcasted_iota(jnp.int32, (SPAN, ROWS), 1)
    mine = rows
    for h in range(1, HEADS):
        mine = jnp.where(rows >= h * SPAN, rows - h * SPAN, mine)
    visible = keys <= mine
    k = km_ref[0, 0:SPAN, :]
    v = jnp.transpose(km_ref[0, SPAN : 2 * SPAN, :].astype(F32)).astype(BF16)
    for half in range(2):
        part = slice(half * HD, (half + 1) * HD)
        s = dot(k[:, part], qm_ref[part, :]) * SCALE
        s = jnp.where(visible, s, -1e30)
        shift = jnp.maximum(jnp.max(s, axis=0, keepdims=True), 0.0)
        p = jnp.where(visible, jnp.exp2(s - shift), 0.0)
        out_ref[part, :] = dot(v[part, :], p.astype(BF16))
        total = jnp.sum(p, axis=0, keepdims=True)
        out_ref[128 + 8 * half : 136 + 8 * half, :] = jnp.broadcast_to(total, (8, ROWS))
        out_ref[144 + 8 * half : 152 + 8 * half, :] = jnp.broadcast_to(shift, (8, ROWS))


def chunk_masks(keys, q_ref):
    info = keys[:, 2 * SPAN : 2 * SPAN + 16, :].astype(F32)[:, 0:1, :]
    own = q_ref[128:144, 0:128].astype(F32)[0:1, :]
    below = jnp.where(info < own[None], 1.0, 0.0)
    above = jnp.where(info > own[None], 1.0, 0.0)
    return below, above


def along_lanes(mask):
    lanes = lax.broadcasted_iota(jnp.int32, (16, CHUNK), 1)
    wide = [
        jnp.concatenate([jnp.broadcast_to(mask[b], (16, 128))] * (CHUNK // 128), axis=1)
        for b in range(GROUP)
    ]
    out = wide[0]
    for b in range(1, GROUP):
        out = jnp.where(lanes >= b * SPAN, wide[b], out)
    return out


def transposed_values(keys):
    return jnp.transpose(keys[:, SPAN : 2 * SPAN, :].reshape(CHUNK, 128))


def chunk_operands(keys, q_ref, vt):
    below, above = chunk_masks(keys, q_ref)
    k = keys[:, 0:SPAN, :]
    lanes = lax.broadcasted_iota(jnp.int32, (GROUP, 1, 128), 2)
    keep = jnp.where(lanes < HD, below, above).astype(BF16)
    chosen = (k * keep).reshape(CHUNK, 128)
    low, high = along_lanes(below), along_lanes(above)
    rows = lax.broadcasted_iota(jnp.int32, (16, CHUNK), 0)
    ones = jnp.where(rows < 8, low, high).astype(BF16)
    low, high = low[0:1].astype(BF16), high[0:1].astype(BF16)
    values = jnp.concatenate([vt[:HD] * low, vt[HD:] * high, ones], axis=0)
    return k.reshape(CHUNK, 128), chosen, values


def each(count, body):
    if count == 1:
        body(0)
    else:
        pl.loop(0, count)(body)


def attend(nq, nc, at, packed, *refs):
    q_refs, refs = refs[:nq], refs[nq:]
    key_refs, refs = refs[:nc], refs[nc:]
    if at is not None:
        old_ref, refs = refs[0], refs[1:]
    out_ref, refs = refs[0], refs[1:]
    sums = refs[0] if packed else out_ref
    queries, keys = refs[-2], refs[-1]
    for q in range(nq):
        queries[q] = q_refs[q][...]
        sums[q] = jnp.zeros((PART, ROWS), F32) if at is None else old_ref[at + q]
    for c in range(nc):
        keys[c] = key_refs[c][...]

    def add(c):
        chunk = keys[c]
        vt = transposed_values(chunk)
        first = jnp.concatenate([vt[:HD], jnp.ones((16, CHUNK), BF16)], axis=0)

        def one(q):
            q_ref = queries.at[q]
            k, chosen, values = chunk_operands(chunk, q_ref, vt)
            a = dot(k[:, :HD], q_ref[HD:128, :])
            b = dot(chosen, q_ref[0:128, :])
            pa = jnp.exp2(a * SCALE).astype(BF16)
            pb = jnp.exp2(b * SCALE).astype(BF16)
            oa = dot(first, pa)
            ob = dot(values, pb)
            sums[q, 0:HD, :] += ob[:HD]
            sums[q, HD:128, :] += oa[:HD] + ob[HD:128]
            sums[q, 128:136, :] += ob[128:136]
            sums[q, 136:144, :] += oa[HD : HD + 8] + ob[136:144]

        each(nq, one)

    each(nc, add)

    def check(q):
        bad = jnp.sum(jnp.where(sums[q, 128:144, :] < LIMIT, 0.0, 1.0))
        bad = bad + jnp.sum(sums[q, 144:160, :])

        @pl.when(bad > 0.0)
        def _():
            for k in range(nq):

                @pl.when(q == k)
                def _():
                    sums[k] = jnp.zeros((PART, ROWS), F32) if at is None else old_ref[at + k]

            @pl.loop(0, nc)
            def _(c):
                careful(keys.at[c], queries.at[q], sums.at[q])

    each(nq, check)

    if packed:
        for q in range(nq):
            out_ref[0:128, :] = sums[q, 0:128, :].astype(BF16)
            rows = lax.broadcasted_iota(jnp.int32, (16, ROWS), 0)
            stats = jnp.zeros((16, ROWS), F32)
            for row, start in ((0, 128), (2, 136)):
                total = jnp.broadcast_to(sums[q, start : start + 1, :], (16, ROWS))
                high = total.astype(BF16).astype(F32)
                stats = jnp.where(rows == row, high, stats)
                stats = jnp.where(rows == row + 1, total - high, stats)
            for row, start in ((4, 144), (5, 152)):
                shift = jnp.broadcast_to(sums[q, start : start + 1, :], (16, ROWS))
                stats = jnp.where(rows == row, shift, stats)
            out_ref[128:144, :] = stats.astype(BF16)


def careful(keys, q_ref, out_ref):
    def raise_shift(half, top):
        old = out_ref[144 + 8 * half : 145 + 8 * half, :]
        new = jnp.maximum(old, jnp.maximum(top, 0.0).astype(BF16).astype(F32))
        factor = jnp.exp2(old - new)
        out_ref[half * HD : (half + 1) * HD, :] *= factor
        out_ref[128 + 8 * half : 136 + 8 * half, :] *= factor
        out_ref[144 + 8 * half : 152 + 8 * half, :] = jnp.broadcast_to(new, (8, ROWS))
        return new

    def add(half, values, p):
        p = p.astype(BF16)
        out_ref[half * HD : (half + 1) * HD, :] += dot(values, p)
        out_ref[128 + 8 * half : 136 + 8 * half, :] += dot(jnp.ones((16, SPAN), BF16), p)[:8]

    def wide(row):
        return jnp.concatenate([row] * (ROWS // 128), axis=1)

    own = wide(q_ref[128:144, 0:128].astype(F32)[0:1, :])

    @pl.loop(0, GROUP)
    def _(b):
        k = keys[b, 0:SPAN, :]
        vt = jnp.transpose(keys[b, SPAN : 2 * SPAN, :].astype(F32)).astype(BF16)
        info = wide(keys[b, 2 * SPAN : 2 * SPAN + 16, :].astype(F32)[0:1, :])
        low = dot(k[:, :HD], q_ref[HD:128, :]) * SCALE
        shift = raise_shift(1, jnp.max(low, axis=0, keepdims=True))
        add(1, vt[:HD], jnp.exp2(low - shift))
        for half, seen in ((0, info < own), (1, info > own)):
            part = slice(half * HD, (half + 1) * HD)
            s = dot(k[:, part], q_ref[part, :]) * SCALE
            top = jnp.where(seen, jnp.max(s, axis=0, keepdims=True), -1e30)
            shift = raise_shift(half, top)
            add(half, vt[part], jnp.where(seen, jnp.exp2(s - shift), 0.0))


def finish(diag_ref, own_ref, message, out_ref):
    swapped = jnp.broadcast_to(diag_ref[PART : PART + 1, 0:128], (SPAN, 128)) > 0.5
    held = []
    for half in range(2):
        part = slice(half * HD, (half + 1) * HD)
        stat = 128 + 8 * half
        shifts = [p[stat + 16 : stat + 17, :] for p in (diag_ref, own_ref)]
        top = jnp.maximum(*shifts)
        total = jnp.exp2(diag_ref[PART + 8 : PART + 9, :] * LOG2E - top)
        sums = jnp.zeros((HD, ROWS), F32)
        for p, shift in zip((diag_ref, own_ref), shifts):
            factor = jnp.exp2(shift - top)
            total = total + p[stat : stat + 1, :] * factor
            sums = sums + p[part, :] * factor
        held.append((top, total, sums))
    stats = message[128:144, :].astype(F32)
    results = []
    for half, (top, total, sums) in enumerate(held):
        shift = stats[4 + half : 5 + half]
        new = jnp.maximum(top, shift)
        kept, added = jnp.exp2(top - new), jnp.exp2(shift - new)
        more = stats[2 * half : 2 * half + 1] + stats[2 * half + 1 : 2 * half + 2]
        scale = 1.0 / (total * kept + more * added)
        sent = message[half * HD : (half + 1) * HD, :].astype(F32)
        results.append(sums * (kept * scale) + sent * (added * scale))
    both = jnp.transpose(jnp.concatenate(results, axis=0))
    for g in range(HEADS // 2):
        even, odd = both[2 * g * SPAN : (2 * g + 1) * SPAN], both[(2 * g + 1) * SPAN : (2 * g + 2) * SPAN]
        lo = jnp.concatenate([even[:, :HD], odd[:, :HD]], axis=1)
        up = jnp.concatenate([even[:, HD:], odd[:, HD:]], axis=1)
        lanes = slice(128 * g, 128 * (g + 1))
        out_ref[0:SPAN, lanes] = jnp.where(swapped, up, lo).astype(BF16)
        out_ref[SPAN : 2 * SPAN, lanes] = jnp.where(swapped, lo, up).astype(BF16)


def partials(queries, chunks, old=None, at=None, packed=False):
    nq, nc = len(queries), len(chunks)
    pairs = nq * nc * 2 * CHUNK * ROWS
    operands = [*queries, *chunks, *([] if at is None else [old])]
    sums = (nq, PART, ROWS)
    shape = jax.ShapeDtypeStruct(sums, F32)
    if packed:
        shape = jax.ShapeDtypeStruct((QMSG, ROWS), BF16)
    return pl.pallas_call(
        functools.partial(attend, nq, nc, at, packed),
        out_shape=shape,
        in_specs=[VMEM] * len(operands),
        out_specs=VMEM,
        scratch_shapes=([pltpu.VMEM(sums, F32)] if packed else [])
        + [pltpu.VMEM((nq, QMSG, ROWS), BF16), pltpu.VMEM((nc, GROUP, MSG, 128), BF16)],
        compiler_params=PARAMS,
        cost_estimate=pl.CostEstimate(
            flops=pairs * 16, bytes_accessed=nc * 2**14, transcendentals=0
        ),
        name="attend",
    )(*operands)


def simple(kernel, shape, name, *operands):
    return pl.pallas_call(
        kernel,
        out_shape=shape,
        in_specs=[VMEM] * len(operands),
        out_specs=VMEM,
        compiler_params=PARAMS,
        name=name,
    )(*operands)


def place(index):
    inner, outer = divmod(index, 16)
    return inner % 4, inner // 4 * 2 + outer // 2 % 2, outer // 4, outer % 2


def index_of(x, y, z, core):
    return (y // 2 * 4 + x) * 16 + z * 4 + y % 2 * 2 + core


def permute(array, target):
    pairs = []
    for source in range(128):
        x, y, z, core = place(source)
        x, y, z, core = target(x, y, z, core)
        pairs.append((source, index_of(x % 4, y % 4, z % 4, core % 2)))
    return lax.ppermute(array, ("inner", "outer"), pairs)


def along_first(array, d):
    return permute(array, lambda x, y, z, c: (x, y, z + d, c) if c else (x + d, y, z, c))


def along_second(array, d):
    return permute(array, lambda x, y, z, c: (x + d, y, z, c) if c else (x, y, z + d, c))


def y_neighbour(array):
    return permute(array, lambda x, y, z, c: (x, y ^ 1, z, c))


def y_mirror(array):
    return permute(array, lambda x, y, z, c: (x, 3 - y, z, c))


def other_core(array):
    return permute(array, lambda x, y, z, c: (x, y, z, c + 1))


def after(array, *others):
    return lax.optimization_barrier((array, *others))[0]


def prepared(kernel, name, operands, scratch, *shapes):
    return pl.pallas_call(
        kernel,
        out_shape=shapes,
        in_specs=[HBM] * len(operands),
        out_specs=(VMEM,) * len(shapes),
        scratch_shapes=[*scratch, pltpu.SemaphoreType.DMA((len(operands),))],
        compiler_params=pltpu.CompilerParams(vmem_limit_bytes=63 << 20),
        name=name,
    )(*operands)


def shards(queries, key_value, positions, sinks):
    (km,) = prepared(
        prepare_keys,
        "prepare_keys",
        (positions, key_value),
        [pltpu.SMEM(positions.shape, jnp.int32), pltpu.VMEM(key_value.shape, BF16)],
        jax.ShapeDtypeStruct((1, MSG, 128), BF16),
    )
    qm, flag = prepared(
        prepare_queries,
        "prepare_queries",
        (positions, after(queries, km), sinks),
        [
            pltpu.SMEM(positions.shape, jnp.int32),
            pltpu.VMEM(queries.shape, BF16),
            pltpu.SMEM(sinks.shape, F32),
        ],
        jax.ShapeDtypeStruct((QMSG, ROWS), BF16),
        jax.ShapeDtypeStruct((16, ROWS), F32),
    )
    pair = jnp.concatenate([after(km, qm), y_mirror(km)], axis=0)
    asked = y_neighbour(qm)
    left, right, far = [along_first(pair, d) for d in (-1, 1, 2)]
    diag = simple(
        diagonal, jax.ShapeDtypeStruct((PART + 16, ROWS), F32), "diagonal", after(qm, far), km, flag
    )
    near = jnp.concatenate([after(pair, asked, diag), left, right, far], axis=0)
    side3, side1, side2 = [along_second(near, d) for d in (2, 1, -1)]
    own = partials([qm], [near])
    near2 = other_core(near)
    mate = partials([after(asked, own)], [near])
    mate = partials([after(asked, mate)], [near2], mate, 0)
    own = partials([after(qm, mate)], [near2], own, 0)
    mate = partials([after(asked, own)], [side1], mate, 0)
    own = partials([after(qm, mate)], [side1], own, 0)
    swap1 = other_core(after(side1, own))
    mate = partials([after(asked, own)], [side2], mate, 0)
    swap2, swap3 = [other_core(after(side, mate)) for side in (side2, side3)]
    mate = partials([asked], [side3, swap1], mate, 0)
    sent = partials([asked], [swap2, swap3], mate, 0, packed=True)
    back = y_neighbour(sent)
    own = partials([after(qm, sent)], [swap3, swap2], own, 0)
    own = partials([qm], [swap1, side3], own, 0)
    own = partials([qm], [side2], own, 0)
    return pl.pallas_call(
        finish,
        out_shape=jax.ShapeDtypeStruct(queries.shape, BF16),
        in_specs=[VMEM] * 3,
        out_specs=VMEM,
        compiler_params=PARAMS,
        name="finish",
    )(diag, own.reshape(PART, ROWS), back)


def solution(mesh):
    return jax.shard_map(
        shards,
        mesh=mesh,
        in_specs=(
            P(("inner", "outer"), None),
            P(("inner", "outer"), None),
            P(("inner", "outer")),
            P(),
        ),
        out_specs=P(("inner", "outer"), None),
        check_vma=False,
    )
```

```python
import functools

import jax
import jax.numpy as jnp
from jax import lax
from jax.experimental import pallas as pl
from jax.experimental.pallas import tpu as pltpu
from jax.sharding import PartitionSpec as P

HEADS = 8
HD = 64
SPAN = 96
ROWS = HEADS * SPAN
GROUP = 8
CHUNK = GROUP * SPAN
MSG = 208
QMSG = 144
PART = 160
LOG2E = 1.4426950408889634
SCALE = HD**-0.5 * LOG2E
LIMIT = 1e36
F32 = jnp.float32
BF16 = jnp.bfloat16
VMEM = pl.BlockSpec(memory_space=pltpu.VMEM)
HBM = pl.BlockSpec(memory_space=pltpu.HBM)
PARAMS = pltpu.CompilerParams(vmem_limit_bytes=20 << 20)


def dot(a, b):
    return jnp.dot(a, b, preferred_element_type=F32)


def load(pairs, sems):
    copies = [
        pltpu.make_async_copy(source, target, sems.at[n]) for n, (source, target) in enumerate(pairs)
    ]
    for copy in copies:
        copy.start()
    for copy in copies:
        copy.wait()


def order(pos_ref, ref):
    run = pos_ref[0] // SPAN
    swapped = run >= 128
    first, second = ref[0:SPAN, :], ref[SPAN : 2 * SPAN, :]
    lower = jnp.where(swapped, 255 - run, run).astype(F32)
    return swapped, lower, jnp.where(swapped, second, first), jnp.where(swapped, first, second)


def prepare_keys(pos_hbm, kv_hbm, km_ref, pos_ref, kv_ref, sems):
    load(((pos_hbm, pos_ref), (kv_hbm, kv_ref)), sems)
    _, lower, lo, up = order(pos_ref, kv_ref)
    km_ref[0, 0:SPAN, :] = jnp.concatenate([lo[:, :HD], up[:, :HD]], axis=1)
    km_ref[0, SPAN : 2 * SPAN, :] = jnp.concatenate([lo[:, HD:], up[:, HD:]], axis=1)
    km_ref[0, 2 * SPAN :, :] = jnp.full((MSG - 2 * SPAN, 128), lower, F32).astype(BF16)


def prepare_queries(pos_hbm, q_hbm, sink_hbm, qm_ref, flag_ref, pos_ref, q_ref, sink_ref, sems):
    load(((pos_hbm, pos_ref), (q_hbm, q_ref), (sink_hbm, sink_ref)), sems)
    swapped, lower, lo, up = order(pos_ref, q_ref)
    stacked = jnp.concatenate(
        [
            jnp.concatenate([lo[:, h * HD : (h + 1) * HD], up[:, h * HD : (h + 1) * HD]], axis=1)
            for h in range(HEADS)
        ],
        axis=0,
    )
    qm_ref[0:128, :] = jnp.transpose(stacked)
    qm_ref[128:, :] = jnp.full((QMSG - 128, ROWS), lower, F32).astype(BF16)
    flag_ref[0:8, :] = jnp.full((8, ROWS), jnp.where(swapped, 1.0, 0.0), F32)
    lanes = lax.broadcasted_iota(jnp.int32, (8, ROWS), 1)
    sinks = jnp.full((8, ROWS), sink_ref[0], F32)
    for h in range(1, HEADS):
        sinks = jnp.where(lanes >= h * SPAN, sink_ref[h], sinks)
    flag_ref[8:16, :] = sinks


def diagonal(qm_ref, km_ref, flag_ref, out_ref):
    out_ref[PART:, :] = flag_ref[...]
    keys = lax.broadcasted_iota(jnp.int32, (SPAN, ROWS), 0)
    rows = lax.broadcasted_iota(jnp.int32, (SPAN, ROWS), 1)
    mine = rows
    for h in range(1, HEADS):
        mine = jnp.where(rows >= h * SPAN, rows - h * SPAN, mine)
    visible = keys <= mine
    k = km_ref[0, 0:SPAN, :]
    v = jnp.transpose(km_ref[0, SPAN : 2 * SPAN, :].astype(F32)).astype(BF16)
    for half in range(2):
        part = slice(half * HD, (half + 1) * HD)
        s = dot(k[:, part], qm_ref[part, :]) * SCALE
        s = jnp.where(visible, s, -1e30)
        shift = jnp.maximum(jnp.max(s, axis=0, keepdims=True), 0.0)
        p = jnp.where(visible, jnp.exp2(s - shift), 0.0)
        out_ref[part, :] = dot(v[part, :], p.astype(BF16))
        out_ref[128 + 8 * half : 136 + 8 * half, :] = jnp.sum(p.reshape(SPAN // 8, 8, ROWS), axis=0)
        out_ref[144 + 8 * half : 152 + 8 * half, :] = jnp.broadcast_to(shift, (8, ROWS))


def chunk_masks(keys, q_ref):
    info = keys[:, 2 * SPAN : 2 * SPAN + 16, :].astype(F32)[:, 0:1, :]
    own = q_ref[128:144, 0:128].astype(F32)[0:1, :]
    below = jnp.where(info < own[None], 1.0, 0.0)
    above = jnp.where(info > own[None], 1.0, 0.0)
    return below, above


def along_lanes(mask):
    lanes = lax.broadcasted_iota(jnp.int32, (16, CHUNK), 1)
    wide = [
        jnp.concatenate([jnp.broadcast_to(mask[b], (16, 128))] * (CHUNK // 128), axis=1)
        for b in range(GROUP)
    ]
    out = wide[0]
    for b in range(1, GROUP):
        out = jnp.where(lanes >= b * SPAN, wide[b], out)
    return out


def transposed_values(keys):
    return jnp.transpose(keys[:, SPAN : 2 * SPAN, :].reshape(CHUNK, 128))


def chunk_operands(keys, q_ref, vt):
    below, above = chunk_masks(keys, q_ref)
    k = keys[:, 0:SPAN, :]
    lanes = lax.broadcasted_iota(jnp.int32, (GROUP, 1, 128), 2)
    keep = jnp.where(lanes < HD, below, above).astype(BF16)
    chosen = (k * keep).reshape(CHUNK, 128)
    low, high = along_lanes(below), along_lanes(above)
    low, high = low[0:1].astype(BF16), high[0:1].astype(BF16)
    values = jnp.concatenate([vt[:HD] * low, vt[HD:] * high], axis=0)
    return k.reshape(CHUNK, 128), chosen, values


def each(count, body):
    if count == 1:
        body(0)
    else:
        pl.loop(0, count)(body)


def attend(nq, nc, at, packed, *refs):
    q_refs, refs = refs[:nq], refs[nq:]
    key_refs, refs = refs[:nc], refs[nc:]
    if at is not None:
        old_ref, refs = refs[0], refs[1:]
    out_ref, refs = refs[0], refs[1:]
    sums = refs[0] if packed else out_ref
    queries, keys = refs[-2], refs[-1]
    for q in range(nq):
        queries[q] = q_refs[q][...]
        sums[q] = jnp.zeros((PART, ROWS), F32) if at is None else old_ref[at + q]
    for c in range(nc):
        keys[c] = key_refs[c][...]

    def add(c):
        chunk = keys[c]
        vt = transposed_values(chunk)

        def one(q):
            q_ref = queries.at[q]
            k, chosen, values = chunk_operands(chunk, q_ref, vt)
            a = jnp.exp2(dot(k[:, :HD], q_ref[HD:128, :]) * SCALE)
            b = jnp.exp2(dot(chosen, q_ref[0:128, :]) * SCALE)
            oa = dot(vt[:HD], a.astype(BF16))
            ob = dot(values, b.astype(BF16))
            below, above = [
                jnp.concatenate([mask] * (ROWS // 128), axis=2) for mask in chunk_masks(chunk, q_ref)
            ]
            some = jnp.sum(b.reshape(GROUP, SPAN // 8, 8, ROWS), axis=1)
            sums[q, 0:HD, :] += ob[:HD]
            sums[q, HD:128, :] += oa + ob[HD:128]
            sums[q, 128:136, :] += jnp.sum(some * below, axis=0)
            sums[q, 136:144, :] += jnp.sum(a.reshape(CHUNK // 8, 8, ROWS), axis=0) + jnp.sum(
                some * above, axis=0
            )

        each(nq, one)

    each(nc, add)

    def check(q):
        bad = jnp.sum(jnp.where(sums[q, 128:144, :] < LIMIT, 0.0, 1.0))
        bad = bad + jnp.sum(sums[q, 144:160, :])

        @pl.when(bad > 0.0)
        def _():
            for k in range(nq):

                @pl.when(q == k)
                def _():
                    sums[k] = jnp.zeros((PART, ROWS), F32) if at is None else old_ref[at + k]

            @pl.loop(0, nc)
            def _(c):
                careful(keys.at[c], queries.at[q], sums.at[q])

    each(nq, check)

    if packed:
        for q in range(nq):
            out_ref[0:128, :] = sums[q, 0:128, :].astype(BF16)
            rows = lax.broadcasted_iota(jnp.int32, (16, ROWS), 0)
            stats = jnp.zeros((16, ROWS), F32)
            for row, start in ((0, 128), (2, 136)):
                total = jnp.sum(sums[q, start : start + 8, :], axis=0, keepdims=True)
                total = jnp.broadcast_to(total, (16, ROWS))
                high = total.astype(BF16).astype(F32)
                stats = jnp.where(rows == row, high, stats)
                stats = jnp.where(rows == row + 1, total - high, stats)
            for row, start in ((4, 144), (5, 152)):
                shift = jnp.broadcast_to(sums[q, start : start + 1, :], (16, ROWS))
                stats = jnp.where(rows == row, shift, stats)
            out_ref[128:144, :] = stats.astype(BF16)


def careful(keys, q_ref, out_ref):
    def raise_shift(half, top):
        old = out_ref[144 + 8 * half : 145 + 8 * half, :]
        new = jnp.maximum(old, jnp.maximum(top, 0.0).astype(BF16).astype(F32))
        factor = jnp.exp2(old - new)
        out_ref[half * HD : (half + 1) * HD, :] *= factor
        out_ref[128 + 8 * half : 136 + 8 * half, :] *= factor
        out_ref[144 + 8 * half : 152 + 8 * half, :] = jnp.broadcast_to(new, (8, ROWS))
        return new

    def add(half, values, p):
        p = p.astype(BF16)
        out_ref[half * HD : (half + 1) * HD, :] += dot(values, p)
        rows = lax.broadcasted_iota(jnp.int32, (16, SPAN), 0)
        once = jnp.where(rows == 0, 1.0, 0.0).astype(BF16)
        out_ref[128 + 8 * half : 136 + 8 * half, :] += dot(once, p)[:8]

    def wide(row):
        return jnp.concatenate([row] * (ROWS // 128), axis=1)

    own = wide(q_ref[128:144, 0:128].astype(F32)[0:1, :])

    @pl.loop(0, GROUP)
    def _(b):
        k = keys[b, 0:SPAN, :]
        vt = jnp.transpose(keys[b, SPAN : 2 * SPAN, :].astype(F32)).astype(BF16)
        info = wide(keys[b, 2 * SPAN : 2 * SPAN + 16, :].astype(F32)[0:1, :])
        low = dot(k[:, :HD], q_ref[HD:128, :]) * SCALE
        shift = raise_shift(1, jnp.max(low, axis=0, keepdims=True))
        add(1, vt[:HD], jnp.exp2(low - shift))
        for half, seen in ((0, info < own), (1, info > own)):
            part = slice(half * HD, (half + 1) * HD)
            s = dot(k[:, part], q_ref[part, :]) * SCALE
            top = jnp.where(seen, jnp.max(s, axis=0, keepdims=True), -1e30)
            shift = raise_shift(half, top)
            add(half, vt[part], jnp.where(seen, jnp.exp2(s - shift), 0.0))


def finish(diag_ref, own_ref, message, out_ref):
    swapped = jnp.broadcast_to(diag_ref[PART : PART + 1, 0:128], (SPAN, 128)) > 0.5
    held = []
    for half in range(2):
        part = slice(half * HD, (half + 1) * HD)
        stat = 128 + 8 * half
        shifts = [p[stat + 16 : stat + 17, :] for p in (diag_ref, own_ref)]
        top = jnp.maximum(*shifts)
        total = jnp.exp2(diag_ref[PART + 8 : PART + 9, :] * LOG2E - top)
        sums = jnp.zeros((HD, ROWS), F32)
        for p, shift in zip((diag_ref, own_ref), shifts):
            factor = jnp.exp2(shift - top)
            total = total + jnp.sum(p[stat : stat + 8, :], axis=0, keepdims=True) * factor
            sums = sums + p[part, :] * factor
        held.append((top, total, sums))
    stats = message[128:144, :].astype(F32)
    results = []
    for half, (top, total, sums) in enumerate(held):
        shift = stats[4 + half : 5 + half]
        new = jnp.maximum(top, shift)
        kept, added = jnp.exp2(top - new), jnp.exp2(shift - new)
        more = stats[2 * half : 2 * half + 1] + stats[2 * half + 1 : 2 * half + 2]
        scale = 1.0 / (total * kept + more * added)
        sent = message[half * HD : (half + 1) * HD, :].astype(F32)
        results.append(sums * (kept * scale) + sent * (added * scale))
    both = jnp.transpose(jnp.concatenate(results, axis=0))
    for g in range(HEADS // 2):
        even, odd = both[2 * g * SPAN : (2 * g + 1) * SPAN], both[(2 * g + 1) * SPAN : (2 * g + 2) * SPAN]
        lo = jnp.concatenate([even[:, :HD], odd[:, :HD]], axis=1)
        up = jnp.concatenate([even[:, HD:], odd[:, HD:]], axis=1)
        lanes = slice(128 * g, 128 * (g + 1))
        out_ref[0:SPAN, lanes] = jnp.where(swapped, up, lo).astype(BF16)
        out_ref[SPAN : 2 * SPAN, lanes] = jnp.where(swapped, lo, up).astype(BF16)


def partials(queries, chunks, old=None, at=None, packed=False):
    nq, nc = len(queries), len(chunks)
    pairs = nq * nc * 2 * CHUNK * ROWS
    operands = [*queries, *chunks, *([] if at is None else [old])]
    sums = (nq, PART, ROWS)
    shape = jax.ShapeDtypeStruct(sums, F32)
    if packed:
        shape = jax.ShapeDtypeStruct((QMSG, ROWS), BF16)
    return pl.pallas_call(
        functools.partial(attend, nq, nc, at, packed),
        out_shape=shape,
        in_specs=[VMEM] * len(operands),
        out_specs=VMEM,
        scratch_shapes=([pltpu.VMEM(sums, F32)] if packed else [])
        + [pltpu.VMEM((nq, QMSG, ROWS), BF16), pltpu.VMEM((nc, GROUP, MSG, 128), BF16)],
        compiler_params=PARAMS,
        cost_estimate=pl.CostEstimate(
            flops=pairs * 16, bytes_accessed=nc * 2**14, transcendentals=0
        ),
        name="attend",
    )(*operands)


def simple(kernel, shape, name, *operands):
    return pl.pallas_call(
        kernel,
        out_shape=shape,
        in_specs=[VMEM] * len(operands),
        out_specs=VMEM,
        compiler_params=PARAMS,
        name=name,
    )(*operands)


def place(index):
    inner, outer = divmod(index, 16)
    return inner % 4, inner // 4 * 2 + outer // 2 % 2, outer // 4, outer % 2


def index_of(x, y, z, core):
    return (y // 2 * 4 + x) * 16 + z * 4 + y % 2 * 2 + core


def permute(array, target):
    pairs = []
    for source in range(128):
        x, y, z, core = place(source)
        x, y, z, core = target(x, y, z, core)
        pairs.append((source, index_of(x % 4, y % 4, z % 4, core % 2)))
    return lax.ppermute(array, ("inner", "outer"), pairs)


def along_first(array, d):
    return permute(array, lambda x, y, z, c: (x, y, z + d, c) if c else (x + d, y, z, c))


def along_second(array, d):
    return permute(array, lambda x, y, z, c: (x + d, y, z, c) if c else (x, y, z + d, c))


def y_neighbour(array):
    return permute(array, lambda x, y, z, c: (x, y ^ 1, z, c))


def y_mirror(array):
    return permute(array, lambda x, y, z, c: (x, 3 - y, z, c))


def other_core(array):
    return permute(array, lambda x, y, z, c: (x, y, z, c + 1))


def after(array, *others):
    return lax.optimization_barrier((array, *others))[0]


def prepared(kernel, name, operands, scratch, *shapes):
    return pl.pallas_call(
        kernel,
        out_shape=shapes,
        in_specs=[HBM] * len(operands),
        out_specs=(VMEM,) * len(shapes),
        scratch_shapes=[*scratch, pltpu.SemaphoreType.DMA((len(operands),))],
        compiler_params=pltpu.CompilerParams(vmem_limit_bytes=63 << 20),
        name=name,
    )(*operands)


def shards(queries, key_value, positions, sinks):
    (km,) = prepared(
        prepare_keys,
        "prepare_keys",
        (positions, key_value),
        [pltpu.SMEM(positions.shape, jnp.int32), pltpu.VMEM(key_value.shape, BF16)],
        jax.ShapeDtypeStruct((1, MSG, 128), BF16),
    )
    qm, flag = prepared(
        prepare_queries,
        "prepare_queries",
        (positions, after(queries, km), sinks),
        [
            pltpu.SMEM(positions.shape, jnp.int32),
            pltpu.VMEM(queries.shape, BF16),
            pltpu.SMEM(sinks.shape, F32),
        ],
        jax.ShapeDtypeStruct((QMSG, ROWS), BF16),
        jax.ShapeDtypeStruct((16, ROWS), F32),
    )
    pair = jnp.concatenate([after(km, qm), y_mirror(km)], axis=0)
    asked = y_neighbour(qm)
    left, right, far = [along_first(pair, d) for d in (-1, 1, 2)]
    diag = simple(
        diagonal, jax.ShapeDtypeStruct((PART + 16, ROWS), F32), "diagonal", after(qm, far), km, flag
    )
    near = jnp.concatenate([after(pair, asked, diag), left, right, far], axis=0)
    side3, side1, side2 = [along_second(near, d) for d in (2, 1, -1)]
    own = partials([qm], [near])
    near2 = other_core(near)
    mate = partials([after(asked, own)], [near])
    mate = partials([after(asked, mate)], [near2], mate, 0)
    own = partials([after(qm, mate)], [near2], own, 0)
    mate = partials([after(asked, own)], [side1], mate, 0)
    own = partials([after(qm, mate)], [side1], own, 0)
    swap1 = other_core(after(side1, own))
    mate = partials([after(asked, own)], [side2], mate, 0)
    swap2, swap3 = [other_core(after(side, mate)) for side in (side2, side3)]
    mate = partials([asked], [side3, swap1], mate, 0)
    sent = partials([asked], [swap2, swap3], mate, 0, packed=True)
    back = y_neighbour(sent)
    own = partials([after(qm, sent)], [swap3, swap2], own, 0)
    own = partials([qm], [swap1, side3], own, 0)
    own = partials([qm], [side2], own, 0)
    return pl.pallas_call(
        finish,
        out_shape=jax.ShapeDtypeStruct(queries.shape, BF16),
        in_specs=[VMEM] * 3,
        out_specs=VMEM,
        compiler_params=PARAMS,
        name="finish",
    )(diag, own.reshape(PART, ROWS), back)


def solution(mesh):
    return jax.shard_map(
        shards,
        mesh=mesh,
        in_specs=(
            P(("inner", "outer"), None),
            P(("inner", "outer"), None),
            P(("inner", "outer")),
            P(),
        ),
        out_specs=P(("inner", "outer"), None),
        check_vma=False,
    )
```

```python
import functools

import jax
import jax.numpy as jnp
from jax import lax
from jax.experimental import pallas as pl
from jax.experimental.pallas import tpu as pltpu
from jax.sharding import PartitionSpec as P

HEADS = 8
HD = 64
SPAN = 96
ROWS = HEADS * SPAN
GROUP = 8
CHUNK = GROUP * SPAN
MSG = 208
QMSG = 144
PART = 160
LOG2E = 1.4426950408889634
SCALE = HD**-0.5 * LOG2E
LIMIT = 1e36
F32 = jnp.float32
BF16 = jnp.bfloat16
VMEM = pl.BlockSpec(memory_space=pltpu.VMEM)
HBM = pl.BlockSpec(memory_space=pltpu.HBM)
PARAMS = pltpu.CompilerParams(vmem_limit_bytes=20 << 20)


def dot(a, b):
    return jnp.dot(a, b, preferred_element_type=F32)


def load(pairs, sems):
    copies = [
        pltpu.make_async_copy(source, target, sems.at[n]) for n, (source, target) in enumerate(pairs)
    ]
    for copy in copies:
        copy.start()
    for copy in copies:
        copy.wait()


def order(pos_ref, ref):
    run = pos_ref[0] // SPAN
    swapped = run >= 128
    first, second = ref[0:SPAN, :], ref[SPAN : 2 * SPAN, :]
    lower = jnp.where(swapped, 255 - run, run).astype(F32)
    return swapped, lower, jnp.where(swapped, second, first), jnp.where(swapped, first, second)


def prepare_keys(pos_hbm, kv_hbm, km_ref, pos_ref, kv_ref, sems):
    load(((pos_hbm, pos_ref), (kv_hbm, kv_ref)), sems)
    _, lower, lo, up = order(pos_ref, kv_ref)
    km_ref[0, 0:SPAN, :] = jnp.concatenate([lo[:, :HD], up[:, :HD]], axis=1)
    km_ref[0, SPAN : 2 * SPAN, :] = jnp.concatenate([lo[:, HD:], up[:, HD:]], axis=1)
    km_ref[0, 2 * SPAN :, :] = jnp.full((MSG - 2 * SPAN, 128), lower, F32).astype(BF16)


def prepare_queries(pos_hbm, q_hbm, sink_hbm, qm_ref, flag_ref, pos_ref, q_ref, sink_ref, sems):
    load(((pos_hbm, pos_ref), (q_hbm, q_ref), (sink_hbm, sink_ref)), sems)
    swapped, lower, lo, up = order(pos_ref, q_ref)
    stacked = jnp.concatenate(
        [
            jnp.concatenate([lo[:, h * HD : (h + 1) * HD], up[:, h * HD : (h + 1) * HD]], axis=1)
            for h in range(HEADS)
        ],
        axis=0,
    )
    qm_ref[0:128, :] = jnp.transpose(stacked)
    qm_ref[128:, :] = jnp.full((QMSG - 128, ROWS), lower, F32).astype(BF16)
    flag_ref[0:8, :] = jnp.full((8, ROWS), jnp.where(swapped, 1.0, 0.0), F32)
    lanes = lax.broadcasted_iota(jnp.int32, (8, ROWS), 1)
    sinks = jnp.full((8, ROWS), sink_ref[0], F32)
    for h in range(1, HEADS):
        sinks = jnp.where(lanes >= h * SPAN, sink_ref[h], sinks)
    flag_ref[8:16, :] = sinks


def diagonal(qm_ref, km_ref, flag_ref, out_ref):
    out_ref[PART:, :] = flag_ref[...]
    keys = lax.broadcasted_iota(jnp.int32, (SPAN, ROWS), 0)
    rows = lax.broadcasted_iota(jnp.int32, (SPAN, ROWS), 1)
    mine = rows
    for h in range(1, HEADS):
        mine = jnp.where(rows >= h * SPAN, rows - h * SPAN, mine)
    visible = keys <= mine
    k = km_ref[0, 0:SPAN, :]
    v = jnp.transpose(km_ref[0, SPAN : 2 * SPAN, :].astype(F32)).astype(BF16)
    for half in range(2):
        part = slice(half * HD, (half + 1) * HD)
        s = dot(k[:, part], qm_ref[part, :]) * SCALE
        s = jnp.where(visible, s, -1e30)
        shift = jnp.maximum(jnp.max(s, axis=0, keepdims=True), 0.0)
        p = jnp.where(visible, jnp.exp2(s - shift), 0.0)
        out_ref[part, :] = dot(v[part, :], p.astype(BF16))
        total = jnp.sum(p, axis=0, keepdims=True)
        out_ref[128 + 8 * half : 136 + 8 * half, :] = jnp.broadcast_to(total, (8, ROWS))
        out_ref[144 + 8 * half : 152 + 8 * half, :] = jnp.broadcast_to(shift, (8, ROWS))


def chunk_masks(keys, q_ref):
    info = keys[:, 2 * SPAN : 2 * SPAN + 16, :].astype(F32)[:, 0:1, :]
    own = q_ref[128:144, 0:128].astype(F32)[0:1, :]
    below = jnp.where(info < own[None], 1.0, 0.0)
    above = jnp.where(info > own[None], 1.0, 0.0)
    return below, above


def along_lanes(mask):
    lanes = lax.broadcasted_iota(jnp.int32, (16, CHUNK), 1)
    wide = [
        jnp.concatenate([jnp.broadcast_to(mask[b], (16, 128))] * (CHUNK // 128), axis=1)
        for b in range(GROUP)
    ]
    out = wide[0]
    for b in range(1, GROUP):
        out = jnp.where(lanes >= b * SPAN, wide[b], out)
    return out


def transposed_values(keys):
    return jnp.transpose(keys[:, SPAN : 2 * SPAN, :].reshape(CHUNK, 128))


def chunk_operands(keys, q_ref, vt):
    below, above = chunk_masks(keys, q_ref)
    k = keys[:, 0:SPAN, :]
    lanes = lax.broadcasted_iota(jnp.int32, (GROUP, 1, 128), 2)
    keep = jnp.where(lanes < HD, below, above).astype(BF16)
    chosen = (k * keep).reshape(CHUNK, 128)
    low, high = along_lanes(below), along_lanes(above)
    rows = lax.broadcasted_iota(jnp.int32, (16, CHUNK), 0)
    ones = jnp.where(rows < 8, low, high).astype(BF16)
    low, high = low[0:1].astype(BF16), high[0:1].astype(BF16)
    values = jnp.concatenate([vt[:HD] * low, vt[HD:] * high, ones], axis=0)
    return k.reshape(CHUNK, 128), chosen, values


def each(count, body):
    if count == 1:
        body(0)
    else:
        pl.loop(0, count)(body)


def attend(nq, nc, at, packed, *refs):
    q_refs, refs = refs[:nq], refs[nq:]
    key_refs, refs = refs[:nc], refs[nc:]
    if at is not None:
        old_ref, refs = refs[0], refs[1:]
    out_ref, refs = refs[0], refs[1:]
    sums = refs[0] if packed else out_ref
    queries, keys = refs[-2], refs[-1]
    direct = nc == 1
    start = slice(144, PART) if direct else slice(0, PART)
    for q in range(nq):
        if nq > 1:
            queries[q] = q_refs[q][...]
        sums[q, start] = jnp.zeros_like(sums[q, start]) if at is None else old_ref[at + q, start]
    for c in range(nc):
        if not direct:
            keys[c] = key_refs[c][...]

    def keys_at(c):
        return key_refs[0] if direct else keys.at[c]

    def query_at(q):
        return q_refs[0] if nq == 1 else queries.at[q]

    def store(q, rows, value):
        if not direct:
            sums[q, rows] += value
        elif at is None:
            sums[q, rows] = value
        else:
            sums[q, rows] = old_ref[at + q, rows] + value

    def add(c):
        chunk = keys_at(c)[...]
        vt = transposed_values(chunk)
        first = jnp.concatenate([vt[:HD], jnp.ones((16, CHUNK), BF16)], axis=0)

        def one(q):
            q_ref = query_at(q)
            k, chosen, values = chunk_operands(chunk, q_ref, vt)
            a = dot(k[:, :HD], q_ref[HD:128, :])
            b = dot(chosen, q_ref[0:128, :])
            pa = jnp.exp2(a * SCALE).astype(BF16)
            pb = jnp.exp2(b * SCALE).astype(BF16)
            oa = dot(first, pa)
            ob = dot(values, pb)
            store(q, slice(0, HD), ob[:HD])
            store(q, slice(HD, 128), oa[:HD] + ob[HD:128])
            store(q, slice(128, 136), ob[128:136])
            store(q, slice(136, 144), oa[HD : HD + 8] + ob[136:144])

        each(nq, one)

    each(nc, add)

    def check(q):
        bad = jnp.sum(jnp.where(sums[q, 128:144, :] < LIMIT, 0.0, 1.0))
        bad = bad + jnp.sum(sums[q, 144:160, :])

        @pl.when(bad > 0.0)
        def _():
            for k in range(nq):

                @pl.when(q == k)
                def _():
                    sums[k] = jnp.zeros((PART, ROWS), F32) if at is None else old_ref[at + k]

            each(nc, lambda c: careful(keys_at(c), query_at(q), sums.at[q]))

    each(nq, check)

    if packed:
        for q in range(nq):
            out_ref[0:128, :] = sums[q, 0:128, :].astype(BF16)
            rows = lax.broadcasted_iota(jnp.int32, (16, ROWS), 0)
            stats = jnp.zeros((16, ROWS), F32)
            for row, start in ((0, 128), (2, 136)):
                total = jnp.broadcast_to(sums[q, start : start + 1, :], (16, ROWS))
                high = total.astype(BF16).astype(F32)
                stats = jnp.where(rows == row, high, stats)
                stats = jnp.where(rows == row + 1, total - high, stats)
            for row, start in ((4, 144), (5, 152)):
                shift = jnp.broadcast_to(sums[q, start : start + 1, :], (16, ROWS))
                stats = jnp.where(rows == row, shift, stats)
            out_ref[128:144, :] = stats.astype(BF16)


def careful(keys, q_ref, out_ref):
    def raise_shift(half, top):
        old = out_ref[144 + 8 * half : 145 + 8 * half, :]
        new = jnp.maximum(old, jnp.maximum(top, 0.0).astype(BF16).astype(F32))
        factor = jnp.exp2(old - new)
        out_ref[half * HD : (half + 1) * HD, :] *= factor
        out_ref[128 + 8 * half : 136 + 8 * half, :] *= factor
        out_ref[144 + 8 * half : 152 + 8 * half, :] = jnp.broadcast_to(new, (8, ROWS))
        return new

    def add(half, values, p):
        p = p.astype(BF16)
        out_ref[half * HD : (half + 1) * HD, :] += dot(values, p)
        out_ref[128 + 8 * half : 136 + 8 * half, :] += dot(jnp.ones((16, SPAN), BF16), p)[:8]

    def wide(row):
        return jnp.concatenate([row] * (ROWS // 128), axis=1)

    own = wide(q_ref[128:144, 0:128].astype(F32)[0:1, :])

    @pl.loop(0, GROUP)
    def _(b):
        k = keys[b, 0:SPAN, :]
        vt = jnp.transpose(keys[b, SPAN : 2 * SPAN, :].astype(F32)).astype(BF16)
        info = wide(keys[b, 2 * SPAN : 2 * SPAN + 16, :].astype(F32)[0:1, :])
        low = dot(k[:, :HD], q_ref[HD:128, :]) * SCALE
        shift = raise_shift(1, jnp.max(low, axis=0, keepdims=True))
        add(1, vt[:HD], jnp.exp2(low - shift))
        for half, seen in ((0, info < own), (1, info > own)):
            part = slice(half * HD, (half + 1) * HD)
            s = dot(k[:, part], q_ref[part, :]) * SCALE
            top = jnp.where(seen, jnp.max(s, axis=0, keepdims=True), -1e30)
            shift = raise_shift(half, top)
            add(half, vt[part], jnp.where(seen, jnp.exp2(s - shift), 0.0))


def finish(diag_ref, own_ref, message, out_ref):
    swapped = jnp.broadcast_to(diag_ref[PART : PART + 1, 0:128], (SPAN, 128)) > 0.5
    held = []
    for half in range(2):
        part = slice(half * HD, (half + 1) * HD)
        stat = 128 + 8 * half
        shifts = [p[stat + 16 : stat + 17, :] for p in (diag_ref, own_ref)]
        top = jnp.maximum(*shifts)
        total = jnp.exp2(diag_ref[PART + 8 : PART + 9, :] * LOG2E - top)
        sums = jnp.zeros((HD, ROWS), F32)
        for p, shift in zip((diag_ref, own_ref), shifts):
            factor = jnp.exp2(shift - top)
            total = total + p[stat : stat + 1, :] * factor
            sums = sums + p[part, :] * factor
        held.append((top, total, sums))
    stats = message[128:144, :].astype(F32)
    results = []
    for half, (top, total, sums) in enumerate(held):
        shift = stats[4 + half : 5 + half]
        new = jnp.maximum(top, shift)
        kept, added = jnp.exp2(top - new), jnp.exp2(shift - new)
        more = stats[2 * half : 2 * half + 1] + stats[2 * half + 1 : 2 * half + 2]
        scale = 1.0 / (total * kept + more * added)
        sent = message[half * HD : (half + 1) * HD, :].astype(F32)
        results.append(sums * (kept * scale) + sent * (added * scale))
    both = jnp.transpose(jnp.concatenate(results, axis=0))
    for g in range(HEADS // 2):
        even, odd = both[2 * g * SPAN : (2 * g + 1) * SPAN], both[(2 * g + 1) * SPAN : (2 * g + 2) * SPAN]
        lo = jnp.concatenate([even[:, :HD], odd[:, :HD]], axis=1)
        up = jnp.concatenate([even[:, HD:], odd[:, HD:]], axis=1)
        lanes = slice(128 * g, 128 * (g + 1))
        out_ref[0:SPAN, lanes] = jnp.where(swapped, up, lo).astype(BF16)
        out_ref[SPAN : 2 * SPAN, lanes] = jnp.where(swapped, lo, up).astype(BF16)


def partials(queries, chunks, old=None, at=None, packed=False):
    nq, nc = len(queries), len(chunks)
    pairs = nq * nc * 2 * CHUNK * ROWS
    operands = [*queries, *chunks, *([] if at is None else [old])]
    sums = (nq, PART, ROWS)
    shape = jax.ShapeDtypeStruct(sums, F32)
    if packed:
        shape = jax.ShapeDtypeStruct((QMSG, ROWS), BF16)
    return pl.pallas_call(
        functools.partial(attend, nq, nc, at, packed),
        out_shape=shape,
        in_specs=[VMEM] * len(operands),
        out_specs=VMEM,
        scratch_shapes=([pltpu.VMEM(sums, F32)] if packed else [])
        + [pltpu.VMEM((nq, QMSG, ROWS), BF16), pltpu.VMEM((nc, GROUP, MSG, 128), BF16)],
        compiler_params=PARAMS,
        cost_estimate=pl.CostEstimate(
            flops=pairs * 16, bytes_accessed=nc * 2**14, transcendentals=0
        ),
        name="attend",
    )(*operands)


def simple(kernel, shape, name, *operands):
    return pl.pallas_call(
        kernel,
        out_shape=shape,
        in_specs=[VMEM] * len(operands),
        out_specs=VMEM,
        compiler_params=PARAMS,
        name=name,
    )(*operands)


def place(index):
    inner, outer = divmod(index, 16)
    return inner % 4, inner // 4 * 2 + outer // 2 % 2, outer // 4, outer % 2


def index_of(x, y, z, core):
    return (y // 2 * 4 + x) * 16 + z * 4 + y % 2 * 2 + core


def permute(array, target):
    pairs = []
    for source in range(128):
        x, y, z, core = place(source)
        x, y, z, core = target(x, y, z, core)
        pairs.append((source, index_of(x % 4, y % 4, z % 4, core % 2)))
    return lax.ppermute(array, ("inner", "outer"), pairs)


def along_first(array, d):
    return permute(array, lambda x, y, z, c: (x, y, z + d, c) if c else (x + d, y, z, c))


def along_second(array, d):
    return permute(array, lambda x, y, z, c: (x + d, y, z, c) if c else (x, y, z + d, c))


def y_neighbour(array):
    return permute(array, lambda x, y, z, c: (x, y ^ 1, z, c))


def y_mirror(array):
    return permute(array, lambda x, y, z, c: (x, 3 - y, z, c))


def other_core(array):
    return permute(array, lambda x, y, z, c: (x, y, z, c + 1))


def after(array, *others):
    return lax.optimization_barrier((array, *others))[0]


def prepared(kernel, name, operands, scratch, *shapes):
    return pl.pallas_call(
        kernel,
        out_shape=shapes,
        in_specs=[HBM] * len(operands),
        out_specs=(VMEM,) * len(shapes),
        scratch_shapes=[*scratch, pltpu.SemaphoreType.DMA((len(operands),))],
        compiler_params=pltpu.CompilerParams(vmem_limit_bytes=63 << 20),
        name=name,
    )(*operands)


def shards(queries, key_value, positions, sinks):
    (km,) = prepared(
        prepare_keys,
        "prepare_keys",
        (positions, key_value),
        [pltpu.SMEM(positions.shape, jnp.int32), pltpu.VMEM(key_value.shape, BF16)],
        jax.ShapeDtypeStruct((1, MSG, 128), BF16),
    )
    qm, flag = prepared(
        prepare_queries,
        "prepare_queries",
        (positions, after(queries, km), sinks),
        [
            pltpu.SMEM(positions.shape, jnp.int32),
            pltpu.VMEM(queries.shape, BF16),
            pltpu.SMEM(sinks.shape, F32),
        ],
        jax.ShapeDtypeStruct((QMSG, ROWS), BF16),
        jax.ShapeDtypeStruct((16, ROWS), F32),
    )
    pair = jnp.concatenate([after(km, qm), y_mirror(km)], axis=0)
    asked = y_neighbour(qm)
    left, right, far = [along_first(pair, d) for d in (-1, 1, 2)]
    diag = simple(
        diagonal, jax.ShapeDtypeStruct((PART + 16, ROWS), F32), "diagonal", after(qm, far), km, flag
    )
    near = jnp.concatenate([after(pair, asked, diag), left, right, far], axis=0)
    side3, side1, side2 = [along_second(near, d) for d in (2, 1, -1)]
    own = partials([qm], [near])
    near2 = other_core(near)
    mate = partials([after(asked, own)], [near])
    mate = partials([after(asked, mate)], [near2], mate, 0)
    own = partials([after(qm, mate)], [near2], own, 0)
    mate = partials([after(asked, own)], [side1], mate, 0)
    own = partials([after(qm, mate)], [side1], own, 0)
    swap1 = other_core(after(side1, own))
    mate = partials([after(asked, own)], [side2], mate, 0)
    swap2, swap3 = [other_core(after(side, mate)) for side in (side2, side3)]
    mate = partials([asked], [side3, swap1], mate, 0)
    sent = partials([asked], [swap2, swap3], mate, 0, packed=True)
    back = y_neighbour(sent)
    own = partials([after(qm, sent)], [swap3, swap2], own, 0)
    own = partials([qm], [swap1, side3], own, 0)
    own = partials([qm], [side2], own, 0)
    return pl.pallas_call(
        finish,
        out_shape=jax.ShapeDtypeStruct(queries.shape, BF16),
        in_specs=[VMEM] * 3,
        out_specs=VMEM,
        compiler_params=PARAMS,
        name="finish",
    )(diag, own.reshape(PART, ROWS), back)


def solution(mesh):
    return jax.shard_map(
        shards,
        mesh=mesh,
        in_specs=(
            P(("inner", "outer"), None),
            P(("inner", "outer"), None),
            P(("inner", "outer")),
            P(),
        ),
        out_specs=P(("inner", "outer"), None),
        check_vma=False,
    )
```

```python
import functools

import jax
import jax.numpy as jnp
from jax import lax
from jax.experimental import pallas as pl
from jax.experimental.pallas import tpu as pltpu
from jax.sharding import PartitionSpec as P

HEADS = 8
HD = 64
SPAN = 96
ROWS = HEADS * SPAN
GROUP = 8
CHUNK = GROUP * SPAN
MSG = 208
QMSG = 144
PART = 160
LOG2E = 1.4426950408889634
SCALE = HD**-0.5 * LOG2E
LIMIT = 1e36
F32 = jnp.float32
BF16 = jnp.bfloat16
VMEM = pl.BlockSpec(memory_space=pltpu.VMEM)
HBM = pl.BlockSpec(memory_space=pltpu.HBM)
PARAMS = pltpu.CompilerParams(vmem_limit_bytes=20 << 20)


def dot(a, b):
    return jnp.dot(a, b, preferred_element_type=F32)


def load(pairs, sems):
    copies = [
        pltpu.make_async_copy(source, target, sems.at[n]) for n, (source, target) in enumerate(pairs)
    ]
    for copy in copies:
        copy.start()
    for copy in copies:
        copy.wait()


def order(pos_ref, ref):
    run = pos_ref[0] // SPAN
    swapped = run >= 128
    first, second = ref[0:SPAN, :], ref[SPAN : 2 * SPAN, :]
    lower = jnp.where(swapped, 255 - run, run).astype(F32)
    return swapped, lower, jnp.where(swapped, second, first), jnp.where(swapped, first, second)


def prepare_keys(pos_hbm, kv_hbm, km_ref, pos_ref, kv_ref, sems):
    load(((pos_hbm, pos_ref), (kv_hbm, kv_ref)), sems)
    _, lower, lo, up = order(pos_ref, kv_ref)
    km_ref[0, 0:SPAN, :] = jnp.concatenate([lo[:, :HD], up[:, :HD]], axis=1)
    km_ref[0, SPAN : 2 * SPAN, :] = jnp.concatenate([lo[:, HD:], up[:, HD:]], axis=1)
    km_ref[0, 2 * SPAN :, :] = jnp.full((MSG - 2 * SPAN, 128), lower, F32).astype(BF16)


def prepare_queries(pos_hbm, q_hbm, sink_hbm, qm_ref, flag_ref, pos_ref, q_ref, sink_ref, sems):
    load(((pos_hbm, pos_ref), (q_hbm, q_ref), (sink_hbm, sink_ref)), sems)
    swapped, lower, lo, up = order(pos_ref, q_ref)
    stacked = jnp.concatenate(
        [
            jnp.concatenate([lo[:, h * HD : (h + 1) * HD], up[:, h * HD : (h + 1) * HD]], axis=1)
            for h in range(HEADS)
        ],
        axis=0,
    )
    qm_ref[0:128, :] = jnp.transpose(stacked)
    qm_ref[128:, :] = jnp.full((QMSG - 128, ROWS), lower, F32).astype(BF16)
    flag_ref[0:8, :] = jnp.full((8, ROWS), jnp.where(swapped, 1.0, 0.0), F32)
    lanes = lax.broadcasted_iota(jnp.int32, (8, ROWS), 1)
    sinks = jnp.full((8, ROWS), sink_ref[0], F32)
    for h in range(1, HEADS):
        sinks = jnp.where(lanes >= h * SPAN, sink_ref[h], sinks)
    flag_ref[8:16, :] = sinks


def diagonal(qm_ref, km_ref, flag_ref, out_ref):
    out_ref[PART:, :] = flag_ref[...]
    keys = lax.broadcasted_iota(jnp.int32, (SPAN, ROWS), 0)
    rows = lax.broadcasted_iota(jnp.int32, (SPAN, ROWS), 1)
    mine = rows
    for h in range(1, HEADS):
        mine = jnp.where(rows >= h * SPAN, rows - h * SPAN, mine)
    visible = keys <= mine
    k = km_ref[0, 0:SPAN, :]
    v = jnp.transpose(km_ref[0, SPAN : 2 * SPAN, :].astype(F32)).astype(BF16)
    for half in range(2):
        part = slice(half * HD, (half + 1) * HD)
        s = dot(k[:, part], qm_ref[part, :]) * SCALE
        s = jnp.where(visible, s, -1e30)
        shift = jnp.maximum(jnp.max(s, axis=0, keepdims=True), 0.0)
        p = jnp.where(visible, jnp.exp2(s - shift), 0.0)
        out_ref[part, :] = dot(v[part, :], p.astype(BF16))
        total = jnp.sum(p, axis=0, keepdims=True)
        out_ref[128 + 8 * half : 136 + 8 * half, :] = jnp.broadcast_to(total, (8, ROWS))
        out_ref[144 + 8 * half : 152 + 8 * half, :] = jnp.broadcast_to(shift, (8, ROWS))


def chunk_masks(keys, q_ref):
    info = keys[:, 2 * SPAN : 2 * SPAN + 16, :].astype(F32)[:, 0:1, :]
    own = q_ref[128:144, 0:128].astype(F32)[0:1, :]
    below = jnp.where(info < own[None], 1.0, 0.0)
    above = jnp.where(info > own[None], 1.0, 0.0)
    return below, above


def along_lanes(mask):
    lanes = lax.broadcasted_iota(jnp.int32, (16, CHUNK), 1)
    wide = [
        jnp.concatenate([jnp.broadcast_to(mask[b], (16, 128))] * (CHUNK // 128), axis=1)
        for b in range(GROUP)
    ]
    out = wide[0]
    for b in range(1, GROUP):
        out = jnp.where(lanes >= b * SPAN, wide[b], out)
    return out


def transposed_values(keys):
    return jnp.transpose(keys[:, SPAN : 2 * SPAN, :].reshape(CHUNK, 128))


def chunk_operands(keys, q_ref, vt):
    below, above = chunk_masks(keys, q_ref)
    k = keys[:, 0:SPAN, :]
    lanes = lax.broadcasted_iota(jnp.int32, (GROUP, 1, 128), 2)
    keep = jnp.where(lanes < HD, below, above).astype(BF16)
    chosen = (k * keep).reshape(CHUNK, 128)
    low, high = along_lanes(below), along_lanes(above)
    rows = lax.broadcasted_iota(jnp.int32, (16, CHUNK), 0)
    ones = jnp.where(rows < 8, low, high).astype(BF16)
    low, high = low[0:1].astype(BF16), high[0:1].astype(BF16)
    values = jnp.concatenate([vt[:HD] * low, vt[HD:] * high, ones], axis=0)
    return k.reshape(CHUNK, 128), chosen, values


def each(count, body):
    if count == 1:
        body(0)
    else:
        pl.loop(0, count)(body)


def attend(nq, nc, at, packed, *refs):
    q_refs, refs = refs[:nq], refs[nq:]
    key_refs, refs = refs[:nc], refs[nc:]
    if at is not None:
        old_ref, refs = refs[0], refs[1:]
    out_ref, refs = refs[0], refs[1:]
    sums = refs[0] if packed else out_ref
    queries, keys = refs[-2], refs[-1]
    direct = nc == 1
    start = slice(144, PART) if direct else slice(0, PART)
    for q in range(nq):
        if nq > 1:
            queries[q] = q_refs[q][...]
        sums[q, start] = jnp.zeros_like(sums[q, start]) if at is None else old_ref[at + q, start]
    for c in range(nc):
        if not direct:
            keys[c] = key_refs[c][...]

    def keys_at(c):
        return key_refs[0] if direct else keys.at[c]

    def query_at(q):
        return q_refs[0] if nq == 1 else queries.at[q]

    def store(q, rows, value):
        if not direct:
            sums[q, rows] += value
        elif at is None:
            sums[q, rows] = value
        else:
            sums[q, rows] = old_ref[at + q, rows] + value

    def add(c):
        chunk = keys_at(c)[...]
        vt = transposed_values(chunk)
        first = jnp.concatenate([vt[:HD], jnp.ones((16, CHUNK), BF16)], axis=0)

        def one(q):
            q_ref = query_at(q)
            k, chosen, values = chunk_operands(chunk, q_ref, vt)
            a = dot(k[:, :HD], q_ref[HD:128, :])
            b = dot(chosen, q_ref[0:128, :])
            pa = jnp.exp2(a * SCALE).astype(BF16)
            pb = jnp.exp2(b * SCALE).astype(BF16)
            oa = dot(first, pa)
            ob = dot(values, pb)
            store(q, slice(0, HD), ob[:HD])
            store(q, slice(HD, 128), oa[:HD] + ob[HD:128])
            store(q, slice(128, 136), ob[128:136])
            store(q, slice(136, 144), oa[HD : HD + 8] + ob[136:144])

        each(nq, one)

    each(nc, add)

    def check(q):
        bad = jnp.sum(jnp.where(sums[q, 128:144, :] < LIMIT, 0.0, 1.0))
        bad = bad + jnp.sum(sums[q, 144:160, :])

        @pl.when(bad > 0.0)
        def _():
            for k in range(nq):

                @pl.when(q == k)
                def _():
                    sums[k] = jnp.zeros((PART, ROWS), F32) if at is None else old_ref[at + k]

            each(nc, lambda c: careful(keys_at(c), query_at(q), sums.at[q]))

    each(nq, check)

    if packed:
        for q in range(nq):
            out_ref[0:128, :] = sums[q, 0:128, :].astype(BF16)
            rows = lax.broadcasted_iota(jnp.int32, (16, ROWS), 0)
            stats = jnp.zeros((16, ROWS), F32)
            for row, start in ((0, 128), (2, 136)):
                total = jnp.broadcast_to(sums[q, start : start + 1, :], (16, ROWS))
                high = total.astype(BF16).astype(F32)
                stats = jnp.where(rows == row, high, stats)
                stats = jnp.where(rows == row + 1, total - high, stats)
            for row, start in ((4, 144), (5, 152)):
                shift = jnp.broadcast_to(sums[q, start : start + 1, :], (16, ROWS))
                stats = jnp.where(rows == row, shift, stats)
            out_ref[128:144, :] = stats.astype(BF16)


def careful(keys, q_ref, out_ref):
    def raise_shift(half, top):
        old = out_ref[144 + 8 * half : 145 + 8 * half, :]
        new = jnp.maximum(old, jnp.maximum(top, 0.0).astype(BF16).astype(F32))
        factor = jnp.exp2(old - new)
        out_ref[half * HD : (half + 1) * HD, :] *= factor
        out_ref[128 + 8 * half : 136 + 8 * half, :] *= factor
        out_ref[144 + 8 * half : 152 + 8 * half, :] = jnp.broadcast_to(new, (8, ROWS))
        return new

    def add(half, values, p):
        p = p.astype(BF16)
        out_ref[half * HD : (half + 1) * HD, :] += dot(values, p)
        out_ref[128 + 8 * half : 136 + 8 * half, :] += dot(jnp.ones((16, SPAN), BF16), p)[:8]

    def wide(row):
        return jnp.concatenate([row] * (ROWS // 128), axis=1)

    own = wide(q_ref[128:144, 0:128].astype(F32)[0:1, :])

    @pl.loop(0, GROUP)
    def _(b):
        k = keys[b, 0:SPAN, :]
        vt = jnp.transpose(keys[b, SPAN : 2 * SPAN, :].astype(F32)).astype(BF16)
        info = wide(keys[b, 2 * SPAN : 2 * SPAN + 16, :].astype(F32)[0:1, :])
        low = dot(k[:, :HD], q_ref[HD:128, :]) * SCALE
        shift = raise_shift(1, jnp.max(low, axis=0, keepdims=True))
        add(1, vt[:HD], jnp.exp2(low - shift))
        for half, seen in ((0, info < own), (1, info > own)):
            part = slice(half * HD, (half + 1) * HD)
            s = dot(k[:, part], q_ref[part, :]) * SCALE
            top = jnp.where(seen, jnp.max(s, axis=0, keepdims=True), -1e30)
            shift = raise_shift(half, top)
            add(half, vt[part], jnp.where(seen, jnp.exp2(s - shift), 0.0))


def finish(diag_ref, own_ref, message, out_ref):
    swapped = jnp.broadcast_to(diag_ref[PART : PART + 1, 0:128], (SPAN, 128)) > 0.5
    held = []
    for half in range(2):
        part = slice(half * HD, (half + 1) * HD)
        stat = 128 + 8 * half
        shifts = [p[stat + 16 : stat + 17, :] for p in (diag_ref, own_ref)]
        top = jnp.maximum(*shifts)
        total = jnp.exp2(diag_ref[PART + 8 : PART + 9, :] * LOG2E - top)
        sums = jnp.zeros((HD, ROWS), F32)
        for p, shift in zip((diag_ref, own_ref), shifts):
            factor = jnp.exp2(shift - top)
            total = total + p[stat : stat + 1, :] * factor
            sums = sums + p[part, :] * factor
        held.append((top, total, sums))
    stats = message[128:144, :].astype(F32)
    results = []
    for half, (top, total, sums) in enumerate(held):
        shift = stats[4 + half : 5 + half]
        new = jnp.maximum(top, shift)
        kept, added = jnp.exp2(top - new), jnp.exp2(shift - new)
        more = stats[2 * half : 2 * half + 1] + stats[2 * half + 1 : 2 * half + 2]
        scale = 1.0 / (total * kept + more * added)
        sent = message[half * HD : (half + 1) * HD, :].astype(F32)
        results.append(sums * (kept * scale) + sent * (added * scale))
    both = jnp.transpose(jnp.concatenate(results, axis=0))
    for g in range(HEADS // 2):
        even, odd = both[2 * g * SPAN : (2 * g + 1) * SPAN], both[(2 * g + 1) * SPAN : (2 * g + 2) * SPAN]
        lo = jnp.concatenate([even[:, :HD], odd[:, :HD]], axis=1)
        up = jnp.concatenate([even[:, HD:], odd[:, HD:]], axis=1)
        lanes = slice(128 * g, 128 * (g + 1))
        out_ref[0:SPAN, lanes] = jnp.where(swapped, up, lo).astype(BF16)
        out_ref[SPAN : 2 * SPAN, lanes] = jnp.where(swapped, lo, up).astype(BF16)


def partials(queries, chunks, old=None, at=None, packed=False):
    nq, nc = len(queries), len(chunks)
    pairs = nq * nc * 2 * CHUNK * ROWS
    operands = [*queries, *chunks, *([] if at is None else [old])]
    sums = (nq, PART, ROWS)
    shape = jax.ShapeDtypeStruct(sums, F32)
    if packed:
        shape = jax.ShapeDtypeStruct((QMSG, ROWS), BF16)
    return pl.pallas_call(
        functools.partial(attend, nq, nc, at, packed),
        out_shape=shape,
        in_specs=[VMEM] * len(operands),
        out_specs=VMEM,
        scratch_shapes=([pltpu.VMEM(sums, F32)] if packed else [])
        + [pltpu.VMEM((nq, QMSG, ROWS), BF16), pltpu.VMEM((nc, GROUP, MSG, 128), BF16)],
        compiler_params=PARAMS,
        cost_estimate=pl.CostEstimate(
            flops=pairs * 16, bytes_accessed=nc * 2**14, transcendentals=0
        ),
        name="attend",
    )(*operands)


def simple(kernel, shape, name, *operands):
    return pl.pallas_call(
        kernel,
        out_shape=shape,
        in_specs=[VMEM] * len(operands),
        out_specs=VMEM,
        compiler_params=PARAMS,
        name=name,
    )(*operands)


def place(index):
    inner, outer = divmod(index, 16)
    return inner % 4, inner // 4 * 2 + outer // 2 % 2, outer // 4, outer % 2


def index_of(x, y, z, core):
    return (y // 2 * 4 + x) * 16 + z * 4 + y % 2 * 2 + core


def permute(array, target):
    pairs = []
    for source in range(128):
        x, y, z, core = place(source)
        x, y, z, core = target(x, y, z, core)
        pairs.append((source, index_of(x % 4, y % 4, z % 4, core % 2)))
    return lax.ppermute(array, ("inner", "outer"), pairs)


def along_first(array, d):
    return permute(array, lambda x, y, z, c: (x, y, z + d, c) if c else (x + d, y, z, c))


def along_second(array, d):
    return permute(array, lambda x, y, z, c: (x + d, y, z, c) if c else (x, y, z + d, c))


def y_neighbour(array):
    return permute(array, lambda x, y, z, c: (x, y ^ 1, z, c))


def y_mirror(array):
    return permute(array, lambda x, y, z, c: (x, 3 - y, z, c))


def other_core(array):
    return permute(array, lambda x, y, z, c: (x, y, z, c + 1))


def after(array, *others):
    return lax.optimization_barrier((array, *others))[0]


def prepared(kernel, name, operands, scratch, *shapes):
    return pl.pallas_call(
        kernel,
        out_shape=shapes,
        in_specs=[HBM] * len(operands),
        out_specs=(VMEM,) * len(shapes),
        scratch_shapes=[*scratch, pltpu.SemaphoreType.DMA((len(operands),))],
        compiler_params=pltpu.CompilerParams(vmem_limit_bytes=63 << 20),
        name=name,
    )(*operands)


def shards(queries, key_value, positions, sinks):
    (km,) = prepared(
        prepare_keys,
        "prepare_keys",
        (positions, key_value),
        [pltpu.SMEM(positions.shape, jnp.int32), pltpu.VMEM(key_value.shape, BF16)],
        jax.ShapeDtypeStruct((1, MSG, 128), BF16),
    )
    qm, flag = prepared(
        prepare_queries,
        "prepare_queries",
        (positions, after(queries, km), sinks),
        [
            pltpu.SMEM(positions.shape, jnp.int32),
            pltpu.VMEM(queries.shape, BF16),
            pltpu.SMEM(sinks.shape, F32),
        ],
        jax.ShapeDtypeStruct((QMSG, ROWS), BF16),
        jax.ShapeDtypeStruct((16, ROWS), F32),
    )
    pair = jnp.concatenate([after(km, qm), y_mirror(km)], axis=0)
    asked = y_neighbour(qm)
    left, right, far = [along_first(pair, d) for d in (-1, 1, 2)]
    near = jnp.concatenate([after(pair, asked), left, right, far], axis=0)
    side3, side1, side2 = [along_second(near, d) for d in (2, 1, -1)]
    own = partials([qm], [near])
    near2 = other_core(near)
    mate = partials([after(asked, own)], [near])
    mate = partials([after(asked, mate)], [near2], mate, 0)
    own = partials([after(qm, mate)], [near2], own, 0)
    mate = partials([after(asked, own)], [side1], mate, 0)
    own = partials([after(qm, mate)], [side1], own, 0)
    swap1 = other_core(after(side1, own))
    mate = partials([after(asked, own)], [side2], mate, 0)
    swap2, swap3 = [other_core(after(side, mate)) for side in (side2, side3)]
    mate = partials([asked], [side3, swap1], mate, 0)
    sent = partials([asked], [swap2, swap3], mate, 0, packed=True)
    back = y_neighbour(sent)
    own = partials([after(qm, sent)], [swap3, swap2], own, 0)
    own = partials([qm], [swap1, side3], own, 0)
    diag = simple(
        diagonal, jax.ShapeDtypeStruct((PART + 16, ROWS), F32), "diagonal", after(qm, own), km, flag
    )
    own = partials([after(qm, diag)], [side2], own, 0)
    return pl.pallas_call(
        finish,
        out_shape=jax.ShapeDtypeStruct(queries.shape, BF16),
        in_specs=[VMEM] * 3,
        out_specs=VMEM,
        compiler_params=PARAMS,
        name="finish",
    )(diag, own.reshape(PART, ROWS), back)


def solution(mesh):
    return jax.shard_map(
        shards,
        mesh=mesh,
        in_specs=(
            P(("inner", "outer"), None),
            P(("inner", "outer"), None),
            P(("inner", "outer")),
            P(),
        ),
        out_specs=P(("inner", "outer"), None),
        check_vma=False,
    )
```

```python
import functools

import jax
import jax.numpy as jnp
from jax import lax
from jax.experimental import pallas as pl
from jax.experimental.pallas import tpu as pltpu
from jax.sharding import PartitionSpec as P

HEADS = 8
HD = 64
SPAN = 96
ROWS = HEADS * SPAN
GROUP = 8
CHUNK = GROUP * SPAN
MSG = 208
QMSG = 144
PART = 160
LOG2E = 1.4426950408889634
SCALE = HD**-0.5 * LOG2E
LIMIT = 1e36
F32 = jnp.float32
BF16 = jnp.bfloat16
VMEM = pl.BlockSpec(memory_space=pltpu.VMEM)
HBM = pl.BlockSpec(memory_space=pltpu.HBM)
PARAMS = pltpu.CompilerParams(vmem_limit_bytes=20 << 20)


def dot(a, b):
    return jnp.dot(a, b, preferred_element_type=F32)


def load(pairs, sems):
    copies = [
        pltpu.make_async_copy(source, target, sems.at[n]) for n, (source, target) in enumerate(pairs)
    ]
    for copy in copies:
        copy.start()
    for copy in copies:
        copy.wait()


def order(pos_ref, ref):
    run = pos_ref[0] // SPAN
    swapped = run >= 128
    first, second = ref[0:SPAN, :], ref[SPAN : 2 * SPAN, :]
    lower = jnp.where(swapped, 255 - run, run).astype(F32)
    return swapped, lower, jnp.where(swapped, second, first), jnp.where(swapped, first, second)


def prepare_keys(pos_hbm, kv_hbm, km_ref, pos_ref, kv_ref, sems):
    load(((pos_hbm, pos_ref), (kv_hbm, kv_ref)), sems)
    _, lower, lo, up = order(pos_ref, kv_ref)
    km_ref[0, 0:SPAN, :] = jnp.concatenate([lo[:, :HD], up[:, :HD]], axis=1)
    km_ref[0, SPAN : 2 * SPAN, :] = jnp.concatenate([lo[:, HD:], up[:, HD:]], axis=1)
    km_ref[0, 2 * SPAN :, :] = jnp.full((MSG - 2 * SPAN, 128), lower, F32).astype(BF16)


def prepare_queries(pos_hbm, q_hbm, sink_hbm, qm_ref, flag_ref, pos_ref, q_ref, sink_ref, sems):
    load(((pos_hbm, pos_ref), (q_hbm, q_ref), (sink_hbm, sink_ref)), sems)
    swapped, lower, lo, up = order(pos_ref, q_ref)
    stacked = jnp.concatenate(
        [
            jnp.concatenate([lo[:, h * HD : (h + 1) * HD], up[:, h * HD : (h + 1) * HD]], axis=1)
            for h in range(HEADS)
        ],
        axis=0,
    )
    qm_ref[0:128, :] = jnp.transpose(stacked)
    qm_ref[128:, :] = jnp.full((QMSG - 128, ROWS), lower, F32).astype(BF16)
    flag_ref[0:8, :] = jnp.full((8, ROWS), jnp.where(swapped, 1.0, 0.0), F32)
    lanes = lax.broadcasted_iota(jnp.int32, (8, ROWS), 1)
    sinks = jnp.full((8, ROWS), sink_ref[0], F32)
    for h in range(1, HEADS):
        sinks = jnp.where(lanes >= h * SPAN, sink_ref[h], sinks)
    flag_ref[8:16, :] = sinks


def diagonal(qm_ref, km_ref, flag_ref, out_ref):
    out_ref[PART:, :] = flag_ref[...]
    keys = lax.broadcasted_iota(jnp.int32, (SPAN, ROWS), 0)
    rows = lax.broadcasted_iota(jnp.int32, (SPAN, ROWS), 1)
    mine = rows
    for h in range(1, HEADS):
        mine = jnp.where(rows >= h * SPAN, rows - h * SPAN, mine)
    visible = keys <= mine
    k = km_ref[0, 0:SPAN, :]
    v = jnp.transpose(km_ref[0, SPAN : 2 * SPAN, :].astype(F32)).astype(BF16)
    for half in range(2):
        part = slice(half * HD, (half + 1) * HD)
        s = dot(k[:, part], qm_ref[part, :]) * SCALE
        s = jnp.where(visible, s, -1e30)
        shift = jnp.maximum(jnp.max(s, axis=0, keepdims=True), 0.0)
        p = jnp.where(visible, jnp.exp2(s - shift), 0.0)
        out_ref[part, :] = dot(v[part, :], p.astype(BF16))
        total = jnp.sum(p, axis=0, keepdims=True)
        out_ref[128 + 8 * half : 136 + 8 * half, :] = jnp.broadcast_to(total, (8, ROWS))
        out_ref[144 + 8 * half : 152 + 8 * half, :] = jnp.broadcast_to(shift, (8, ROWS))


def chunk_masks(keys, q_ref):
    info = keys[:, 2 * SPAN : 2 * SPAN + 16, :].astype(F32)[:, 0:1, :]
    own = q_ref[128:144, 0:128].astype(F32)[0:1, :]
    below = jnp.where(info < own[None], 1.0, 0.0)
    above = jnp.where(info > own[None], 1.0, 0.0)
    return below, above


def along_lanes(mask):
    lanes = lax.broadcasted_iota(jnp.int32, (16, CHUNK), 1)
    wide = [
        jnp.concatenate([jnp.broadcast_to(mask[b], (16, 128))] * (CHUNK // 128), axis=1)
        for b in range(GROUP)
    ]
    out = wide[0]
    for b in range(1, GROUP):
        out = jnp.where(lanes >= b * SPAN, wide[b], out)
    return out


def transposed_values(keys):
    return jnp.transpose(keys[:, SPAN : 2 * SPAN, :].reshape(CHUNK, 128))


def chunk_operands(keys, q_ref, vt):
    below, above = chunk_masks(keys, q_ref)
    k = keys[:, 0:SPAN, :]
    lanes = lax.broadcasted_iota(jnp.int32, (GROUP, 1, 128), 2)
    keep = jnp.where(lanes < HD, below, above).astype(BF16)
    chosen = (k * keep).reshape(CHUNK, 128)
    low, high = along_lanes(below), along_lanes(above)
    rows = lax.broadcasted_iota(jnp.int32, (16, CHUNK), 0)
    ones = jnp.where(rows < 8, low, high).astype(BF16)
    low, high = low[0:1].astype(BF16), high[0:1].astype(BF16)
    values = jnp.concatenate([vt[:HD] * low, vt[HD:] * high, ones], axis=0)
    return k.reshape(CHUNK, 128), chosen, values


def each(count, body):
    if count == 1:
        body(0)
    else:
        pl.loop(0, count)(body)


def attend(nq, nc, at, packed, *refs):
    q_refs, refs = refs[:nq], refs[nq:]
    key_refs, refs = refs[:nc], refs[nc:]
    if at is not None:
        old_ref, refs = refs[0], refs[1:]
    out_ref, refs = refs[0], refs[1:]
    sums = refs[0] if packed else out_ref
    queries, keys = refs[-2], refs[-1]
    direct = nc == 1
    start = slice(144, PART) if direct else slice(0, PART)
    for q in range(nq):
        if nq > 1:
            queries[q] = q_refs[q][...]
        sums[q, start] = jnp.zeros_like(sums[q, start]) if at is None else old_ref[at + q, start]
    for c in range(nc):
        if not direct:
            keys[c] = key_refs[c][...]

    def keys_at(c):
        return key_refs[0] if direct else keys.at[c]

    def query_at(q):
        return q_refs[0] if nq == 1 else queries.at[q]

    def store(q, rows, value):
        if not direct:
            sums[q, rows] += value
        elif at is None:
            sums[q, rows] = value
        else:
            sums[q, rows] = old_ref[at + q, rows] + value

    def add(c):
        chunk = keys_at(c)[...]
        vt = transposed_values(chunk)
        first = jnp.concatenate([vt[:HD], jnp.ones((16, CHUNK), BF16)], axis=0)

        def one(q):
            q_ref = query_at(q)
            k, chosen, values = chunk_operands(chunk, q_ref, vt)
            a = dot(k[:, :HD], q_ref[HD:128, :])
            b = dot(chosen, q_ref[0:128, :])
            pa = jnp.exp2(a * SCALE).astype(BF16)
            pb = jnp.exp2(b * SCALE).astype(BF16)
            oa = dot(first, pa)
            ob = dot(values, pb)
            store(q, slice(0, HD), ob[:HD])
            store(q, slice(HD, 128), oa[:HD] + ob[HD:128])
            store(q, slice(128, 136), ob[128:136])
            store(q, slice(136, 144), oa[HD : HD + 8] + ob[136:144])

        each(nq, one)

    each(nc, add)

    def check(q):
        bad = jnp.sum(jnp.where(sums[q, 128:144, :] < LIMIT, 0.0, 1.0))
        bad = bad + jnp.sum(sums[q, 144:160, :])

        @pl.when(bad > 0.0)
        def _():
            for k in range(nq):

                @pl.when(q == k)
                def _():
                    sums[k] = jnp.zeros((PART, ROWS), F32) if at is None else old_ref[at + k]

            each(nc, lambda c: careful(keys_at(c), query_at(q), sums.at[q]))

    each(nq, check)

    if packed:
        for q in range(nq):
            out_ref[0:128, :] = sums[q, 0:128, :].astype(BF16)
            rows = lax.broadcasted_iota(jnp.int32, (16, ROWS), 0)
            stats = jnp.zeros((16, ROWS), F32)
            for row, start in ((0, 128), (2, 136)):
                total = jnp.broadcast_to(sums[q, start : start + 1, :], (16, ROWS))
                high = total.astype(BF16).astype(F32)
                stats = jnp.where(rows == row, high, stats)
                stats = jnp.where(rows == row + 1, total - high, stats)
            for row, start in ((4, 144), (5, 152)):
                shift = jnp.broadcast_to(sums[q, start : start + 1, :], (16, ROWS))
                stats = jnp.where(rows == row, shift, stats)
            out_ref[128:144, :] = stats.astype(BF16)


def careful(keys, q_ref, out_ref):
    def raise_shift(half, top):
        old = out_ref[144 + 8 * half : 145 + 8 * half, :]
        new = jnp.maximum(old, jnp.maximum(top, 0.0).astype(BF16).astype(F32))
        factor = jnp.exp2(old - new)
        out_ref[half * HD : (half + 1) * HD, :] *= factor
        out_ref[128 + 8 * half : 136 + 8 * half, :] *= factor
        out_ref[144 + 8 * half : 152 + 8 * half, :] = jnp.broadcast_to(new, (8, ROWS))
        return new

    def add(half, values, p):
        p = p.astype(BF16)
        out_ref[half * HD : (half + 1) * HD, :] += dot(values, p)
        out_ref[128 + 8 * half : 136 + 8 * half, :] += dot(jnp.ones((16, SPAN), BF16), p)[:8]

    def wide(row):
        return jnp.concatenate([row] * (ROWS // 128), axis=1)

    own = wide(q_ref[128:144, 0:128].astype(F32)[0:1, :])

    @pl.loop(0, GROUP)
    def _(b):
        k = keys[b, 0:SPAN, :]
        vt = jnp.transpose(keys[b, SPAN : 2 * SPAN, :].astype(F32)).astype(BF16)
        info = wide(keys[b, 2 * SPAN : 2 * SPAN + 16, :].astype(F32)[0:1, :])
        low = dot(k[:, :HD], q_ref[HD:128, :]) * SCALE
        shift = raise_shift(1, jnp.max(low, axis=0, keepdims=True))
        add(1, vt[:HD], jnp.exp2(low - shift))
        for half, seen in ((0, info < own), (1, info > own)):
            part = slice(half * HD, (half + 1) * HD)
            s = dot(k[:, part], q_ref[part, :]) * SCALE
            top = jnp.where(seen, jnp.max(s, axis=0, keepdims=True), -1e30)
            shift = raise_shift(half, top)
            add(half, vt[part], jnp.where(seen, jnp.exp2(s - shift), 0.0))


def finish(diag_ref, own_ref, message, out_ref):
    swapped = jnp.broadcast_to(diag_ref[PART : PART + 1, 0:128], (SPAN, 128)) > 0.5
    held = []
    for half in range(2):
        part = slice(half * HD, (half + 1) * HD)
        stat = 128 + 8 * half
        shifts = [p[stat + 16 : stat + 17, :] for p in (diag_ref, own_ref)]
        top = jnp.maximum(*shifts)
        total = jnp.exp2(diag_ref[PART + 8 : PART + 9, :] * LOG2E - top)
        sums = jnp.zeros((HD, ROWS), F32)
        for p, shift in zip((diag_ref, own_ref), shifts):
            factor = jnp.exp2(shift - top)
            total = total + p[stat : stat + 1, :] * factor
            sums = sums + p[part, :] * factor
        held.append((top, total, sums))
    stats = message[128:144, :].astype(F32)
    results = []
    for half, (top, total, sums) in enumerate(held):
        shift = stats[4 + half : 5 + half]
        new = jnp.maximum(top, shift)
        kept, added = jnp.exp2(top - new), jnp.exp2(shift - new)
        more = stats[2 * half : 2 * half + 1] + stats[2 * half + 1 : 2 * half + 2]
        scale = 1.0 / (total * kept + more * added)
        sent = message[half * HD : (half + 1) * HD, :].astype(F32)
        results.append(sums * (kept * scale) + sent * (added * scale))
    both = jnp.transpose(jnp.concatenate(results, axis=0))
    for g in range(HEADS // 2):
        even, odd = both[2 * g * SPAN : (2 * g + 1) * SPAN], both[(2 * g + 1) * SPAN : (2 * g + 2) * SPAN]
        lo = jnp.concatenate([even[:, :HD], odd[:, :HD]], axis=1)
        up = jnp.concatenate([even[:, HD:], odd[:, HD:]], axis=1)
        lanes = slice(128 * g, 128 * (g + 1))
        out_ref[0:SPAN, lanes] = jnp.where(swapped, up, lo).astype(BF16)
        out_ref[SPAN : 2 * SPAN, lanes] = jnp.where(swapped, lo, up).astype(BF16)


def partials(queries, chunks, old=None, at=None, packed=False):
    nq, nc = len(queries), len(chunks)
    pairs = nq * nc * 2 * CHUNK * ROWS
    operands = [*queries, *chunks, *([] if at is None else [old])]
    sums = (nq, PART, ROWS)
    shape = jax.ShapeDtypeStruct(sums, F32)
    if packed:
        shape = jax.ShapeDtypeStruct((QMSG, ROWS), BF16)
    return pl.pallas_call(
        functools.partial(attend, nq, nc, at, packed),
        out_shape=shape,
        in_specs=[VMEM] * len(operands),
        out_specs=VMEM,
        scratch_shapes=([pltpu.VMEM(sums, F32)] if packed else [])
        + [pltpu.VMEM((nq, QMSG, ROWS), BF16), pltpu.VMEM((nc, GROUP, MSG, 128), BF16)],
        compiler_params=PARAMS,
        cost_estimate=pl.CostEstimate(
            flops=pairs * 16, bytes_accessed=nc * 2**14, transcendentals=0
        ),
        name="attend",
    )(*operands)


def simple(kernel, shape, name, *operands):
    return pl.pallas_call(
        kernel,
        out_shape=shape,
        in_specs=[VMEM] * len(operands),
        out_specs=VMEM,
        compiler_params=PARAMS,
        name=name,
    )(*operands)


def place(index):
    inner, outer = divmod(index, 16)
    return inner % 4, inner // 4 * 2 + outer // 2 % 2, outer // 4, outer % 2


def index_of(x, y, z, core):
    return (y // 2 * 4 + x) * 16 + z * 4 + y % 2 * 2 + core


def permute(array, target):
    pairs = []
    for source in range(128):
        x, y, z, core = place(source)
        x, y, z, core = target(x, y, z, core)
        pairs.append((source, index_of(x % 4, y % 4, z % 4, core % 2)))
    return lax.ppermute(array, ("inner", "outer"), pairs)


def along_first(array, d):
    return permute(array, lambda x, y, z, c: (x, y, z + d, c) if c else (x + d, y, z, c))


def along_second(array, d):
    return permute(array, lambda x, y, z, c: (x + d, y, z, c) if c else (x, y, z + d, c))


def y_neighbour(array):
    return permute(array, lambda x, y, z, c: (x, y ^ 1, z, c))


def y_mirror(array):
    return permute(array, lambda x, y, z, c: (x, 3 - y, z, c))


def other_core(array):
    return permute(array, lambda x, y, z, c: (x, y, z, c + 1))


def after(array, *others):
    return lax.optimization_barrier((array, *others))[0]


def prepared(kernel, name, operands, scratch, *shapes):
    return pl.pallas_call(
        kernel,
        out_shape=shapes,
        in_specs=[HBM] * len(operands),
        out_specs=(VMEM,) * len(shapes),
        scratch_shapes=[*scratch, pltpu.SemaphoreType.DMA((len(operands),))],
        compiler_params=pltpu.CompilerParams(vmem_limit_bytes=63 << 20),
        name=name,
    )(*operands)


def shards(queries, key_value, positions, sinks):
    (km,) = prepared(
        prepare_keys,
        "prepare_keys",
        (positions, key_value),
        [pltpu.SMEM(positions.shape, jnp.int32), pltpu.VMEM(key_value.shape, BF16)],
        jax.ShapeDtypeStruct((1, MSG, 128), BF16),
    )
    qm, flag = prepared(
        prepare_queries,
        "prepare_queries",
        (positions, after(queries, km), sinks),
        [
            pltpu.SMEM(positions.shape, jnp.int32),
            pltpu.VMEM(queries.shape, BF16),
            pltpu.SMEM(sinks.shape, F32),
        ],
        jax.ShapeDtypeStruct((QMSG, ROWS), BF16),
        jax.ShapeDtypeStruct((16, ROWS), F32),
    )
    pair = jnp.concatenate([after(km, qm), y_mirror(km)], axis=0)
    asked = y_neighbour(qm)
    left, right, far = [along_first(pair, d) for d in (-1, 1, 2)]
    diag = simple(
        diagonal, jax.ShapeDtypeStruct((PART + 16, ROWS), F32), "diagonal", after(qm, far), km, flag
    )
    near = jnp.concatenate([after(pair, asked, diag), left, right, far], axis=0)
    side3, side1, side2 = [along_second(near, d) for d in (2, 1, -1)]
    own = partials([qm], [near])
    near2 = other_core(near)
    mate = partials([after(asked, own)], [near])
    mate = partials([after(asked, mate)], [near2], mate, 0)
    own = partials([after(qm, mate)], [near2], own, 0)
    mate = partials([after(asked, own)], [side1], mate, 0)
    own = partials([after(qm, mate)], [side1], own, 0)
    mate = partials([after(asked, own)], [side2], mate, 0)
    swap1, swap2, swap3 = [other_core(after(side, mate)) for side in (side1, side2, side3)]
    mate = partials([asked], [side3, swap1], mate, 0)
    sent = partials([asked], [swap2, swap3], mate, 0, packed=True)
    back = y_neighbour(sent)
    own = partials([after(qm, sent)], [swap3, swap2], own, 0)
    own = partials([qm], [swap1, side3], own, 0)
    own = partials([qm], [side2], own, 0)
    return pl.pallas_call(
        finish,
        out_shape=jax.ShapeDtypeStruct(queries.shape, BF16),
        in_specs=[VMEM] * 3,
        out_specs=VMEM,
        compiler_params=PARAMS,
        name="finish",
    )(diag, own.reshape(PART, ROWS), back)


def solution(mesh):
    return jax.shard_map(
        shards,
        mesh=mesh,
        in_specs=(
            P(("inner", "outer"), None),
            P(("inner", "outer"), None),
            P(("inner", "outer")),
            P(),
        ),
        out_specs=P(("inner", "outer"), None),
        check_vma=False,
    )
```
